32 devices in a mesh: parts: 2 (over y), inner: 4 (over z), outer: 2 (over x), rep: 2 (over core).
Axes of the slice: x: 2, y: 2, z: 4, core: 2. Of those that a mesh axis runs over, the one named last changes fastest.
Arguments:
- tokens: bfloat16 [512, 1024], P(('parts', 'inner', 'outer'), 'rep'), parts along dimension 0, may hold values from -6 to 6
- teacher: bfloat16 [512, 1024], P(('parts', 'inner', 'outer'), 'rep'), parts along dimension 0, may hold values from -1.5 to 1.5
- expert_ids: int32 [512, 8], P(('parts', 'inner', 'outer')), parts along dimension 0, may hold values from 0 to 7, as said below
- gate_codes: int32 [512, 8], P(('parts', 'inner', 'outer')), parts along dimension 0, may hold values from 49152 to 65535
- gate_up_latent: float32 [8, 2, 384, 1024], P(('inner', 'outer'), None, 'rep'), may hold values from -6 to 6
- down_latent: float32 [8, 384, 1024], P(('inner', 'outer'), 'rep'), may hold values from -6 to 6
Outputs:
- student_out: bfloat16 [512, 1024], P(('parts', 'inner', 'outer'), 'rep'), parts along dimension 0
- new_gate_up: float32 [16, 2, 384, 1024], P(('parts', 'inner', 'outer'), None, 'rep'), parts along dimension 0
- new_down: float32 [16, 384, 1024], P(('parts', 'inner', 'outer'), 'rep'), parts along dimension 0
The draws below stay inside these ranges and needn't reach their ends.
There are 2 independent parts, one for each index of `parts`. The reference program is written for one: setup_inputs(seed, part) draws one part's arguments, and reference() takes and returns one part's arrays. A program takes and returns all parts, laid end to end along the dimension named above; an argument that names none is the same for every part. Nothing has to cross between parts.
Inputs may be any that keep to these rules, and one draw needn't show every extreme that they name: `expert_ids`: each token names 8 different experts. Each aligned block of 32 tokens (the tokens of one device) names any expert at most 32 times, and one expert, the same in every block of a part, exactly 32 times in every block.
All inputs are finite; a program needn't handle non-finite values. Where the reference program divides by a largest or mean magnitude, that divisor is 1e-20 or more.
Results may differ from the reference program's by a relative error of at most 0.012.
Values may be sent and summed in bfloat16 or wider, within the bound.
A program may use at most 64 MiB of HBM per device.

```python
import math
import jax
import jax.numpy as jnp
from jax import lax

D = 1024
HID = 384
TOPK = 8
TOK_DEV = 32
EXPERTS = 8
CAP = 32
TOKENS = 256
N_REP = 2


def draw_expert_ids(key, part):
    heat_level = jax.random.randint(jax.random.fold_in(key, 11), (EXPERTS,), 0, 4)
    hottest = jax.random.randint(jax.random.fold_in(key, 12), (), 0, EXPERTS)
    heat_level = jnp.where(jnp.arange(EXPERTS) == hottest, 5, heat_level)
    candidate = jnp.repeat(jnp.arange(EXPERTS, dtype=jnp.int32), CAP)
    priority = heat_level[candidate]
    pool_size = EXPERTS * CAP

    def draw_block(block_key):
        jitter = jax.random.randint(jax.random.fold_in(block_key, 1), (pool_size,), 0, 65536)
        scores = (priority * 65536 + jitter) * pool_size + jnp.arange(pool_size, dtype=jnp.int32)
        chosen = jnp.sort(candidate[lax.top_k(scores, TOK_DEV * TOPK)[1]])
        table = chosen.reshape(TOPK, TOK_DEV).T
        rotation = jax.random.randint(jax.random.fold_in(block_key, 2), (TOK_DEV, 1), 0, TOPK)
        column = (jnp.arange(TOPK, dtype=jnp.int32)[None, :] + rotation) % TOPK
        return jnp.take_along_axis(table, column, axis=1)
    block_keys = jax.random.split(jax.random.fold_in(key, 13), TOKENS // TOK_DEV)
    return jax.vmap(draw_block)(block_keys).reshape(TOKENS, TOPK).astype(jnp.int32)


def plant(array, rng, least, largest):
    index_at = [jax.random.randint(jax.random.fold_in(rng, axis), (), 0, length) for axis, length in enumerate(array.shape)]
    main_axis = array.shape.index(max(array.shape))
    beside = index_at[:main_axis] + [(index_at[main_axis] + 1) % array.shape[main_axis]] + index_at[main_axis + 1:]
    return array.at[tuple(index_at)].set(least).at[tuple(beside)].set(largest)


def shard_levels(rng, dims, cuts, least, high):
    level = 1.0
    for axis_at, shards_of in cuts:
        steps = jax.random.uniform(jax.random.fold_in(jax.random.fold_in(rng, 6), axis_at), (shards_of,), jnp.float32, least / len(cuts), high / len(cuts))
        level = level * jnp.repeat(jnp.exp(steps), dims[axis_at] // shards_of).reshape((-1,) + (1,) * (len(dims) - 1 - axis_at))
    return level


def noise(stream_key, shape, scale, reach, pieces=(), kind=jnp.bfloat16):
    array = jax.random.normal(stream_key, shape, jnp.float32) * scale
    if len(pieces) > 0:
        array = shard_levels(stream_key, shape, pieces, -0.22, 0.18) * array
    return jnp.clip(array, min=-reach, max=reach).astype(kind)


def setup_inputs(seed: int = 0, part: int = 0) -> dict:
    streams_of = jax.random.split(jax.random.key(seed), 7)
    part_keys = jax.random.split(jax.random.fold_in(streams_of[6], part), 7)
    tokens = noise(part_keys[0], (TOKENS, D), 1.0, 6.0, ((0, 8), (1, 2)))
    teacher = jnp.clip(jax.random.uniform(part_keys[1], (TOKENS, D), jnp.float32, -1.5, 1.5) * shard_levels(part_keys[1], (TOKENS, D), ((0, 8), (1, 2)), -0.4, 0.0), -1.5, 1.5).astype(jnp.bfloat16)
    expert_ids = draw_expert_ids(jax.random.fold_in(jax.random.fold_in(streams_of[6], part), 71), part)
    gate_codes = plant(jax.random.randint(part_keys[3], (TOKENS, TOPK), 49152, 65536), jax.random.fold_in(part_keys[3], 1), 49152, 65535).astype(jnp.int32)
    gate_up_latent = noise(streams_of[4], (EXPERTS, 2, HID, D), 1.0, 6.0, ((0, 8), (2, 2)), jnp.float32)
    down_latent = noise(streams_of[5], (EXPERTS, HID, D), 1.0, 6.0, ((0, 8), (1, 2)), jnp.float32)
    return dict(tokens=tokens, teacher=teacher, expert_ids=expert_ids, gate_codes=gate_codes, gate_up_latent=gate_up_latent, down_latent=down_latent)


learn_rate = 1.0

def soften(latent, fan_in):
    row_scale = lax.optimization_barrier(jnp.mean(jnp.abs(latent), axis=-1, keepdims=True)) + 1e-06
    normed = latent / row_scale
    lower = jnp.tanh(4.0 * (normed - 0.5))
    upper = jnp.tanh(4.0 * (normed + 0.5))
    fan_root = 1.0 / math.sqrt(fan_in)
    weight = (row_scale * 0.5 * (lower + upper) * fan_root).astype(jnp.bfloat16)
    slope = 2.0 * (2.0 - lower * lower - upper * upper) * fan_root
    return (weight, slope)

def expert_forward(gate_latent, down_part, inputs):
    gu_weight, gu_slope = soften(gate_latent, D)
    dn_weight, dn_slope = soften(down_part, HID)
    pre_gate = jnp.dot(gu_weight[0], inputs.T, preferred_element_type=jnp.float32)
    pre_up = jnp.dot(gu_weight[1], inputs.T, preferred_element_type=jnp.float32)
    sigmoid_gate = jax.nn.sigmoid(pre_gate)
    activated = pre_gate * sigmoid_gate
    hidden = (activated * pre_up).astype(jnp.bfloat16)
    return (gu_weight, gu_slope, dn_weight, dn_slope, pre_gate, pre_up, sigmoid_gate, activated, hidden)

def reference(tokens, teacher, expert_ids, gate_codes, gate_up_latent, down_latent):
    sources = TOKENS // TOK_DEV
    slot_rows = sources * CAP
    block_ids = expert_ids.reshape(sources, TOK_DEV * TOPK)
    one_hot = (block_ids[:, :, None] == jnp.arange(EXPERTS, dtype=jnp.int32)[None, None, :]).astype(jnp.int32)
    before = jnp.cumsum(one_hot, axis=1) - one_hot
    route_slot = lax.optimization_barrier(jnp.sum(before * one_hot, axis=2))
    source_index = jnp.arange(sources, dtype=jnp.int32)[:, None]
    target = (block_ids * slot_rows + source_index * CAP + route_slot).reshape(-1).astype(jnp.int32)
    routed = jnp.repeat(tokens, TOPK, axis=0)
    dispatched = jnp.zeros((EXPERTS * slot_rows, D), jnp.bfloat16).at[target].set(routed)
    dispatched = dispatched.reshape(EXPERTS, slot_rows, D)

    def forward(operands):
        gate_latent, down_part, inputs = operands
        parts = expert_forward(gate_latent, down_part, inputs)
        hidden = parts[8]
        dn_weight = parts[2]
        share_hidden = hidden.reshape(N_REP, HID // N_REP, -1).astype(jnp.float32)
        share_down = dn_weight.reshape(N_REP, HID // N_REP, D).astype(jnp.float32)
        shares = jnp.einsum('khr,khd->krd', share_hidden, share_down).astype(jnp.bfloat16)
        return lax.optimization_barrier(jnp.sum(shares.astype(jnp.float32), axis=0)).astype(jnp.bfloat16)
    expert_out = lax.map(forward, (gate_up_latent, down_latent, dispatched))
    gating = gate_codes.astype(jnp.float32) / 65536.0
    picked = expert_out.reshape(-1, D)[target].reshape(TOKENS, TOPK, D)
    mixed = lax.optimization_barrier(jnp.sum(gating[:, :, None] * picked.astype(jnp.float32), axis=1))
    student_out = mixed.astype(jnp.bfloat16)
    residual = mixed - teacher.astype(jnp.float32)
    pair_grad = (gating[:, :, None] * residual[:, None, :]).astype(jnp.bfloat16).reshape(-1, D)
    out_grad = jnp.zeros((EXPERTS * slot_rows, D), jnp.bfloat16).at[target].set(pair_grad)
    out_grad = out_grad.reshape(EXPERTS, slot_rows, D)

    def backward(operands):
        gate_latent, down_part, inputs, grads = operands
        gu_weight, gu_slope, dn_weight, dn_slope, pre_gate, pre_up, sigmoid_gate, activated, hidden = expert_forward(gate_latent, down_part, inputs)
        down_grad = jnp.dot(hidden, grads, preferred_element_type=jnp.float32)
        hidden_grad = jnp.dot(dn_weight, grads.T, preferred_element_type=jnp.float32)
        gate_grad = (hidden_grad * pre_up * sigmoid_gate * (1.0 + pre_gate * (1.0 - sigmoid_gate))).astype(jnp.bfloat16)
        up_grad = (hidden_grad * activated).astype(jnp.bfloat16)
        gate_wgrad = jnp.dot(gate_grad, inputs, preferred_element_type=jnp.float32)
        up_wgrad = jnp.dot(up_grad, inputs, preferred_element_type=jnp.float32)
        weight_grads = jnp.stack([gate_wgrad, up_wgrad])
        return (gate_latent - learn_rate * gu_slope * weight_grads, down_part - learn_rate * dn_slope * down_grad)
    new_gate_up, new_down = lax.map(backward, (gate_up_latent, down_latent, dispatched, out_grad))
    return (student_out, new_gate_up, new_down)
```

```python
import functools
import math

import jax
import jax.numpy as jnp
from jax import lax
from jax.experimental import pallas as pl
from jax.experimental.pallas import tpu as pltpu
from jax.sharding import PartitionSpec as P

D = 1024
HID = 384


learn_rate = 1.0


def soften(latent, fan_in):
    row_scale = jnp.mean(jnp.abs(latent), axis=-1, keepdims=True) + 1e-06
    normed = latent / row_scale
    lower = jnp.tanh(4.0 * (normed - 0.5))
    upper = jnp.tanh(4.0 * (normed + 0.5))
    fan_root = 1.0 / math.sqrt(fan_in)
    weight = (row_scale * 0.5 * (lower + upper) * fan_root).astype(jnp.bfloat16)
    slope = 2.0 * (2.0 - lower * lower - upper * upper) * fan_root
    return (weight, slope)


def dispatch_rows(outbox):
    return lax.all_to_all(outbox, ("inner", "outer"), split_axis=0, concat_axis=0, tiled=True)


def combine_rows(outbox):
    return lax.all_to_all(outbox, ("inner", "outer"), split_axis=0, concat_axis=0, tiled=True)


def upstream_rows(outbox):
    return lax.all_to_all(outbox, ("inner", "outer"), split_axis=0, concat_axis=0, tiled=True)


def routed_step(tokens, teacher, expert_ids, gate_codes, gate_up_latent, down_latent):
    experts = lax.axis_size("inner") * lax.axis_size("outer")
    tok_rows, top_count = expert_ids.shape
    part_width = tokens.shape[1]
    capacity = min(tok_rows, 2 * tok_rows * top_count // experts)
    flat_ids = expert_ids.reshape(-1)
    one_hot = (flat_ids[:, None] == jnp.arange(experts, dtype=jnp.int32)[None, :]).astype(jnp.int32)
    before = jnp.cumsum(one_hot, axis=0) - one_hot
    route_slot = jnp.sum(before * one_hot, axis=1)
    target = flat_ids * capacity + route_slot
    payload = jnp.repeat(tokens, top_count, axis=0)
    outbox = jnp.zeros((experts * capacity, part_width), jnp.bfloat16).at[target].set(payload)
    received = dispatch_rows(outbox)
    expert_rows = lax.all_gather(received, "rep", axis=1, tiled=True)
    gu_weight, gu_slope = soften(gate_up_latent[0], D)
    dn_weight, dn_slope = soften(down_latent[0], HID)
    projected = lax.dot_general(
        gu_weight, expert_rows, (((2,), (1,)), ((), ())), preferred_element_type=jnp.float32
    )
    pre_gate = projected[0]
    pre_up = projected[1]
    sigmoid_gate = jax.nn.sigmoid(pre_gate)
    activated = pre_gate * sigmoid_gate
    hidden = (activated * pre_up).astype(jnp.bfloat16)
    partial_out = lax.dot_general(
        hidden, dn_weight, (((0,), (0,)), ((), ())), preferred_element_type=jnp.float32
    )
    expert_out = lax.psum_scatter(
        partial_out.astype(jnp.bfloat16), "rep", scatter_dimension=1, tiled=True
    )
    returned = combine_rows(expert_out)
    picked = returned[target].reshape(tok_rows, top_count, part_width)
    gating = gate_codes.astype(jnp.float32) / 65536.0
    mixed = jnp.sum(gating[:, :, None] * picked.astype(jnp.float32), axis=1)
    student_out = mixed.astype(jnp.bfloat16)
    residual = mixed - teacher.astype(jnp.float32)
    pair_grad = (
        (gating[:, :, None] * residual[:, None, :]).astype(jnp.bfloat16).reshape(-1, part_width)
    )
    grad_outbox = (
        jnp.zeros((experts * capacity, part_width), jnp.bfloat16).at[target].set(pair_grad)
    )
    grad_part = upstream_rows(grad_outbox)
    out_grad = lax.all_gather(grad_part, "rep", axis=1, tiled=True)
    down_grad = jnp.dot(hidden, out_grad, preferred_element_type=jnp.float32)
    hidden_grad = lax.dot_general(
        dn_weight, out_grad, (((1,), (1,)), ((), ())), preferred_element_type=jnp.float32
    )
    gate_grad = (
        hidden_grad * pre_up * sigmoid_gate * (1.0 + pre_gate * (1.0 - sigmoid_gate))
    ).astype(jnp.bfloat16)
    up_grad = (hidden_grad * activated).astype(jnp.bfloat16)
    weight_grads = lax.dot_general(
        jnp.stack([gate_grad, up_grad]),
        expert_rows,
        (((2,), (0,)), ((), ())),
        preferred_element_type=jnp.float32,
    )
    new_gate_up = gate_up_latent - learn_rate * (gu_slope * weight_grads)[None]
    new_down = down_latent - learn_rate * (dn_slope * down_grad)[None]
    return (student_out, new_gate_up, new_down)


MESH = pl.DeviceIdType.MESH
LANES = 128
BF16 = jnp.bfloat16
F32 = jnp.float32


def dot_t(a, b):
    return lax.dot_general(a, b, (((1,), (1,)), ((), ())), preferred_element_type=F32)


def dense_kernel(
    n_inner, n_outer,
    tokens_ref, teacher_ref, ids_ref, codes_ref, gu_ref, dn_ref,
    student_ref, new_gu_ref, new_dn_ref,
    rows, resid, resid_own, gates_own, gates, latent, weight, slope,
    gated_hidden, factor, half_out, half_in, mine, sums, returned,
    load_sem, store_sem, gate_send, gate_recv, tok_send, tok_recv, tok_rep,
    half_send, half_recv, sum_send, sum_recv, res_send, res_recv, res_rep,
):
    n = n_inner * n_outer
    tok_rows, width = tokens_ref.shape
    hid = latent.shape[1]
    inner, outer, rep = lax.axis_index("inner"), lax.axis_index("outer"), lax.axis_index("rep")
    me = inner * n_outer + outer
    partner = {"rep": 1 - rep}

    def inner_at(step):
        return lax.rem(inner + step + n_inner, n_inner)

    def outer_at(step):
        return lax.rem(outer + step + n_outer, n_outer)

    def peer_at(step):
        peer = lax.rem(me + step + n, n)
        return peer, {"inner": peer // n_outer, "outer": lax.rem(peer, n_outer)}

    def remote(source, target, send, recv, device):
        return pltpu.make_async_remote_copy(
            src_ref=source, dst_ref=target, send_sem=send, recv_sem=recv,
            device_id=device, device_id_type=MESH,
        )

    loads = [
        pltpu.make_async_copy(gu_ref.at[0, 0], latent.at[0], load_sem.at[0]),
        pltpu.make_async_copy(gu_ref.at[0, 1], latent.at[1], load_sem.at[1]),
        pltpu.make_async_copy(dn_ref.at[0], latent.at[2], load_sem.at[2]),
    ]
    for load in loads:
        load.start()

    barrier = pltpu.get_barrier_semaphore()
    pl.semaphore_signal(barrier, inc=1, device_id=partner, device_id_type=MESH)
    for step in range(1, n):
        pl.semaphore_signal(barrier, inc=1, device_id=peer_at(step)[1], device_id_type=MESH)
    pl.semaphore_wait(barrier, n)

    def gather_start(own, buf, send, recv, rep_recv):
        sent = []

        def push(source, slot, sem, device):
            copy = remote(source, buf.at[rep, slot], send.at[len(sent)], sem, device)
            copy.start()
            sent.append(copy)

        for step in range(1, n_inner):
            push(own, me, recv.at[me], {"inner": inner_at(step)})
        for step in range(1, n_outer):
            push(own, me, recv.at[me], {"outer": outer_at(step)})
        push(own, me, rep_recv.at[me], partner)
        buf[rep, me] = own[...]
        return sent, push

    def gather_rest(own, buf, send, recv, rep_recv, sent, push, between):
        def arrived(slot):
            remote(own, buf.at[rep, slot], send.at[0], recv.at[slot], partner).wait_recv()

        for step in range(1, n_inner):
            slot = inner_at(-step) * n_outer + outer
            arrived(slot)
            for across in range(1, n_outer):
                push(buf.at[rep, slot], slot, recv.at[slot], {"outer": outer_at(across)})
            push(buf.at[rep, slot], slot, rep_recv.at[slot], partner)
            between()
        for step in range(n_inner):
            for across in range(1, n_outer):
                slot = inner_at(-step) * n_outer + outer_at(-across)
                arrived(slot)
                push(buf.at[rep, slot], slot, rep_recv.at[slot], partner)
            between()
        for slot in range(n):
            remote(own, buf.at[1 - rep, slot], send.at[0], rep_recv.at[slot], partner).wait_recv()
        for copy in sent:
            copy.wait_send()

    tok_sent, tok_push = gather_start(tokens_ref, rows, tok_send, tok_recv, tok_rep)

    ids = ids_ref[...]
    gate_of = codes_ref[...].astype(F32) * (1.0 / 65536.0)
    lane = lax.broadcasted_iota(jnp.int32, (LANES, LANES), 1)
    table = jnp.zeros((LANES, LANES), F32)
    for expert in range(n):
        column = jnp.sum(jnp.where(ids == expert, gate_of, 0.0), axis=1, keepdims=True)
        column = jnp.concatenate([column, jnp.zeros((LANES - tok_rows, 1), F32)], axis=0)
        table = jnp.where(lane == expert, column, table)
    gates_own[...] = table.T[: gates_own.shape[0]]
    gate_sent = []
    for step in range(1, n):
        copy = remote(
            gates_own, gates.at[me], gate_send.at[step - 1], gate_recv.at[me], peer_at(step)[1]
        )
        copy.start()
        gate_sent.append(copy)
    gates[me] = gates_own[...]

    fan_root = [1.0 / math.sqrt(latent.shape[2])] * 2 + [1.0 / math.sqrt(2 * hid)]
    piece = 32

    def soften_rows(matrix, first, last):
        root = fan_root[matrix]

        def body(at, carry):
            part = pl.ds(pl.multiple_of(at * piece, piece), piece)
            value = latent[matrix, part, :]
            row_scale = jnp.mean(jnp.abs(value), axis=-1, keepdims=True) + 1e-06
            normed = value / row_scale
            lower = jnp.tanh(4.0 * (normed - 0.5))
            upper = jnp.tanh(4.0 * (normed + 0.5))
            weight[matrix, part, :] = (row_scale * (0.5 * root) * (lower + upper)).astype(BF16)
            slope[matrix, part, :] = (2.0 * root) * (2.0 - lower * lower - upper * upper)
            return carry

        lax.fori_loop(first, last, body, 0)

    half = hid // piece // 2
    work = [(m, a, b) for m in range(3) for a, b in ((0, half), (half, hid // piece))]

    def soften_next():
        if work:
            matrix, first, last = work.pop(0)
            if first == 0:
                loads[matrix].wait()
            soften_rows(matrix, first, last)

    soften_next()
    gather_rest(
        tokens_ref, rows, tok_send, tok_recv, tok_rep, tok_sent, tok_push, soften_next
    )
    while work:
        soften_next()

    for step in range(1, n):
        slot = peer_at(-step)[0]
        remote(gates_own, gates.at[slot], gate_send.at[0], gate_recv.at[slot], partner).wait_recv()
    for copy in gate_sent:
        copy.wait_send()
    spread = LANES // tok_rows
    gate_row = jnp.concatenate(
        [
            sum(
                pltpu.roll(gates[base + at, pl.ds(me, 1), :], at * tok_rows, 1) if at
                else gates[base, pl.ds(me, 1), :]
                for at in range(spread)
            )
            for base in range(0, n, spread)
        ],
        axis=1,
    )

    def flat(ref, index):
        return ref[index].reshape(n * tok_rows, width)

    both = weight[0:2].reshape(2 * hid, 2 * width)
    pre = dot_t(both[:, :width], flat(rows, 0)) + dot_t(both[:, width:], flat(rows, 1))
    pre_gate, pre_up = pre[:hid], pre[hid:]
    sigmoid_gate = jax.nn.sigmoid(pre_gate)
    activated = pre_gate * sigmoid_gate
    hidden = activated * pre_up * gate_row
    gated_hidden[...] = hidden.astype(BF16)
    hidden_t = hidden.T.astype(BF16)

    other_cols = pl.ds(pl.multiple_of((1 - rep) * width, width), width)
    own_cols = pl.ds(pl.multiple_of(rep * width, width), width)
    half_out[...] = (
        jnp.dot(hidden_t, weight[2, :, other_cols], preferred_element_type=F32)
        .astype(BF16).reshape(n, tok_rows, width)
    )
    order = [peer_at(step) for step in range(1, n)] + [(me, None)]
    half_sent = []
    for slot, _ in order:
        copy = remote(half_out.at[slot], half_in.at[slot], half_send.at[slot], half_recv.at[slot], partner)
        copy.start()
        half_sent.append(copy)
    mine[...] = jnp.dot(
        hidden_t, weight[2, :, own_cols], preferred_element_type=F32
    ).reshape(n, tok_rows, width)

    sum_sent = []
    for at, (slot, device) in enumerate(order):
        half_sent[at].wait_recv()
        total = mine[slot] + half_in[slot].astype(F32)
        if device is None:
            mine[slot] = total
        else:
            sums[slot] = total.astype(BF16)
            copy = remote(
                sums.at[slot], returned.at[me], sum_send.at[at], sum_recv.at[me], device
            )
            copy.start()
            sum_sent.append(copy)

    factor[0] = gate_row * pre_up * sigmoid_gate * (1.0 + pre_gate * (1.0 - sigmoid_gate))
    factor[1] = gate_row * activated

    mixed = mine[me]
    for step in range(1, n):
        slot = peer_at(-step)[0]
        remote(resid_own, returned.at[slot], sum_send.at[0], sum_recv.at[slot], partner).wait_recv()
        mixed = mixed + returned[slot].astype(F32)
    student_ref[...] = mixed.astype(BF16)
    resid_own[...] = (mixed - teacher_ref[...].astype(F32)).astype(BF16)

    res_sent, res_push = gather_start(resid_own, resid, res_send, res_recv, res_rep)
    gather_rest(
        resid_own, resid, res_send, res_recv, res_rep, res_sent, res_push, lambda: None
    )
    for copy in half_sent + sum_sent:
        copy.wait_send()

    down = weight[2]
    hidden_grad = dot_t(down[:, :width], flat(resid, 0)) + dot_t(down[:, width:], flat(resid, 1))
    grads = [
        (hidden_grad * factor[0]).astype(BF16),
        (hidden_grad * factor[1]).astype(BF16),
        gated_hidden[...],
    ]
    targets = [new_gu_ref.at[0, 0], new_gu_ref.at[0, 1], new_dn_ref.at[0]]
    tile = min(width, 256)
    stores = []
    for matrix in (2, 0, 1):
        source = resid if matrix == 2 else rows
        for side in range(2):
            for first in range(0, width, tile):
                block = source[side, :, :, first : first + tile].reshape(n * tok_rows, tile)
                grad = jnp.dot(grads[matrix], block, preferred_element_type=F32)
                cols = slice(side * width + first, side * width + first + tile)
                slope[matrix, :, cols] = latent[matrix, :, cols] - learn_rate * (
                    slope[matrix, :, cols] * grad
                )
        store = pltpu.make_async_copy(slope.at[matrix], targets[matrix], store_sem.at[matrix])
        store.start()
        stores.append(store)
    for store in stores:
        store.wait()


def dense_step(tokens, teacher, expert_ids, gate_codes, gate_up_latent, down_latent):
    n_inner, n_outer = lax.axis_size("inner"), lax.axis_size("outer")
    n = n_inner * n_outer
    tok_rows, width = tokens.shape
    hid, full = down_latent.shape[1:]
    sublanes = -(-n // 8) * 8
    gather_sends = (n_inner - 1) * (1 + n_outer) + (n_outer - 1) * (1 + n_inner) + 1
    dma = pltpu.SemaphoreType.DMA
    block = (n, tok_rows, width)
    vmem = pl.BlockSpec(memory_space=pltpu.VMEM)
    hbm = pl.BlockSpec(memory_space=pl.ANY)
    return pl.pallas_call(
        functools.partial(dense_kernel, n_inner, n_outer),
        out_shape=(
            jax.ShapeDtypeStruct(tokens.shape, BF16),
            jax.ShapeDtypeStruct(gate_up_latent.shape, F32),
            jax.ShapeDtypeStruct(down_latent.shape, F32),
        ),
        in_specs=[vmem, vmem, vmem, vmem, hbm, hbm],
        out_specs=(vmem, hbm, hbm),
        scratch_shapes=[
            pltpu.VMEM((2, *block), BF16),
            pltpu.VMEM((2, *block), BF16),
            pltpu.VMEM((tok_rows, width), BF16),
            pltpu.VMEM((sublanes, LANES), F32),
            pltpu.VMEM((n, sublanes, LANES), F32),
            pltpu.VMEM((3, hid, full), F32),
            pltpu.VMEM((3, hid, full), BF16),
            pltpu.VMEM((3, hid, full), F32),
            pltpu.VMEM((hid, n * tok_rows), BF16),
            pltpu.VMEM((2, hid, n * tok_rows), F32),
            pltpu.VMEM(block, BF16),
            pltpu.VMEM(block, BF16),
            pltpu.VMEM(block, F32),
            pltpu.VMEM(block, BF16),
            pltpu.VMEM(block, BF16),
            dma((3,)),
            dma((3,)),
            dma((n,)),
            dma((n,)),
            dma((gather_sends,)),
            dma((n,)),
            dma((n,)),
            dma((n,)),
            dma((n,)),
            dma((n,)),
            dma((n,)),
            dma((gather_sends,)),
            dma((n,)),
            dma((n,)),
        ],
        compiler_params=pltpu.CompilerParams(
            collective_id=0, has_side_effects=True, vmem_limit_bytes=40 * 1024 * 1024
        ),
    )(tokens, teacher, expert_ids, gate_codes, gate_up_latent, down_latent)


def on_device(tokens, teacher, expert_ids, gate_codes, gate_up_latent, down_latent):
    experts = lax.axis_size("inner") * lax.axis_size("outer")
    tok_rows, top_count = expert_ids.shape
    whole_block = 2 * top_count >= experts
    fits = (
        lax.axis_size("rep") == 2
        and LANES % tok_rows == 0
        and tok_rows % 16 == 0
        and experts <= LANES
        and experts * tok_rows % LANES == 0
        and tokens.shape[1] % LANES == 0
        and down_latent.shape[1] % 64 == 0
    )
    step = dense_step if whole_block and fits else routed_step
    return step(tokens, teacher, expert_ids, gate_codes, gate_up_latent, down_latent)


def solution(mesh):
    return jax.shard_map(
        on_device,
        mesh=mesh,
        in_specs=(
            P(("parts", "inner", "outer"), "rep"),
            P(("parts", "inner", "outer"), "rep"),
            P(("parts", "inner", "outer"), None),
            P(("parts", "inner", "outer"), None),
            P(("inner", "outer"), None, "rep", None),
            P(("inner", "outer"), "rep", None),
        ),
        out_specs=(
            P(("parts", "inner", "outer"), "rep"),
            P(("parts", "inner", "outer"), None, "rep", None),
            P(("parts", "inner", "outer"), "rep", None),
        ),
        check_vma=False,
    )
```

```python
import functools
import math

import jax
import jax.numpy as jnp
from jax import lax
from jax.experimental import pallas as pl
from jax.experimental.pallas import tpu as pltpu
from jax.sharding import PartitionSpec as P

D = 1024
HID = 384


learn_rate = 1.0


def soften(latent, fan_in):
    row_scale = jnp.mean(jnp.abs(latent), axis=-1, keepdims=True) + 1e-06
    normed = latent / row_scale
    lower = jnp.tanh(4.0 * (normed - 0.5))
    upper = jnp.tanh(4.0 * (normed + 0.5))
    fan_root = 1.0 / math.sqrt(fan_in)
    weight = (row_scale * 0.5 * (lower + upper) * fan_root).astype(jnp.bfloat16)
    slope = 2.0 * (2.0 - lower * lower - upper * upper) * fan_root
    return (weight, slope)


def dispatch_rows(outbox):
    return lax.all_to_all(outbox, ("inner", "outer"), split_axis=0, concat_axis=0, tiled=True)


def combine_rows(outbox):
    return lax.all_to_all(outbox, ("inner", "outer"), split_axis=0, concat_axis=0, tiled=True)


def upstream_rows(outbox):
    return lax.all_to_all(outbox, ("inner", "outer"), split_axis=0, concat_axis=0, tiled=True)


def routed_step(tokens, teacher, expert_ids, gate_codes, gate_up_latent, down_latent):
    experts = lax.axis_size("inner") * lax.axis_size("outer")
    tok_rows, top_count = expert_ids.shape
    part_width = tokens.shape[1]
    capacity = min(tok_rows, 2 * tok_rows * top_count // experts)
    flat_ids = expert_ids.reshape(-1)
    one_hot = (flat_ids[:, None] == jnp.arange(experts, dtype=jnp.int32)[None, :]).astype(jnp.int32)
    before = jnp.cumsum(one_hot, axis=0) - one_hot
    route_slot = jnp.sum(before * one_hot, axis=1)
    target = flat_ids * capacity + route_slot
    payload = jnp.repeat(tokens, top_count, axis=0)
    outbox = jnp.zeros((experts * capacity, part_width), jnp.bfloat16).at[target].set(payload)
    received = dispatch_rows(outbox)
    expert_rows = lax.all_gather(received, "rep", axis=1, tiled=True)
    gu_weight, gu_slope = soften(gate_up_latent[0], D)
    dn_weight, dn_slope = soften(down_latent[0], HID)
    projected = lax.dot_general(
        gu_weight, expert_rows, (((2,), (1,)), ((), ())), preferred_element_type=jnp.float32
    )
    pre_gate = projected[0]
    pre_up = projected[1]
    sigmoid_gate = jax.nn.sigmoid(pre_gate)
    activated = pre_gate * sigmoid_gate
    hidden = (activated * pre_up).astype(jnp.bfloat16)
    partial_out = lax.dot_general(
        hidden, dn_weight, (((0,), (0,)), ((), ())), preferred_element_type=jnp.float32
    )
    expert_out = lax.psum_scatter(
        partial_out.astype(jnp.bfloat16), "rep", scatter_dimension=1, tiled=True
    )
    returned = combine_rows(expert_out)
    picked = returned[target].reshape(tok_rows, top_count, part_width)
    gating = gate_codes.astype(jnp.float32) / 65536.0
    mixed = jnp.sum(gating[:, :, None] * picked.astype(jnp.float32), axis=1)
    student_out = mixed.astype(jnp.bfloat16)
    residual = mixed - teacher.astype(jnp.float32)
    pair_grad = (
        (gating[:, :, None] * residual[:, None, :]).astype(jnp.bfloat16).reshape(-1, part_width)
    )
    grad_outbox = (
        jnp.zeros((experts * capacity, part_width), jnp.bfloat16).at[target].set(pair_grad)
    )
    grad_part = upstream_rows(grad_outbox)
    out_grad = lax.all_gather(grad_part, "rep", axis=1, tiled=True)
    down_grad = jnp.dot(hidden, out_grad, preferred_element_type=jnp.float32)
    hidden_grad = lax.dot_general(
        dn_weight, out_grad, (((1,), (1,)), ((), ())), preferred_element_type=jnp.float32
    )
    gate_grad = (
        hidden_grad * pre_up * sigmoid_gate * (1.0 + pre_gate * (1.0 - sigmoid_gate))
    ).astype(jnp.bfloat16)
    up_grad = (hidden_grad * activated).astype(jnp.bfloat16)
    weight_grads = lax.dot_general(
        jnp.stack([gate_grad, up_grad]),
        expert_rows,
        (((2,), (0,)), ((), ())),
        preferred_element_type=jnp.float32,
    )
    new_gate_up = gate_up_latent - learn_rate * (gu_slope * weight_grads)[None]
    new_down = down_latent - learn_rate * (dn_slope * down_grad)[None]
    return (student_out, new_gate_up, new_down)


MESH = pl.DeviceIdType.MESH
LANES = 128
BF16 = jnp.bfloat16
F32 = jnp.float32


def dot_t(a, b):
    return lax.dot_general(a, b, (((1,), (1,)), ((), ())), preferred_element_type=F32)


def dense_kernel(
    n_inner, n_outer,
    tokens_ref, teacher_ref, ids_ref, codes_ref, gu_ref, dn_ref,
    student, grads, rows, resid, latent, slope,
    teacher, ids, codes, resid_own, gates_own, gates, weight,
    factor, half_out, half_in, mine, sums, returned,
    load_sem, gate_send, gate_recv, tok_send, tok_recv, tok_rep,
    half_send, half_recv, sum_send, sum_recv, res_send, res_recv, res_rep,
):
    n = n_inner * n_outer
    tok_rows, width = tokens_ref.shape
    hid = latent.shape[1]
    inner, outer, rep = lax.axis_index("inner"), lax.axis_index("outer"), lax.axis_index("rep")
    me = inner * n_outer + outer
    partner = {"rep": 1 - rep}

    def inner_at(step):
        return lax.rem(inner + step + n_inner, n_inner)

    def outer_at(step):
        return lax.rem(outer + step + n_outer, n_outer)

    def peer_at(step):
        peer = lax.rem(me + step + n, n)
        return peer, {"inner": peer // n_outer, "outer": lax.rem(peer, n_outer)}

    def remote(source, target, send, recv, device):
        return pltpu.make_async_remote_copy(
            src_ref=source, dst_ref=target, send_sem=send, recv_sem=recv,
            device_id=device, device_id_type=MESH,
        )

    loads = [
        pltpu.make_async_copy(gu_ref.at[0, 0], latent.at[0], load_sem.at[0]),
        pltpu.make_async_copy(gu_ref.at[0, 1], latent.at[1], load_sem.at[1]),
        pltpu.make_async_copy(dn_ref.at[0], latent.at[2], load_sem.at[2]),
        pltpu.make_async_copy(tokens_ref, rows.at[rep, me], load_sem.at[3]),
        pltpu.make_async_copy(teacher_ref, teacher, load_sem.at[4]),
        pltpu.make_async_copy(ids_ref, ids, load_sem.at[5]),
        pltpu.make_async_copy(codes_ref, codes, load_sem.at[6]),
    ]
    for load in loads:
        load.start()

    barrier = pltpu.get_barrier_semaphore()
    pl.semaphore_signal(barrier, inc=1, device_id=partner, device_id_type=MESH)
    for step in range(1, n):
        pl.semaphore_signal(barrier, inc=1, device_id=peer_at(step)[1], device_id_type=MESH)
    pl.semaphore_wait(barrier, n)

    def gather_start(own, buf, send, recv, rep_recv):
        sent = []

        def push(source, slot, sem, device):
            copy = remote(source, buf.at[rep, slot], send.at[len(sent)], sem, device)
            copy.start()
            sent.append(copy)

        for step in range(1, n_inner):
            push(own, me, recv.at[me], {"inner": inner_at(step)})
        for step in range(1, n_outer):
            push(own, me, recv.at[me], {"outer": outer_at(step)})
        push(own, me, rep_recv.at[me], partner)
        return sent, push

    def gather_rest(own, buf, send, recv, rep_recv, sent, push, between):
        def arrived(slot):
            remote(own, buf.at[rep, slot], send.at[0], recv.at[slot], partner).wait_recv()

        for step in range(1, n_inner):
            slot = inner_at(-step) * n_outer + outer
            arrived(slot)
            for across in range(1, n_outer):
                push(buf.at[rep, slot], slot, recv.at[slot], {"outer": outer_at(across)})
            push(buf.at[rep, slot], slot, rep_recv.at[slot], partner)
            between()
        for step in range(n_inner):
            for across in range(1, n_outer):
                slot = inner_at(-step) * n_outer + outer_at(-across)
                arrived(slot)
                push(buf.at[rep, slot], slot, rep_recv.at[slot], partner)
            between()
        for slot in range(n):
            remote(own, buf.at[1 - rep, slot], send.at[0], rep_recv.at[slot], partner).wait_recv()

    tok_sent, tok_push = gather_start(tokens_ref, rows, tok_send, tok_recv, tok_rep)

    loads[5].wait()
    loads[6].wait()
    gate_of = codes[...].astype(F32) * (1.0 / 65536.0)
    line = lax.broadcasted_iota(jnp.int32, (gates_own.shape[0], tok_rows), 0)
    table = jnp.zeros((gates_own.shape[0], tok_rows), F32)
    for expert in range(n):
        row = jnp.sum(jnp.where(ids[...] == expert, gate_of, 0.0), axis=0, keepdims=True)
        table = jnp.where(line == expert, row, table)
    gates_own[...] = jnp.zeros_like(gates_own)
    gates_own[:, :tok_rows] = table
    gate_sent = []
    for step in range(1, n):
        copy = remote(
            gates_own, gates.at[me], gate_send.at[step - 1], gate_recv.at[me], peer_at(step)[1]
        )
        copy.start()
        gate_sent.append(copy)
    gates[me] = gates_own[...]

    fan_root = [1.0 / math.sqrt(latent.shape[2])] * 2 + [1.0 / math.sqrt(2 * hid)]
    piece = 32

    def soften_rows(matrix, first, last):
        root = fan_root[matrix]

        def body(at, carry):
            part = pl.ds(pl.multiple_of(at * piece, piece), piece)
            value = latent[matrix, part, :]
            row_scale = jnp.mean(jnp.abs(value), axis=-1, keepdims=True) + 1e-06
            normed = value / row_scale
            lower = jnp.tanh(4.0 * (normed - 0.5))
            upper = jnp.tanh(4.0 * (normed + 0.5))
            weight[matrix, part, :] = (row_scale * (0.5 * root) * (lower + upper)).astype(BF16)
            slope[matrix, part, :] = (2.0 * root) * (2.0 - lower * lower - upper * upper)
            return carry

        lax.fori_loop(first, last, body, 0)

    half = hid // piece // 2
    work = [(m, a, b) for m in range(3) for a, b in ((0, half), (half, hid // piece))]

    def soften_next():
        if work:
            matrix, first, last = work.pop(0)
            if first == 0:
                loads[matrix].wait()
            soften_rows(matrix, first, last)

    soften_next()
    gather_rest(
        tokens_ref, rows, tok_send, tok_recv, tok_rep, tok_sent, tok_push, soften_next
    )
    while work:
        soften_next()
    loads[3].wait()

    for step in range(1, n):
        slot = peer_at(-step)[0]
        remote(gates_own, gates.at[slot], gate_send.at[0], gate_recv.at[slot], partner).wait_recv()
    spread = LANES // tok_rows
    gate_row = jnp.concatenate(
        [
            sum(
                pltpu.roll(gates[base + at, pl.ds(me, 1), :], at * tok_rows, 1) if at
                else gates[base, pl.ds(me, 1), :]
                for at in range(spread)
            )
            for base in range(0, n, spread)
        ],
        axis=1,
    )

    def flat(ref, index):
        return ref[index].reshape(n * tok_rows, width)

    both = weight[0:2].reshape(2 * hid, 2 * width)
    pre = dot_t(both[:, :width], flat(rows, 0)) + dot_t(both[:, width:], flat(rows, 1))
    pre_gate, pre_up = pre[:hid], pre[hid:]
    sigmoid_gate = jax.nn.sigmoid(pre_gate)
    activated = pre_gate * sigmoid_gate
    hidden = activated * pre_up * gate_row
    grads[2] = hidden.astype(BF16)
    hidden_t = hidden.T.astype(BF16)

    other_cols = pl.ds(pl.multiple_of((1 - rep) * width, width), width)
    own_cols = pl.ds(pl.multiple_of(rep * width, width), width)
    half_out[...] = (
        jnp.dot(hidden_t, weight[2, :, other_cols], preferred_element_type=F32)
        .astype(BF16).reshape(n, tok_rows, width)
    )
    order = [peer_at(step) for step in range(1, n)] + [(me, None)]
    half_sent = []
    for slot, _ in order:
        copy = remote(half_out.at[slot], half_in.at[slot], half_send.at[slot], half_recv.at[slot], partner)
        copy.start()
        half_sent.append(copy)
    mine[...] = jnp.dot(
        hidden_t, weight[2, :, own_cols], preferred_element_type=F32
    ).reshape(n, tok_rows, width)

    sum_sent = []
    for at, (slot, device) in enumerate(order):
        half_sent[at].wait_recv()
        total = mine[slot] + half_in[slot].astype(F32)
        if device is None:
            mine[slot] = total
        else:
            sums[slot] = total.astype(BF16)
            copy = remote(
                sums.at[slot], returned.at[me], sum_send.at[at], sum_recv.at[me], device
            )
            copy.start()
            sum_sent.append(copy)

    factor[0] = gate_row * pre_up * sigmoid_gate * (1.0 + pre_gate * (1.0 - sigmoid_gate))
    factor[1] = gate_row * activated

    mixed = mine[me]
    for step in range(1, n):
        slot = peer_at(-step)[0]
        remote(resid_own, returned.at[slot], sum_send.at[0], sum_recv.at[slot], partner).wait_recv()
        mixed = mixed + returned[slot].astype(F32)
    student[...] = mixed.astype(BF16)
    loads[4].wait()
    resid_own[...] = (mixed - teacher[...].astype(F32)).astype(BF16)
    resid[rep, me] = resid_own[...]

    res_sent, res_push = gather_start(resid_own, resid, res_send, res_recv, res_rep)
    gather_rest(
        resid_own, resid, res_send, res_recv, res_rep, res_sent, res_push, lambda: None
    )

    down = weight[2]
    hidden_grad = dot_t(down[:, :width], flat(resid, 0)) + dot_t(down[:, width:], flat(resid, 1))
    grads[0] = (hidden_grad * factor[0]).astype(BF16)
    grads[1] = (hidden_grad * factor[1]).astype(BF16)
    for copy in tok_sent + gate_sent + half_sent + sum_sent + res_sent:
        copy.wait_send()


def update_kernel(
    student, grads, rows, resid, latent, slope,
    student_ref, new_gu_ref, new_dn_ref, fresh, store_sem,
):
    n, tok_rows, width = rows.shape[1:]
    stores = [pltpu.make_async_copy(student, student_ref, store_sem.at[3])]
    stores[0].start()
    targets = [new_gu_ref.at[0, 0], new_gu_ref.at[0, 1], new_dn_ref.at[0]]
    tile = min(width, 256)
    for matrix in range(3):
        source = resid if matrix == 2 else rows
        for side in range(2):
            for first in range(0, width, tile):
                block = source[side, :, :, first : first + tile].reshape(n * tok_rows, tile)
                grad = jnp.dot(grads[matrix], block, preferred_element_type=F32)
                cols = slice(side * width + first, side * width + first + tile)
                fresh[matrix, :, cols] = latent[matrix, :, cols] - learn_rate * (
                    slope[matrix, :, cols] * grad
                )
        store = pltpu.make_async_copy(fresh.at[matrix], targets[matrix], store_sem.at[matrix])
        store.start()
        stores.append(store)
    for store in stores:
        store.wait()


def dense_step(tokens, teacher, expert_ids, gate_codes, gate_up_latent, down_latent):
    n_inner, n_outer = lax.axis_size("inner"), lax.axis_size("outer")
    n = n_inner * n_outer
    tok_rows, width = tokens.shape
    hid, full = down_latent.shape[1:]
    sublanes = -(-n // 8) * 8
    gather_sends = (n_inner - 1) * (1 + n_outer) + (n_outer - 1) * (1 + n_inner) + 1
    dma = pltpu.SemaphoreType.DMA
    block = (n, tok_rows, width)
    vmem = pl.BlockSpec(memory_space=pltpu.VMEM)
    hbm = pl.BlockSpec(memory_space=pltpu.HBM)
    inputs = (tokens, teacher, expert_ids.T, gate_codes.T, gate_up_latent, down_latent)
    state = pl.pallas_call(
        functools.partial(dense_kernel, n_inner, n_outer),
        out_shape=(
            jax.ShapeDtypeStruct(tokens.shape, BF16),
            jax.ShapeDtypeStruct((3, hid, n * tok_rows), BF16),
            jax.ShapeDtypeStruct((2, *block), BF16),
            jax.ShapeDtypeStruct((2, *block), BF16),
            jax.ShapeDtypeStruct((3, hid, full), F32),
            jax.ShapeDtypeStruct((3, hid, full), F32),
        ),
        in_specs=[hbm] * 6,
        out_specs=(vmem,) * 6,
        scratch_shapes=[
            pltpu.VMEM((tok_rows, width), BF16),
            pltpu.VMEM(expert_ids.shape[::-1], jnp.int32),
            pltpu.VMEM(expert_ids.shape[::-1], jnp.int32),
            pltpu.VMEM((tok_rows, width), BF16),
            pltpu.VMEM((sublanes, LANES), F32),
            pltpu.VMEM((n, sublanes, LANES), F32),
            pltpu.VMEM((3, hid, full), BF16),
            pltpu.VMEM((2, hid, n * tok_rows), F32),
            pltpu.VMEM(block, BF16),
            pltpu.VMEM(block, BF16),
            pltpu.VMEM(block, F32),
            pltpu.VMEM(block, BF16),
            pltpu.VMEM(block, BF16),
            dma((7,)),
            dma((n,)),
            dma((n,)),
            dma((gather_sends,)),
            dma((n,)),
            dma((n,)),
            dma((n,)),
            dma((n,)),
            dma((n,)),
            dma((n,)),
            dma((gather_sends,)),
            dma((n,)),
            dma((n,)),
        ],
        compiler_params=pltpu.CompilerParams(
            collective_id=0, has_side_effects=True, vmem_limit_bytes=24 * 1024 * 1024
        ),
    )(*[pltpu.with_memory_space_constraint(value, pltpu.HBM) for value in inputs])
    return pl.pallas_call(
        update_kernel,
        out_shape=(
            jax.ShapeDtypeStruct(tokens.shape, BF16),
            jax.ShapeDtypeStruct(gate_up_latent.shape, F32),
            jax.ShapeDtypeStruct(down_latent.shape, F32),
        ),
        in_specs=[vmem] * 6,
        out_specs=(hbm,) * 3,
        scratch_shapes=[pltpu.VMEM((3, hid, full), F32), dma((4,))],
        compiler_params=pltpu.CompilerParams(vmem_limit_bytes=24 * 1024 * 1024),
    )(*state)


def on_device(tokens, teacher, expert_ids, gate_codes, gate_up_latent, down_latent):
    experts = lax.axis_size("inner") * lax.axis_size("outer")
    tok_rows, top_count = expert_ids.shape
    whole_block = 2 * top_count >= experts
    fits = (
        lax.axis_size("rep") == 2
        and LANES % tok_rows == 0
        and tok_rows % 16 == 0
        and experts <= LANES
        and experts * tok_rows % LANES == 0
        and tokens.shape[1] % LANES == 0
        and down_latent.shape[1] % 64 == 0
    )
    step = dense_step if whole_block and fits else routed_step
    return step(tokens, teacher, expert_ids, gate_codes, gate_up_latent, down_latent)


def solution(mesh):
    return jax.shard_map(
        on_device,
        mesh=mesh,
        in_specs=(
            P(("parts", "inner", "outer"), "rep"),
            P(("parts", "inner", "outer"), "rep"),
            P(("parts", "inner", "outer"), None),
            P(("parts", "inner", "outer"), None),
            P(("inner", "outer"), None, "rep", None),
            P(("inner", "outer"), "rep", None),
        ),
        out_specs=(
            P(("parts", "inner", "outer"), "rep"),
            P(("parts", "inner", "outer"), None, "rep", None),
            P(("parts", "inner", "outer"), "rep", None),
        ),
        check_vma=False,
    )
```

```python
import functools
import math

import jax
import jax.numpy as jnp
from jax import lax
from jax.experimental import pallas as pl
from jax.experimental.pallas import tpu as pltpu
from jax.sharding import PartitionSpec as P

D = 1024
HID = 384


learn_rate = 1.0


def soften(latent, fan_in):
    row_scale = jnp.mean(jnp.abs(latent), axis=-1, keepdims=True) + 1e-06
    normed = latent / row_scale
    lower = jnp.tanh(4.0 * (normed - 0.5))
    upper = jnp.tanh(4.0 * (normed + 0.5))
    fan_root = 1.0 / math.sqrt(fan_in)
    weight = (row_scale * 0.5 * (lower + upper) * fan_root).astype(jnp.bfloat16)
    slope = 2.0 * (2.0 - lower * lower - upper * upper) * fan_root
    return (weight, slope)


def dispatch_rows(outbox):
    return lax.all_to_all(outbox, ("inner", "outer"), split_axis=0, concat_axis=0, tiled=True)


def combine_rows(outbox):
    return lax.all_to_all(outbox, ("inner", "outer"), split_axis=0, concat_axis=0, tiled=True)


def upstream_rows(outbox):
    return lax.all_to_all(outbox, ("inner", "outer"), split_axis=0, concat_axis=0, tiled=True)


def routed_step(tokens, teacher, expert_ids, gate_codes, gate_up_latent, down_latent):
    experts = lax.axis_size("inner") * lax.axis_size("outer")
    tok_rows, top_count = expert_ids.shape
    part_width = tokens.shape[1]
    capacity = min(tok_rows, 2 * tok_rows * top_count // experts)
    flat_ids = expert_ids.reshape(-1)
    one_hot = (flat_ids[:, None] == jnp.arange(experts, dtype=jnp.int32)[None, :]).astype(jnp.int32)
    before = jnp.cumsum(one_hot, axis=0) - one_hot
    route_slot = jnp.sum(before * one_hot, axis=1)
    target = flat_ids * capacity + route_slot
    payload = jnp.repeat(tokens, top_count, axis=0)
    outbox = jnp.zeros((experts * capacity, part_width), jnp.bfloat16).at[target].set(payload)
    received = dispatch_rows(outbox)
    expert_rows = lax.all_gather(received, "rep", axis=1, tiled=True)
    gu_weight, gu_slope = soften(gate_up_latent[0], D)
    dn_weight, dn_slope = soften(down_latent[0], HID)
    projected = lax.dot_general(
        gu_weight, expert_rows, (((2,), (1,)), ((), ())), preferred_element_type=jnp.float32
    )
    pre_gate = projected[0]
    pre_up = projected[1]
    sigmoid_gate = jax.nn.sigmoid(pre_gate)
    activated = pre_gate * sigmoid_gate
    hidden = (activated * pre_up).astype(jnp.bfloat16)
    partial_out = lax.dot_general(
        hidden, dn_weight, (((0,), (0,)), ((), ())), preferred_element_type=jnp.float32
    )
    expert_out = lax.psum_scatter(
        partial_out.astype(jnp.bfloat16), "rep", scatter_dimension=1, tiled=True
    )
    returned = combine_rows(expert_out)
    picked = returned[target].reshape(tok_rows, top_count, part_width)
    gating = gate_codes.astype(jnp.float32) / 65536.0
    mixed = jnp.sum(gating[:, :, None] * picked.astype(jnp.float32), axis=1)
    student_out = mixed.astype(jnp.bfloat16)
    residual = mixed - teacher.astype(jnp.float32)
    pair_grad = (
        (gating[:, :, None] * residual[:, None, :]).astype(jnp.bfloat16).reshape(-1, part_width)
    )
    grad_outbox = (
        jnp.zeros((experts * capacity, part_width), jnp.bfloat16).at[target].set(pair_grad)
    )
    grad_part = upstream_rows(grad_outbox)
    out_grad = lax.all_gather(grad_part, "rep", axis=1, tiled=True)
    down_grad = jnp.dot(hidden, out_grad, preferred_element_type=jnp.float32)
    hidden_grad = lax.dot_general(
        dn_weight, out_grad, (((1,), (1,)), ((), ())), preferred_element_type=jnp.float32
    )
    gate_grad = (
        hidden_grad * pre_up * sigmoid_gate * (1.0 + pre_gate * (1.0 - sigmoid_gate))
    ).astype(jnp.bfloat16)
    up_grad = (hidden_grad * activated).astype(jnp.bfloat16)
    weight_grads = lax.dot_general(
        jnp.stack([gate_grad, up_grad]),
        expert_rows,
        (((2,), (0,)), ((), ())),
        preferred_element_type=jnp.float32,
    )
    new_gate_up = gate_up_latent - learn_rate * (gu_slope * weight_grads)[None]
    new_down = down_latent - learn_rate * (dn_slope * down_grad)[None]
    return (student_out, new_gate_up, new_down)


MESH = pl.DeviceIdType.MESH
LANES = 128
BF16 = jnp.bfloat16
F32 = jnp.float32


def dot_t(a, b):
    return lax.dot_general(a, b, (((1,), (1,)), ((), ())), preferred_element_type=F32)


def dense_kernel(
    n_inner, n_outer,
    tokens_ref, teacher_ref, ids_ref, codes_ref, gu_ref, dn_ref,
    student, grads, rows, resid, latent, slope,
    teacher, ids, codes, resid_own, gates_own, gates, weight,
    factor, half_out, half_in, mine, sums, crossed, returned,
    load_sem, gate_send, gate_recv, tok_send, tok_recv, tok_rep,
    half_send, half_recv, sum_send, sum_recv, cross_recv, res_send, res_recv, res_rep,
):
    n = n_inner * n_outer
    tok_rows, width = tokens_ref.shape
    hid = latent.shape[1]
    inner, outer, rep = lax.axis_index("inner"), lax.axis_index("outer"), lax.axis_index("rep")
    me = inner * n_outer + outer
    partner = {"rep": 1 - rep}

    def inner_at(step):
        return lax.rem(inner + step + n_inner, n_inner)

    def outer_at(step):
        return lax.rem(outer + step + n_outer, n_outer)

    def peer_at(step):
        peer = lax.rem(me + step + n, n)
        return peer, {"inner": peer // n_outer, "outer": lax.rem(peer, n_outer)}

    def remote(source, target, send, recv, device):
        return pltpu.make_async_remote_copy(
            src_ref=source, dst_ref=target, send_sem=send, recv_sem=recv,
            device_id=device, device_id_type=MESH,
        )

    loads = [
        pltpu.make_async_copy(gu_ref.at[0, 0], latent.at[0], load_sem.at[0]),
        pltpu.make_async_copy(gu_ref.at[0, 1], latent.at[1], load_sem.at[1]),
        pltpu.make_async_copy(dn_ref.at[0], latent.at[2], load_sem.at[2]),
        pltpu.make_async_copy(tokens_ref, rows.at[rep, me], load_sem.at[3]),
        pltpu.make_async_copy(teacher_ref, teacher, load_sem.at[4]),
        pltpu.make_async_copy(ids_ref, ids, load_sem.at[5]),
        pltpu.make_async_copy(codes_ref, codes, load_sem.at[6]),
    ]
    for load in loads:
        load.start()

    barrier = pltpu.get_barrier_semaphore()
    pl.semaphore_signal(barrier, inc=1, device_id=partner, device_id_type=MESH)
    for step in range(1, n):
        pl.semaphore_signal(barrier, inc=1, device_id=peer_at(step)[1], device_id_type=MESH)
    pl.semaphore_wait(barrier, n)

    def gather_start(own, buf, send, recv, rep_recv):
        sent = []

        def push(source, slot, sem, device):
            copy = remote(source, buf.at[rep, slot], send.at[len(sent)], sem, device)
            copy.start()
            sent.append(copy)

        for step in range(1, n_inner):
            push(own, me, recv.at[me], {"inner": inner_at(step)})
        for step in range(1, n_outer):
            push(own, me, recv.at[me], {"outer": outer_at(step)})
        push(own, me, rep_recv.at[me], partner)
        return sent, push

    def gather_rest(own, buf, send, recv, rep_recv, sent, push, between):
        def arrived(slot):
            remote(own, buf.at[rep, slot], send.at[0], recv.at[slot], partner).wait_recv()

        for step in range(1, n_inner):
            slot = inner_at(-step) * n_outer + outer
            arrived(slot)
            for across in range(1, n_outer):
                push(buf.at[rep, slot], slot, recv.at[slot], {"outer": outer_at(across)})
            push(buf.at[rep, slot], slot, rep_recv.at[slot], partner)
            between()
        for step in range(n_inner):
            for across in range(1, n_outer):
                slot = inner_at(-step) * n_outer + outer_at(-across)
                arrived(slot)
                push(buf.at[rep, slot], slot, rep_recv.at[slot], partner)
            between()
        for slot in range(n):
            remote(own, buf.at[1 - rep, slot], send.at[0], rep_recv.at[slot], partner).wait_recv()

    tok_sent, tok_push = gather_start(tokens_ref, rows, tok_send, tok_recv, tok_rep)

    loads[5].wait()
    loads[6].wait()
    gate_of = codes[...].astype(F32) * (1.0 / 65536.0)
    line = lax.broadcasted_iota(jnp.int32, (gates_own.shape[0], tok_rows), 0)
    table = jnp.zeros((gates_own.shape[0], tok_rows), F32)
    for expert in range(n):
        row = jnp.sum(jnp.where(ids[...] == expert, gate_of, 0.0), axis=0, keepdims=True)
        table = jnp.where(line == expert, row, table)
    gates_own[...] = jnp.zeros_like(gates_own)
    gates_own[:, :tok_rows] = table
    gate_sent = []
    for step in range(1, n):
        copy = remote(
            gates_own, gates.at[me], gate_send.at[step - 1], gate_recv.at[me], peer_at(step)[1]
        )
        copy.start()
        gate_sent.append(copy)
    gates[me] = gates_own[...]

    fan_root = [1.0 / math.sqrt(latent.shape[2])] * 2 + [1.0 / math.sqrt(2 * hid)]
    piece = 32

    def soften_rows(matrix, first, last):
        root = fan_root[matrix]

        def body(at, carry):
            part = pl.ds(pl.multiple_of(at * piece, piece), piece)
            value = latent[matrix, part, :]
            row_scale = jnp.mean(jnp.abs(value), axis=-1, keepdims=True) + 1e-06
            steep = value * (4.0 / row_scale)
            lower = jnp.tanh(steep - 2.0)
            upper = jnp.tanh(steep + 2.0)
            weight[matrix, part, :] = (row_scale * (0.5 * root) * (lower + upper)).astype(BF16)
            slope[matrix, part, :] = (2.0 * root) * (2.0 - lower * lower - upper * upper)
            return carry

        lax.fori_loop(first, last, body, 0)

    half = hid // piece // 2
    work = [(m, a, b) for m in range(3) for a, b in ((0, half), (half, hid // piece))]

    def soften_next():
        if work:
            matrix, first, last = work.pop(0)
            if first == 0:
                loads[matrix].wait()
            soften_rows(matrix, first, last)

    soften_next()
    gather_rest(
        tokens_ref, rows, tok_send, tok_recv, tok_rep, tok_sent, tok_push, soften_next
    )
    while work:
        soften_next()
    loads[3].wait()

    for step in range(1, n):
        slot = peer_at(-step)[0]
        remote(gates_own, gates.at[slot], gate_send.at[0], gate_recv.at[slot], partner).wait_recv()
    spread = LANES // tok_rows
    gate_row = jnp.concatenate(
        [
            sum(
                pltpu.roll(gates[base + at, pl.ds(me, 1), :], at * tok_rows, 1) if at
                else gates[base, pl.ds(me, 1), :]
                for at in range(spread)
            )
            for base in range(0, n, spread)
        ],
        axis=1,
    )

    def flat(ref, index):
        return ref[index].reshape(n * tok_rows, width)

    both = weight[0:2].reshape(2 * hid, 2 * width)
    pre = dot_t(both[:, :width], flat(rows, 0)) + dot_t(both[:, width:], flat(rows, 1))
    pre_gate, pre_up = pre[:hid], pre[hid:]
    sigmoid_gate = jax.nn.sigmoid(pre_gate)
    activated = pre_gate * sigmoid_gate
    hidden = activated * pre_up * gate_row
    grads[2] = hidden.astype(BF16)
    hidden_t = hidden.T.astype(BF16)

    other_cols = pl.ds(pl.multiple_of((1 - rep) * width, width), width)
    own_cols = pl.ds(pl.multiple_of(rep * width, width), width)
    half_out[...] = (
        jnp.dot(hidden_t, weight[2, :, other_cols], preferred_element_type=F32)
        .astype(BF16).reshape(n, tok_rows, width)
    )
    inner_order = [inner_at(step) for step in range(1, n_inner)] + [inner]
    half_sent = []

    def half_copy(slot):
        return remote(
            half_out.at[slot], half_in.at[slot], half_send.at[slot], half_recv.at[slot], partner
        )

    for across in range(1, n_outer + 1):
        for at in inner_order:
            copy = half_copy(at * n_outer + outer_at(across))
            copy.start()
            half_sent.append(copy)
    mine[...] = jnp.dot(
        hidden_t, weight[2, :, own_cols], preferred_element_type=F32
    ).reshape(n, tok_rows, width)

    sum_sent = []
    for across in range(1, n_outer):
        for at in inner_order:
            slot = at * n_outer + outer_at(across)
            half_copy(slot).wait_recv()
            sums[slot] = (mine[slot] + half_in[slot].astype(F32)).astype(BF16)
            landing = at * n_outer + outer
            copy = remote(
                sums.at[slot], crossed.at[landing], sum_send.at[slot], cross_recv.at[landing],
                {"outer": outer_at(across)},
            )
            copy.start()
            sum_sent.append(copy)

    mixed = None
    for at in inner_order:
        slot = at * n_outer + outer
        half_copy(slot).wait_recv()
        total = mine[slot] + half_in[slot].astype(F32)
        for across in range(1, n_outer):
            landing = at * n_outer + outer_at(-across)
            remote(
                sums.at[slot], crossed.at[landing], sum_send.at[0], cross_recv.at[landing], partner
            ).wait_recv()
            total = total + crossed[landing].astype(F32)
        if at is inner:
            mixed = total
        else:
            sums[slot] = total.astype(BF16)
            copy = remote(
                sums.at[slot], returned.at[inner], sum_send.at[slot], sum_recv.at[inner],
                {"inner": at},
            )
            copy.start()
            sum_sent.append(copy)

    factor[0] = gate_row * pre_up * sigmoid_gate * (1.0 + pre_gate * (1.0 - sigmoid_gate))
    factor[1] = gate_row * activated

    for step in range(1, n_inner):
        slot = inner_at(-step)
        remote(resid_own, returned.at[slot], sum_send.at[0], sum_recv.at[slot], partner).wait_recv()
        mixed = mixed + returned[slot].astype(F32)
    student[...] = mixed.astype(BF16)
    loads[4].wait()
    resid_own[...] = (mixed - teacher[...].astype(F32)).astype(BF16)
    resid[rep, me] = resid_own[...]

    res_sent, res_push = gather_start(resid_own, resid, res_send, res_recv, res_rep)
    gather_rest(
        resid_own, resid, res_send, res_recv, res_rep, res_sent, res_push, lambda: None
    )

    down = weight[2]
    hidden_grad = dot_t(down[:, :width], flat(resid, 0)) + dot_t(down[:, width:], flat(resid, 1))
    grads[0] = (hidden_grad * factor[0]).astype(BF16)
    grads[1] = (hidden_grad * factor[1]).astype(BF16)
    for copy in tok_sent + gate_sent + half_sent + sum_sent + res_sent:
        copy.wait_send()


def update_kernel(
    student, grads, rows, resid, latent, slope,
    student_ref, new_gu_ref, new_dn_ref, fresh, store_sem,
):
    n, tok_rows, width = rows.shape[1:]
    stores = [pltpu.make_async_copy(student, student_ref, store_sem.at[3])]
    stores[0].start()
    targets = [new_gu_ref.at[0, 0], new_gu_ref.at[0, 1], new_dn_ref.at[0]]
    tile = min(width, 256)
    for matrix in range(3):
        source = resid if matrix == 2 else rows
        for side in range(2):
            for first in range(0, width, tile):
                block = source[side, :, :, first : first + tile].reshape(n * tok_rows, tile)
                grad = jnp.dot(grads[matrix], block, preferred_element_type=F32)
                cols = slice(side * width + first, side * width + first + tile)
                fresh[matrix, :, cols] = latent[matrix, :, cols] - learn_rate * (
                    slope[matrix, :, cols] * grad
                )
        store = pltpu.make_async_copy(fresh.at[matrix], targets[matrix], store_sem.at[matrix])
        store.start()
        stores.append(store)
    for store in stores:
        store.wait()


def dense_step(tokens, teacher, expert_ids, gate_codes, gate_up_latent, down_latent):
    n_inner, n_outer = lax.axis_size("inner"), lax.axis_size("outer")
    n = n_inner * n_outer
    tok_rows, width = tokens.shape
    hid, full = down_latent.shape[1:]
    sublanes = -(-n // 8) * 8
    gather_sends = (n_inner - 1) * (1 + n_outer) + (n_outer - 1) * (1 + n_inner) + 1
    dma = pltpu.SemaphoreType.DMA
    block = (n, tok_rows, width)
    vmem = pl.BlockSpec(memory_space=pltpu.VMEM)
    hbm = pl.BlockSpec(memory_space=pltpu.HBM)
    inputs = (tokens, teacher, expert_ids.T, gate_codes.T, gate_up_latent, down_latent)
    state = pl.pallas_call(
        functools.partial(dense_kernel, n_inner, n_outer),
        out_shape=(
            jax.ShapeDtypeStruct(tokens.shape, BF16),
            jax.ShapeDtypeStruct((3, hid, n * tok_rows), BF16),
            jax.ShapeDtypeStruct((2, *block), BF16),
            jax.ShapeDtypeStruct((2, *block), BF16),
            jax.ShapeDtypeStruct((3, hid, full), F32),
            jax.ShapeDtypeStruct((3, hid, full), F32),
        ),
        in_specs=[hbm] * 6,
        out_specs=(vmem,) * 6,
        scratch_shapes=[
            pltpu.VMEM((tok_rows, width), BF16),
            pltpu.VMEM(expert_ids.shape[::-1], jnp.int32),
            pltpu.VMEM(expert_ids.shape[::-1], jnp.int32),
            pltpu.VMEM((tok_rows, width), BF16),
            pltpu.VMEM((sublanes, LANES), F32),
            pltpu.VMEM((n, sublanes, LANES), F32),
            pltpu.VMEM((3, hid, full), BF16),
            pltpu.VMEM((2, hid, n * tok_rows), F32),
            pltpu.VMEM(block, BF16),
            pltpu.VMEM(block, BF16),
            pltpu.VMEM(block, F32),
            pltpu.VMEM(block, BF16),
            pltpu.VMEM(block, BF16),
            pltpu.VMEM((n_inner, tok_rows, width), BF16),
            dma((7,)),
            dma((n,)),
            dma((n,)),
            dma((gather_sends,)),
            dma((n,)),
            dma((n,)),
            dma((n,)),
            dma((n,)),
            dma((n,)),
            dma((n,)),
            dma((n,)),
            dma((gather_sends,)),
            dma((n,)),
            dma((n,)),
        ],
        compiler_params=pltpu.CompilerParams(
            collective_id=0, has_side_effects=True, vmem_limit_bytes=24 * 1024 * 1024
        ),
    )(*[pltpu.with_memory_space_constraint(value, pltpu.HBM) for value in inputs])
    return pl.pallas_call(
        update_kernel,
        out_shape=(
            jax.ShapeDtypeStruct(tokens.shape, BF16),
            jax.ShapeDtypeStruct(gate_up_latent.shape, F32),
            jax.ShapeDtypeStruct(down_latent.shape, F32),
        ),
        in_specs=[vmem] * 6,
        out_specs=(hbm,) * 3,
        scratch_shapes=[pltpu.VMEM((3, hid, full), F32), dma((4,))],
        compiler_params=pltpu.CompilerParams(vmem_limit_bytes=24 * 1024 * 1024),
    )(*state)


def on_device(tokens, teacher, expert_ids, gate_codes, gate_up_latent, down_latent):
    experts = lax.axis_size("inner") * lax.axis_size("outer")
    tok_rows, top_count = expert_ids.shape
    whole_block = 2 * top_count >= experts
    fits = (
        lax.axis_size("rep") == 2
        and LANES % tok_rows == 0
        and tok_rows % 16 == 0
        and experts <= LANES
        and experts * tok_rows % LANES == 0
        and tokens.shape[1] % LANES == 0
        and down_latent.shape[1] % 64 == 0
    )
    step = dense_step if whole_block and fits else routed_step
    return step(tokens, teacher, expert_ids, gate_codes, gate_up_latent, down_latent)


def solution(mesh):
    return jax.shard_map(
        on_device,
        mesh=mesh,
        in_specs=(
            P(("parts", "inner", "outer"), "rep"),
            P(("parts", "inner", "outer"), "rep"),
            P(("parts", "inner", "outer"), None),
            P(("parts", "inner", "outer"), None),
            P(("inner", "outer"), None, "rep", None),
            P(("inner", "outer"), "rep", None),
        ),
        out_specs=(
            P(("parts", "inner", "outer"), "rep"),
            P(("parts", "inner", "outer"), None, "rep", None),
            P(("parts", "inner", "outer"), "rep", None),
        ),
        check_vma=False,
    )
```

```python
import functools
import math

import jax
import jax.numpy as jnp
from jax import lax
from jax.experimental import pallas as pl
from jax.experimental.pallas import tpu as pltpu
from jax.sharding import PartitionSpec as P

D = 1024
HID = 384


learn_rate = 1.0


def soften(latent, fan_in):
    row_scale = jnp.mean(jnp.abs(latent), axis=-1, keepdims=True) + 1e-06
    normed = latent / row_scale
    lower = jnp.tanh(4.0 * (normed - 0.5))
    upper = jnp.tanh(4.0 * (normed + 0.5))
    fan_root = 1.0 / math.sqrt(fan_in)
    weight = (row_scale * 0.5 * (lower + upper) * fan_root).astype(jnp.bfloat16)
    slope = 2.0 * (2.0 - lower * lower - upper * upper) * fan_root
    return (weight, slope)


def dispatch_rows(outbox):
    return lax.all_to_all(outbox, ("inner", "outer"), split_axis=0, concat_axis=0, tiled=True)


def combine_rows(outbox):
    return lax.all_to_all(outbox, ("inner", "outer"), split_axis=0, concat_axis=0, tiled=True)


def upstream_rows(outbox):
    return lax.all_to_all(outbox, ("inner", "outer"), split_axis=0, concat_axis=0, tiled=True)


def routed_step(tokens, teacher, expert_ids, gate_codes, gate_up_latent, down_latent):
    experts = lax.axis_size("inner") * lax.axis_size("outer")
    tok_rows, top_count = expert_ids.shape
    part_width = tokens.shape[1]
    capacity = min(tok_rows, 2 * tok_rows * top_count // experts)
    flat_ids = expert_ids.reshape(-1)
    one_hot = (flat_ids[:, None] == jnp.arange(experts, dtype=jnp.int32)[None, :]).astype(jnp.int32)
    before = jnp.cumsum(one_hot, axis=0) - one_hot
    route_slot = jnp.sum(before * one_hot, axis=1)
    target = flat_ids * capacity + route_slot
    payload = jnp.repeat(tokens, top_count, axis=0)
    outbox = jnp.zeros((experts * capacity, part_width), jnp.bfloat16).at[target].set(payload)
    received = dispatch_rows(outbox)
    expert_rows = lax.all_gather(received, "rep", axis=1, tiled=True)
    gu_weight, gu_slope = soften(gate_up_latent[0], D)
    dn_weight, dn_slope = soften(down_latent[0], HID)
    projected = lax.dot_general(
        gu_weight, expert_rows, (((2,), (1,)), ((), ())), preferred_element_type=jnp.float32
    )
    pre_gate = projected[0]
    pre_up = projected[1]
    sigmoid_gate = jax.nn.sigmoid(pre_gate)
    activated = pre_gate * sigmoid_gate
    hidden = (activated * pre_up).astype(jnp.bfloat16)
    partial_out = lax.dot_general(
        hidden, dn_weight, (((0,), (0,)), ((), ())), preferred_element_type=jnp.float32
    )
    expert_out = lax.psum_scatter(
        partial_out.astype(jnp.bfloat16), "rep", scatter_dimension=1, tiled=True
    )
    returned = combine_rows(expert_out)
    picked = returned[target].reshape(tok_rows, top_count, part_width)
    gating = gate_codes.astype(jnp.float32) / 65536.0
    mixed = jnp.sum(gating[:, :, None] * picked.astype(jnp.float32), axis=1)
    student_out = mixed.astype(jnp.bfloat16)
    residual = mixed - teacher.astype(jnp.float32)
    pair_grad = (
        (gating[:, :, None] * residual[:, None, :]).astype(jnp.bfloat16).reshape(-1, part_width)
    )
    grad_outbox = (
        jnp.zeros((experts * capacity, part_width), jnp.bfloat16).at[target].set(pair_grad)
    )
    grad_part = upstream_rows(grad_outbox)
    out_grad = lax.all_gather(grad_part, "rep", axis=1, tiled=True)
    down_grad = jnp.dot(hidden, out_grad, preferred_element_type=jnp.float32)
    hidden_grad = lax.dot_general(
        dn_weight, out_grad, (((1,), (1,)), ((), ())), preferred_element_type=jnp.float32
    )
    gate_grad = (
        hidden_grad * pre_up * sigmoid_gate * (1.0 + pre_gate * (1.0 - sigmoid_gate))
    ).astype(jnp.bfloat16)
    up_grad = (hidden_grad * activated).astype(jnp.bfloat16)
    weight_grads = lax.dot_general(
        jnp.stack([gate_grad, up_grad]),
        expert_rows,
        (((2,), (0,)), ((), ())),
        preferred_element_type=jnp.float32,
    )
    new_gate_up = gate_up_latent - learn_rate * (gu_slope * weight_grads)[None]
    new_down = down_latent - learn_rate * (dn_slope * down_grad)[None]
    return (student_out, new_gate_up, new_down)


MESH = pl.DeviceIdType.MESH
LANES = 128
BF16 = jnp.bfloat16
F32 = jnp.float32


def dot_t(a, b):
    return lax.dot_general(a, b, (((1,), (1,)), ((), ())), preferred_element_type=F32)


def dense_kernel(
    n_inner, n_outer,
    tokens_ref, teacher_ref, ids_ref, codes_ref, gu_ref, dn_ref,
    student, grads, rows, resid, latent, slope,
    teacher, ids, codes, resid_own, gates_own, gates, weight,
    scales, factor, dn_cols, hidden_t, sums, returned,
    load_sem, gate_send, gate_recv, tok_send, tok_recv, tok_rep,
    pair_send, pair_recv, sum_send, sum_recv, res_send, res_recv, res_rep,
):
    n = n_inner * n_outer
    tok_rows, width = tokens_ref.shape
    hid = latent.shape[1]
    inner, outer, rep = lax.axis_index("inner"), lax.axis_index("outer"), lax.axis_index("rep")
    me = inner * n_outer + outer
    partner = {"rep": 1 - rep}

    def inner_at(step):
        return lax.rem(inner + step + n_inner, n_inner)

    def outer_at(step):
        return lax.rem(outer + step + n_outer, n_outer)

    def peer_at(step):
        peer = lax.rem(me + step + n, n)
        return peer, {"inner": peer // n_outer, "outer": lax.rem(peer, n_outer)}

    def remote(source, target, send, recv, device):
        return pltpu.make_async_remote_copy(
            src_ref=source, dst_ref=target, send_sem=send, recv_sem=recv,
            device_id=device, device_id_type=MESH,
        )

    other_cols = pl.ds(pl.multiple_of((1 - rep) * width, width), width)
    own_cols = pl.ds(pl.multiple_of(rep * width, width), width)
    loads = [
        pltpu.make_async_copy(gu_ref.at[0, 0], latent.at[0], load_sem.at[0]),
        pltpu.make_async_copy(gu_ref.at[0, 1], latent.at[1], load_sem.at[1]),
        pltpu.make_async_copy(dn_ref.at[0], latent.at[2], load_sem.at[2]),
        pltpu.make_async_copy(tokens_ref, rows.at[rep, me], load_sem.at[3]),
        pltpu.make_async_copy(teacher_ref, teacher, load_sem.at[4]),
        pltpu.make_async_copy(ids_ref, ids, load_sem.at[5]),
        pltpu.make_async_copy(codes_ref, codes, load_sem.at[6]),
    ]
    for load in loads:
        load.start()

    barrier = pltpu.get_barrier_semaphore()
    pl.semaphore_signal(barrier, inc=1, device_id=partner, device_id_type=MESH)
    for step in range(1, n):
        pl.semaphore_signal(barrier, inc=1, device_id=peer_at(step)[1], device_id_type=MESH)
    pl.semaphore_wait(barrier, n)

    def gather_start(own, buf, send, recv, rep_recv):
        sent = []

        def push(source, slot, sem, device):
            copy = remote(source, buf.at[rep, slot], send.at[len(sent)], sem, device)
            copy.start()
            sent.append(copy)

        for step in range(1, n_inner):
            push(own, me, recv.at[me], {"inner": inner_at(step)})
        for step in range(1, n_outer):
            push(own, me, recv.at[me], {"outer": outer_at(step)})
        push(own, me, rep_recv.at[me], partner)
        return sent, push

    def gather_rest(own, buf, send, recv, rep_recv, sent, push, between):
        def arrived(slot):
            remote(own, buf.at[rep, slot], send.at[0], recv.at[slot], partner).wait_recv()

        for step in range(1, n_inner):
            slot = inner_at(-step) * n_outer + outer
            arrived(slot)
            for across in range(1, n_outer):
                push(buf.at[rep, slot], slot, recv.at[slot], {"outer": outer_at(across)})
            push(buf.at[rep, slot], slot, rep_recv.at[slot], partner)
            between()
        for step in range(n_inner):
            for across in range(1, n_outer):
                slot = inner_at(-step) * n_outer + outer_at(-across)
                arrived(slot)
                push(buf.at[rep, slot], slot, rep_recv.at[slot], partner)
            between()
    def gather_end(own, buf, send, rep_recv):
        for slot in range(n):
            remote(own, buf.at[1 - rep, slot], send.at[0], rep_recv.at[slot], partner).wait_recv()

    tok_sent, tok_push = gather_start(tokens_ref, rows, tok_send, tok_recv, tok_rep)

    loads[5].wait()
    loads[6].wait()
    gate_of = codes[...].astype(F32) * (1.0 / 65536.0)
    line = lax.broadcasted_iota(jnp.int32, (gates_own.shape[0], tok_rows), 0)
    table = jnp.zeros((gates_own.shape[0], tok_rows), F32)
    for expert in range(n):
        row = jnp.sum(jnp.where(ids[...] == expert, gate_of, 0.0), axis=0, keepdims=True)
        table = jnp.where(line == expert, row, table)
    gates_own[...] = jnp.zeros_like(gates_own)
    gates_own[:, :tok_rows] = table
    gate_sent = []
    for step in range(1, n):
        copy = remote(
            gates_own, gates.at[me], gate_send.at[step - 1], gate_recv.at[me], peer_at(step)[1]
        )
        copy.start()
        gate_sent.append(copy)
    gates[me] = gates_own[...]

    fan_root = [1.0 / math.sqrt(latent.shape[2])] * 2 + [1.0 / math.sqrt(2 * hid)]
    piece = 32
    lanes_of = [slice(at, at + LANES) for at in range(0, latent.shape[2], LANES)]

    def scale_rows(matrix):
        total = jnp.abs(latent[matrix, :, lanes_of[0]])
        for lanes in lanes_of[1:]:
            total = total + jnp.abs(latent[matrix, :, lanes])
        row_sum = jnp.sum(total, axis=-1, keepdims=True)
        row_scale = row_sum * (1.0 / latent.shape[2]) + 1e-06
        scales[0, matrix] = jnp.broadcast_to(4.0 / row_scale, (hid, LANES))
        scales[1, matrix] = jnp.broadcast_to(row_scale * (0.5 * fan_root[matrix]), (hid, LANES))

    def soften_rows(matrix, first, last):
        root = fan_root[matrix]

        def body(at, carry):
            part = pl.ds(pl.multiple_of(at * piece, piece), piece)
            steepness, size = scales[0, matrix, part, :], scales[1, matrix, part, :]
            for lanes in lanes_of:
                steep = latent[matrix, part, lanes] * steepness
                lower = jnp.tanh(steep - 2.0)
                upper = jnp.tanh(steep + 2.0)
                weight[matrix, part, lanes] = (size * (lower + upper)).astype(BF16)
                slope[matrix, part, lanes] = (2.0 * root) * (2.0 - lower * lower - upper * upper)
            return carry

        lax.fori_loop(first, last, body, 0)

    half = hid // piece // 2
    work = [(m, a, b) for m in range(3) for a, b in ((0, half), (half, hid // piece))]

    def own_half_dot(matrix, buf):
        return dot_t(matrix, buf[rep].reshape(n * tok_rows, width))

    def other_half_dot(matrix, buf):
        return dot_t(matrix, buf[1 - rep].reshape(n * tok_rows, width))

    def soften_next():
        if work:
            matrix, first, last = work.pop(0)
            if first == 0:
                loads[matrix].wait()
                scale_rows(matrix)
            soften_rows(matrix, first, last)

    soften_next()
    gather_rest(
        tokens_ref, rows, tok_send, tok_recv, tok_rep, tok_sent, tok_push, soften_next
    )
    while work:
        soften_next()
    dn_copy = remote(
        weight.at[2, :, other_cols], dn_cols.at[rep], pair_send.at[0], pair_recv.at[0], partner
    )
    dn_copy.start()
    dn_cols[rep] = weight[2, :, own_cols]
    loads[3].wait()
    pre = own_half_dot(weight[0:2, :, own_cols].reshape(2 * hid, width), rows)
    gather_end(tokens_ref, rows, tok_send, tok_rep)
    pre = pre + other_half_dot(weight[0:2, :, other_cols].reshape(2 * hid, width), rows)

    for step in range(1, n):
        slot = peer_at(-step)[0]
        remote(gates_own, gates.at[slot], gate_send.at[0], gate_recv.at[slot], partner).wait_recv()
    spread = LANES // tok_rows
    gate_row = jnp.concatenate(
        [
            sum(
                pltpu.roll(gates[base + at, pl.ds(me, 1), :], at * tok_rows, 1) if at
                else gates[base, pl.ds(me, 1), :]
                for at in range(spread)
            )
            for base in range(0, n, spread)
        ],
        axis=1,
    )

    pre_gate, pre_up = pre[:hid], pre[hid:]
    sigmoid_gate = jax.nn.sigmoid(pre_gate)
    activated = pre_gate * sigmoid_gate
    hidden = activated * pre_up * gate_row
    grads[2] = hidden.astype(BF16)
    hidden_t[rep] = hidden.T.astype(BF16)
    hidden_copy = remote(
        hidden_t.at[rep], hidden_t.at[rep], pair_send.at[1], pair_recv.at[1], partner
    )
    hidden_copy.start()
    total = jnp.dot(hidden_t[rep], dn_cols[rep], preferred_element_type=F32)
    dn_copy.wait_recv()
    hidden_copy.wait_recv()
    total = total + jnp.dot(hidden_t[1 - rep], dn_cols[1 - rep], preferred_element_type=F32)
    sums[...] = total.astype(BF16).reshape(n, tok_rows, width)

    sum_sent = []
    for step in range(1, n):
        slot, device = peer_at(step)
        copy = remote(
            sums.at[slot], returned.at[me], sum_send.at[step], sum_recv.at[me], device
        )
        copy.start()
        sum_sent.append(copy)

    factor[0] = gate_row * pre_up * sigmoid_gate * (1.0 + pre_gate * (1.0 - sigmoid_gate))
    factor[1] = gate_row * activated

    mixed = sums[me].astype(F32)
    for step in range(1, n):
        slot = peer_at(-step)[0]
        remote(resid_own, returned.at[slot], sum_send.at[0], sum_recv.at[slot], partner).wait_recv()
        mixed = mixed + returned[slot].astype(F32)
    student[...] = mixed.astype(BF16)
    loads[4].wait()
    resid_own[...] = (mixed - teacher[...].astype(F32)).astype(BF16)
    resid[rep, me] = resid_own[...]

    res_sent, res_push = gather_start(resid_own, resid, res_send, res_recv, res_rep)
    gather_rest(
        resid_own, resid, res_send, res_recv, res_rep, res_sent, res_push, lambda: None
    )

    hidden_grad = own_half_dot(weight[2, :, own_cols], resid)
    gather_end(resid_own, resid, res_send, res_rep)
    hidden_grad = hidden_grad + other_half_dot(weight[2, :, other_cols], resid)
    grads[0] = (hidden_grad * factor[0]).astype(BF16)
    grads[1] = (hidden_grad * factor[1]).astype(BF16)
    for copy in tok_sent + gate_sent + [dn_copy, hidden_copy] + sum_sent + res_sent:
        copy.wait_send()


def update_kernel(
    student, grads, rows, resid, latent, slope,
    student_ref, new_gu_ref, new_dn_ref, fresh, store_sem,
):
    n, tok_rows, width = rows.shape[1:]
    stores = [pltpu.make_async_copy(student, student_ref, store_sem.at[3])]
    stores[0].start()
    targets = [new_gu_ref.at[0, 0], new_gu_ref.at[0, 1], new_dn_ref.at[0]]
    tile = min(width, 256)
    for matrix in range(3):
        source = resid if matrix == 2 else rows
        for side in range(2):
            for first in range(0, width, tile):
                block = source[side, :, :, first : first + tile].reshape(n * tok_rows, tile)
                grad = jnp.dot(grads[matrix], block, preferred_element_type=F32)
                cols = slice(side * width + first, side * width + first + tile)
                fresh[matrix, :, cols] = latent[matrix, :, cols] - learn_rate * (
                    slope[matrix, :, cols] * grad
                )
        store = pltpu.make_async_copy(fresh.at[matrix], targets[matrix], store_sem.at[matrix])
        store.start()
        stores.append(store)
    for store in stores:
        store.wait()


def dense_step(tokens, teacher, expert_ids, gate_codes, gate_up_latent, down_latent):
    n_inner, n_outer = lax.axis_size("inner"), lax.axis_size("outer")
    n = n_inner * n_outer
    tok_rows, width = tokens.shape
    hid, full = down_latent.shape[1:]
    sublanes = -(-n // 8) * 8
    gather_sends = (n_inner - 1) * (1 + n_outer) + (n_outer - 1) * (1 + n_inner) + 1
    dma = pltpu.SemaphoreType.DMA
    block = (n, tok_rows, width)
    vmem = pl.BlockSpec(memory_space=pltpu.VMEM)
    hbm = pl.BlockSpec(memory_space=pltpu.HBM)
    inputs = (tokens, teacher, expert_ids.T, gate_codes.T, gate_up_latent, down_latent)
    state = pl.pallas_call(
        functools.partial(dense_kernel, n_inner, n_outer),
        out_shape=(
            jax.ShapeDtypeStruct(tokens.shape, BF16),
            jax.ShapeDtypeStruct((3, hid, n * tok_rows), BF16),
            jax.ShapeDtypeStruct((2, *block), BF16),
            jax.ShapeDtypeStruct((2, *block), BF16),
            jax.ShapeDtypeStruct((3, hid, full), F32),
            jax.ShapeDtypeStruct((3, hid, full), F32),
        ),
        in_specs=[hbm] * 6,
        out_specs=(vmem,) * 6,
        scratch_shapes=[
            pltpu.VMEM((tok_rows, width), BF16),
            pltpu.VMEM(expert_ids.shape[::-1], jnp.int32),
            pltpu.VMEM(expert_ids.shape[::-1], jnp.int32),
            pltpu.VMEM((tok_rows, width), BF16),
            pltpu.VMEM((sublanes, LANES), F32),
            pltpu.VMEM((n, sublanes, LANES), F32),
            pltpu.VMEM((3, hid, full), BF16),
            pltpu.VMEM((2, 3, hid, LANES), F32),
            pltpu.VMEM((2, hid, n * tok_rows), F32),
            pltpu.VMEM((2, hid, width), BF16),
            pltpu.VMEM((2, n * tok_rows, hid), BF16),
            pltpu.VMEM(block, BF16),
            pltpu.VMEM(block, BF16),
            dma((7,)),
            dma((n,)),
            dma((n,)),
            dma((gather_sends,)),
            dma((n,)),
            dma((n,)),
            dma((2,)),
            dma((2,)),
            dma((n,)),
            dma((n,)),
            dma((gather_sends,)),
            dma((n,)),
            dma((n,)),
        ],
        compiler_params=pltpu.CompilerParams(
            collective_id=0, has_side_effects=True, vmem_limit_bytes=24 * 1024 * 1024
        ),
    )(*[pltpu.with_memory_space_constraint(value, pltpu.HBM) for value in inputs])
    return pl.pallas_call(
        update_kernel,
        out_shape=(
            jax.ShapeDtypeStruct(tokens.shape, BF16),
            jax.ShapeDtypeStruct(gate_up_latent.shape, F32),
            jax.ShapeDtypeStruct(down_latent.shape, F32),
        ),
        in_specs=[vmem] * 6,
        out_specs=(hbm,) * 3,
        scratch_shapes=[pltpu.VMEM((3, hid, full), F32), dma((4,))],
        compiler_params=pltpu.CompilerParams(vmem_limit_bytes=24 * 1024 * 1024),
    )(*state)


def on_device(tokens, teacher, expert_ids, gate_codes, gate_up_latent, down_latent):
    experts = lax.axis_size("inner") * lax.axis_size("outer")
    tok_rows, top_count = expert_ids.shape
    whole_block = 2 * top_count >= experts
    fits = (
        lax.axis_size("rep") == 2
        and LANES % tok_rows == 0
        and tok_rows % 16 == 0
        and experts <= LANES
        and experts * tok_rows % LANES == 0
        and tokens.shape[1] % LANES == 0
        and down_latent.shape[1] % 64 == 0
    )
    step = dense_step if whole_block and fits else routed_step
    return step(tokens, teacher, expert_ids, gate_codes, gate_up_latent, down_latent)


def solution(mesh):
    return jax.shard_map(
        on_device,
        mesh=mesh,
        in_specs=(
            P(("parts", "inner", "outer"), "rep"),
            P(("parts", "inner", "outer"), "rep"),
            P(("parts", "inner", "outer"), None),
            P(("parts", "inner", "outer"), None),
            P(("inner", "outer"), None, "rep", None),
            P(("inner", "outer"), "rep", None),
        ),
        out_specs=(
            P(("parts", "inner", "outer"), "rep"),
            P(("parts", "inner", "outer"), None, "rep", None),
            P(("parts", "inner", "outer"), "rep", None),
        ),
        check_vma=False,
    )
```

```python
import functools
import math

import jax
import jax.numpy as jnp
from jax import lax
from jax.experimental import pallas as pl
from jax.experimental.pallas import tpu as pltpu
from jax.sharding import PartitionSpec as P

D = 1024
HID = 384


learn_rate = 1.0


def soften(latent, fan_in):
    row_scale = jnp.mean(jnp.abs(latent), axis=-1, keepdims=True) + 1e-06
    normed = latent / row_scale
    lower = jnp.tanh(4.0 * (normed - 0.5))
    upper = jnp.tanh(4.0 * (normed + 0.5))
    fan_root = 1.0 / math.sqrt(fan_in)
    weight = (row_scale * 0.5 * (lower + upper) * fan_root).astype(jnp.bfloat16)
    slope = 2.0 * (2.0 - lower * lower - upper * upper) * fan_root
    return (weight, slope)


def dispatch_rows(outbox):
    return lax.all_to_all(outbox, ("inner", "outer"), split_axis=0, concat_axis=0, tiled=True)


def combine_rows(outbox):
    return lax.all_to_all(outbox, ("inner", "outer"), split_axis=0, concat_axis=0, tiled=True)


def upstream_rows(outbox):
    return lax.all_to_all(outbox, ("inner", "outer"), split_axis=0, concat_axis=0, tiled=True)


def routed_step(tokens, teacher, expert_ids, gate_codes, gate_up_latent, down_latent):
    experts = lax.axis_size("inner") * lax.axis_size("outer")
    tok_rows, top_count = expert_ids.shape
    part_width = tokens.shape[1]
    capacity = min(tok_rows, 2 * tok_rows * top_count // experts)
    flat_ids = expert_ids.reshape(-1)
    one_hot = (flat_ids[:, None] == jnp.arange(experts, dtype=jnp.int32)[None, :]).astype(jnp.int32)
    before = jnp.cumsum(one_hot, axis=0) - one_hot
    route_slot = jnp.sum(before * one_hot, axis=1)
    target = flat_ids * capacity + route_slot
    payload = jnp.repeat(tokens, top_count, axis=0)
    outbox = jnp.zeros((experts * capacity, part_width), jnp.bfloat16).at[target].set(payload)
    received = dispatch_rows(outbox)
    expert_rows = lax.all_gather(received, "rep", axis=1, tiled=True)
    gu_weight, gu_slope = soften(gate_up_latent[0], D)
    dn_weight, dn_slope = soften(down_latent[0], HID)
    projected = lax.dot_general(
        gu_weight, expert_rows, (((2,), (1,)), ((), ())), preferred_element_type=jnp.float32
    )
    pre_gate = projected[0]
    pre_up = projected[1]
    sigmoid_gate = jax.nn.sigmoid(pre_gate)
    activated = pre_gate * sigmoid_gate
    hidden = (activated * pre_up).astype(jnp.bfloat16)
    partial_out = lax.dot_general(
        hidden, dn_weight, (((0,), (0,)), ((), ())), preferred_element_type=jnp.float32
    )
    expert_out = lax.psum_scatter(
        partial_out.astype(jnp.bfloat16), "rep", scatter_dimension=1, tiled=True
    )
    returned = combine_rows(expert_out)
    picked = returned[target].reshape(tok_rows, top_count, part_width)
    gating = gate_codes.astype(jnp.float32) / 65536.0
    mixed = jnp.sum(gating[:, :, None] * picked.astype(jnp.float32), axis=1)
    student_out = mixed.astype(jnp.bfloat16)
    residual = mixed - teacher.astype(jnp.float32)
    pair_grad = (
        (gating[:, :, None] * residual[:, None, :]).astype(jnp.bfloat16).reshape(-1, part_width)
    )
    grad_outbox = (
        jnp.zeros((experts * capacity, part_width), jnp.bfloat16).at[target].set(pair_grad)
    )
    grad_part = upstream_rows(grad_outbox)
    out_grad = lax.all_gather(grad_part, "rep", axis=1, tiled=True)
    down_grad = jnp.dot(hidden, out_grad, preferred_element_type=jnp.float32)
    hidden_grad = lax.dot_general(
        dn_weight, out_grad, (((1,), (1,)), ((), ())), preferred_element_type=jnp.float32
    )
    gate_grad = (
        hidden_grad * pre_up * sigmoid_gate * (1.0 + pre_gate * (1.0 - sigmoid_gate))
    ).astype(jnp.bfloat16)
    up_grad = (hidden_grad * activated).astype(jnp.bfloat16)
    weight_grads = lax.dot_general(
        jnp.stack([gate_grad, up_grad]),
        expert_rows,
        (((2,), (0,)), ((), ())),
        preferred_element_type=jnp.float32,
    )
    new_gate_up = gate_up_latent - learn_rate * (gu_slope * weight_grads)[None]
    new_down = down_latent - learn_rate * (dn_slope * down_grad)[None]
    return (student_out, new_gate_up, new_down)


MESH = pl.DeviceIdType.MESH
LANES = 128
BF16 = jnp.bfloat16
F32 = jnp.float32


def dot_t(a, b):
    return lax.dot_general(a, b, (((1,), (1,)), ((), ())), preferred_element_type=F32)


def dense_kernel(
    n_inner, n_outer,
    tokens_ref, teacher_ref, ids_ref, codes_ref, gu_ref, dn_ref,
    student, grads, rows, resid, latent, slope,
    teacher, ids, codes, resid_own, gates_own, gates, weight,
    factor, half_out, half_in, mine, sums, returned,
    load_sem, gate_send, gate_recv, tok_send, tok_recv, tok_rep,
    half_send, half_recv, sum_send, sum_recv, res_send, res_recv, res_rep,
):
    n = n_inner * n_outer
    tok_rows, width = tokens_ref.shape
    hid = latent.shape[1]
    inner, outer, rep = lax.axis_index("inner"), lax.axis_index("outer"), lax.axis_index("rep")
    me = inner * n_outer + outer
    partner = {"rep": 1 - rep}

    def inner_at(step):
        return lax.rem(inner + step + n_inner, n_inner)

    def outer_at(step):
        return lax.rem(outer + step + n_outer, n_outer)

    def peer_at(step):
        peer = lax.rem(me + step + n, n)
        return peer, {"inner": peer // n_outer, "outer": lax.rem(peer, n_outer)}

    def remote(source, target, send, recv, device):
        return pltpu.make_async_remote_copy(
            src_ref=source, dst_ref=target, send_sem=send, recv_sem=recv,
            device_id=device, device_id_type=MESH,
        )

    loads = [
        pltpu.make_async_copy(gu_ref.at[0, 0], latent.at[0], load_sem.at[0]),
        pltpu.make_async_copy(gu_ref.at[0, 1], latent.at[1], load_sem.at[1]),
        pltpu.make_async_copy(dn_ref.at[0], latent.at[2], load_sem.at[2]),
        pltpu.make_async_copy(tokens_ref, rows.at[rep, me], load_sem.at[3]),
        pltpu.make_async_copy(teacher_ref, teacher, load_sem.at[4]),
        pltpu.make_async_copy(ids_ref, ids, load_sem.at[5]),
        pltpu.make_async_copy(codes_ref, codes, load_sem.at[6]),
    ]
    for load in loads:
        load.start()

    barrier = pltpu.get_barrier_semaphore()
    pl.semaphore_signal(barrier, inc=1, device_id=partner, device_id_type=MESH)
    for step in range(1, n):
        pl.semaphore_signal(barrier, inc=1, device_id=peer_at(step)[1], device_id_type=MESH)
    pl.semaphore_wait(barrier, n)

    def gather_start(own, buf, send, recv, rep_recv):
        sent = []

        def push(source, slot, sem, device):
            copy = remote(source, buf.at[rep, slot], send.at[len(sent)], sem, device)
            copy.start()
            sent.append(copy)

        for step in range(1, n):
            push(own, me, recv.at[me], peer_at(step)[1])
        push(own, me, rep_recv.at[me], partner)
        return sent, push

    def gather_rest(own, buf, send, recv, rep_recv, sent, push, between):
        def arrived(slot):
            remote(own, buf.at[rep, slot], send.at[0], recv.at[slot], partner).wait_recv()

        for step in range(1, n):
            slot = peer_at(-step)[0]
            arrived(slot)
            push(buf.at[rep, slot], slot, rep_recv.at[slot], partner)
            between()
        for slot in range(n):
            remote(own, buf.at[1 - rep, slot], send.at[0], rep_recv.at[slot], partner).wait_recv()

    tok_sent, tok_push = gather_start(tokens_ref, rows, tok_send, tok_recv, tok_rep)

    loads[5].wait()
    loads[6].wait()
    gate_of = codes[...].astype(F32) * (1.0 / 65536.0)
    line = lax.broadcasted_iota(jnp.int32, (gates_own.shape[0], tok_rows), 0)
    table = jnp.zeros((gates_own.shape[0], tok_rows), F32)
    for expert in range(n):
        row = jnp.sum(jnp.where(ids[...] == expert, gate_of, 0.0), axis=0, keepdims=True)
        table = jnp.where(line == expert, row, table)
    gates_own[...] = jnp.zeros_like(gates_own)
    gates_own[:, :tok_rows] = table
    gate_sent = []
    for step in range(1, n):
        copy = remote(
            gates_own, gates.at[me], gate_send.at[step - 1], gate_recv.at[me], peer_at(step)[1]
        )
        copy.start()
        gate_sent.append(copy)
    gates[me] = gates_own[...]

    fan_root = [1.0 / math.sqrt(latent.shape[2])] * 2 + [1.0 / math.sqrt(2 * hid)]
    piece = 32

    def soften_rows(matrix, first, last):
        root = fan_root[matrix]

        def body(at, carry):
            part = pl.ds(pl.multiple_of(at * piece, piece), piece)
            value = latent[matrix, part, :]
            row_scale = jnp.mean(jnp.abs(value), axis=-1, keepdims=True) + 1e-06
            normed = value / row_scale
            lower = jnp.tanh(4.0 * (normed - 0.5))
            upper = jnp.tanh(4.0 * (normed + 0.5))
            weight[matrix, part, :] = (row_scale * (0.5 * root) * (lower + upper)).astype(BF16)
            slope[matrix, part, :] = (2.0 * root) * (2.0 - lower * lower - upper * upper)
            return carry

        lax.fori_loop(first, last, body, 0)

    half = hid // piece // 2
    work = [(m, a, b) for m in range(3) for a, b in ((0, half), (half, hid // piece))]

    def soften_next():
        if work:
            matrix, first, last = work.pop(0)
            if first == 0:
                loads[matrix].wait()
            soften_rows(matrix, first, last)

    soften_next()
    gather_rest(
        tokens_ref, rows, tok_send, tok_recv, tok_rep, tok_sent, tok_push, soften_next
    )
    while work:
        soften_next()
    loads[3].wait()

    for step in range(1, n):
        slot = peer_at(-step)[0]
        remote(gates_own, gates.at[slot], gate_send.at[0], gate_recv.at[slot], partner).wait_recv()
    spread = LANES // tok_rows
    gate_row = jnp.concatenate(
        [
            sum(
                pltpu.roll(gates[base + at, pl.ds(me, 1), :], at * tok_rows, 1) if at
                else gates[base, pl.ds(me, 1), :]
                for at in range(spread)
            )
            for base in range(0, n, spread)
        ],
        axis=1,
    )

    def flat(ref, index):
        return ref[index].reshape(n * tok_rows, width)

    both = weight[0:2].reshape(2 * hid, 2 * width)
    pre = dot_t(both[:, :width], flat(rows, 0)) + dot_t(both[:, width:], flat(rows, 1))
    pre_gate, pre_up = pre[:hid], pre[hid:]
    sigmoid_gate = jax.nn.sigmoid(pre_gate)
    activated = pre_gate * sigmoid_gate
    hidden = activated * pre_up * gate_row
    grads[2] = hidden.astype(BF16)
    hidden_t = hidden.T.astype(BF16)

    other_cols = pl.ds(pl.multiple_of((1 - rep) * width, width), width)
    own_cols = pl.ds(pl.multiple_of(rep * width, width), width)
    half_out[...] = (
        jnp.dot(hidden_t, weight[2, :, other_cols], preferred_element_type=F32)
        .astype(BF16).reshape(n, tok_rows, width)
    )
    order = [peer_at(step) for step in range(1, n)] + [(me, None)]
    half_sent = []
    for slot, _ in order:
        copy = remote(half_out.at[slot], half_in.at[slot], half_send.at[slot], half_recv.at[slot], partner)
        copy.start()
        half_sent.append(copy)
    mine[...] = jnp.dot(
        hidden_t, weight[2, :, own_cols], preferred_element_type=F32
    ).reshape(n, tok_rows, width)

    sum_sent = []
    for at, (slot, device) in enumerate(order):
        half_sent[at].wait_recv()
        total = mine[slot] + half_in[slot].astype(F32)
        if device is None:
            mine[slot] = total
        else:
            sums[slot] = total.astype(BF16)
            copy = remote(
                sums.at[slot], returned.at[me], sum_send.at[at], sum_recv.at[me], device
            )
            copy.start()
            sum_sent.append(copy)

    factor[0] = gate_row * pre_up * sigmoid_gate * (1.0 + pre_gate * (1.0 - sigmoid_gate))
    factor[1] = gate_row * activated

    mixed = mine[me]
    for step in range(1, n):
        slot = peer_at(-step)[0]
        remote(resid_own, returned.at[slot], sum_send.at[0], sum_recv.at[slot], partner).wait_recv()
        mixed = mixed + returned[slot].astype(F32)
    student[...] = mixed.astype(BF16)
    loads[4].wait()
    resid_own[...] = (mixed - teacher[...].astype(F32)).astype(BF16)
    resid[rep, me] = resid_own[...]

    res_sent, res_push = gather_start(resid_own, resid, res_send, res_recv, res_rep)
    gather_rest(
        resid_own, resid, res_send, res_recv, res_rep, res_sent, res_push, lambda: None
    )

    down = weight[2]
    hidden_grad = dot_t(down[:, :width], flat(resid, 0)) + dot_t(down[:, width:], flat(resid, 1))
    grads[0] = (hidden_grad * factor[0]).astype(BF16)
    grads[1] = (hidden_grad * factor[1]).astype(BF16)
    for copy in tok_sent + gate_sent + half_sent + sum_sent + res_sent:
        copy.wait_send()


def update_kernel(
    student, grads, rows, resid, latent, slope,
    student_ref, new_gu_ref, new_dn_ref, fresh, store_sem,
):
    n, tok_rows, width = rows.shape[1:]
    stores = [pltpu.make_async_copy(student, student_ref, store_sem.at[3])]
    stores[0].start()
    targets = [new_gu_ref.at[0, 0], new_gu_ref.at[0, 1], new_dn_ref.at[0]]
    tile = min(width, 256)
    for matrix in range(3):
        source = resid if matrix == 2 else rows
        for side in range(2):
            for first in range(0, width, tile):
                block = source[side, :, :, first : first + tile].reshape(n * tok_rows, tile)
                grad = jnp.dot(grads[matrix], block, preferred_element_type=F32)
                cols = slice(side * width + first, side * width + first + tile)
                fresh[matrix, :, cols] = latent[matrix, :, cols] - learn_rate * (
                    slope[matrix, :, cols] * grad
                )
        store = pltpu.make_async_copy(fresh.at[matrix], targets[matrix], store_sem.at[matrix])
        store.start()
        stores.append(store)
    for store in stores:
        store.wait()


def dense_step(tokens, teacher, expert_ids, gate_codes, gate_up_latent, down_latent):
    n_inner, n_outer = lax.axis_size("inner"), lax.axis_size("outer")
    n = n_inner * n_outer
    tok_rows, width = tokens.shape
    hid, full = down_latent.shape[1:]
    sublanes = -(-n // 8) * 8
    gather_sends = 2 * n - 1
    dma = pltpu.SemaphoreType.DMA
    block = (n, tok_rows, width)
    vmem = pl.BlockSpec(memory_space=pltpu.VMEM)
    hbm = pl.BlockSpec(memory_space=pltpu.HBM)
    inputs = (tokens, teacher, expert_ids.T, gate_codes.T, gate_up_latent, down_latent)
    state = pl.pallas_call(
        functools.partial(dense_kernel, n_inner, n_outer),
        out_shape=(
            jax.ShapeDtypeStruct(tokens.shape, BF16),
            jax.ShapeDtypeStruct((3, hid, n * tok_rows), BF16),
            jax.ShapeDtypeStruct((2, *block), BF16),
            jax.ShapeDtypeStruct((2, *block), BF16),
            jax.ShapeDtypeStruct((3, hid, full), F32),
            jax.ShapeDtypeStruct((3, hid, full), F32),
        ),
        in_specs=[hbm] * 6,
        out_specs=(vmem,) * 6,
        scratch_shapes=[
            pltpu.VMEM((tok_rows, width), BF16),
            pltpu.VMEM(expert_ids.shape[::-1], jnp.int32),
            pltpu.VMEM(expert_ids.shape[::-1], jnp.int32),
            pltpu.VMEM((tok_rows, width), BF16),
            pltpu.VMEM((sublanes, LANES), F32),
            pltpu.VMEM((n, sublanes, LANES), F32),
            pltpu.VMEM((3, hid, full), BF16),
            pltpu.VMEM((2, hid, n * tok_rows), F32),
            pltpu.VMEM(block, BF16),
            pltpu.VMEM(block, BF16),
            pltpu.VMEM(block, F32),
            pltpu.VMEM(block, BF16),
            pltpu.VMEM(block, BF16),
            dma((7,)),
            dma((n,)),
            dma((n,)),
            dma((gather_sends,)),
            dma((n,)),
            dma((n,)),
            dma((n,)),
            dma((n,)),
            dma((n,)),
            dma((n,)),
            dma((gather_sends,)),
            dma((n,)),
            dma((n,)),
        ],
        compiler_params=pltpu.CompilerParams(
            collective_id=0, has_side_effects=True, vmem_limit_bytes=24 * 1024 * 1024
        ),
    )(*[pltpu.with_memory_space_constraint(value, pltpu.HBM) for value in inputs])
    return pl.pallas_call(
        update_kernel,
        out_shape=(
            jax.ShapeDtypeStruct(tokens.shape, BF16),
            jax.ShapeDtypeStruct(gate_up_latent.shape, F32),
            jax.ShapeDtypeStruct(down_latent.shape, F32),
        ),
        in_specs=[vmem] * 6,
        out_specs=(hbm,) * 3,
        scratch_shapes=[pltpu.VMEM((3, hid, full), F32), dma((4,))],
        compiler_params=pltpu.CompilerParams(vmem_limit_bytes=24 * 1024 * 1024),
    )(*state)


def on_device(tokens, teacher, expert_ids, gate_codes, gate_up_latent, down_latent):
    experts = lax.axis_size("inner") * lax.axis_size("outer")
    tok_rows, top_count = expert_ids.shape
    whole_block = 2 * top_count >= experts
    fits = (
        lax.axis_size("rep") == 2
        and LANES % tok_rows == 0
        and tok_rows % 16 == 0
        and experts <= LANES
        and experts * tok_rows % LANES == 0
        and tokens.shape[1] % LANES == 0
        and down_latent.shape[1] % 64 == 0
    )
    step = dense_step if whole_block and fits else routed_step
    return step(tokens, teacher, expert_ids, gate_codes, gate_up_latent, down_latent)


def solution(mesh):
    return jax.shard_map(
        on_device,
        mesh=mesh,
        in_specs=(
            P(("parts", "inner", "outer"), "rep"),
            P(("parts", "inner", "outer"), "rep"),
            P(("parts", "inner", "outer"), None),
            P(("parts", "inner", "outer"), None),
            P(("inner", "outer"), None, "rep", None),
            P(("inner", "outer"), "rep", None),
        ),
        out_specs=(
            P(("parts", "inner", "outer"), "rep"),
            P(("parts", "inner", "outer"), None, "rep", None),
            P(("parts", "inner", "outer"), "rep", None),
        ),
        check_vma=False,
    )
```

```python
import functools
import math

import jax
import jax.numpy as jnp
from jax import lax
from jax.experimental import pallas as pl
from jax.experimental.pallas import tpu as pltpu
from jax.sharding import PartitionSpec as P

D = 1024
HID = 384


learn_rate = 1.0


def soften(latent, fan_in):
    row_scale = jnp.mean(jnp.abs(latent), axis=-1, keepdims=True) + 1e-06
    normed = latent / row_scale
    lower = jnp.tanh(4.0 * (normed - 0.5))
    upper = jnp.tanh(4.0 * (normed + 0.5))
    fan_root = 1.0 / math.sqrt(fan_in)
    weight = (row_scale * 0.5 * (lower + upper) * fan_root).astype(jnp.bfloat16)
    slope = 2.0 * (2.0 - lower * lower - upper * upper) * fan_root
    return (weight, slope)


def dispatch_rows(outbox):
    return lax.all_to_all(outbox, ("inner", "outer"), split_axis=0, concat_axis=0, tiled=True)


def combine_rows(outbox):
    return lax.all_to_all(outbox, ("inner", "outer"), split_axis=0, concat_axis=0, tiled=True)


def upstream_rows(outbox):
    return lax.all_to_all(outbox, ("inner", "outer"), split_axis=0, concat_axis=0, tiled=True)


def routed_step(tokens, teacher, expert_ids, gate_codes, gate_up_latent, down_latent):
    experts = lax.axis_size("inner") * lax.axis_size("outer")
    tok_rows, top_count = expert_ids.shape
    part_width = tokens.shape[1]
    capacity = min(tok_rows, 2 * tok_rows * top_count // experts)
    flat_ids = expert_ids.reshape(-1)
    one_hot = (flat_ids[:, None] == jnp.arange(experts, dtype=jnp.int32)[None, :]).astype(jnp.int32)
    before = jnp.cumsum(one_hot, axis=0) - one_hot
    route_slot = jnp.sum(before * one_hot, axis=1)
    target = flat_ids * capacity + route_slot
    payload = jnp.repeat(tokens, top_count, axis=0)
    outbox = jnp.zeros((experts * capacity, part_width), jnp.bfloat16).at[target].set(payload)
    received = dispatch_rows(outbox)
    expert_rows = lax.all_gather(received, "rep", axis=1, tiled=True)
    gu_weight, gu_slope = soften(gate_up_latent[0], D)
    dn_weight, dn_slope = soften(down_latent[0], HID)
    projected = lax.dot_general(
        gu_weight, expert_rows, (((2,), (1,)), ((), ())), preferred_element_type=jnp.float32
    )
    pre_gate = projected[0]
    pre_up = projected[1]
    sigmoid_gate = jax.nn.sigmoid(pre_gate)
    activated = pre_gate * sigmoid_gate
    hidden = (activated * pre_up).astype(jnp.bfloat16)
    partial_out = lax.dot_general(
        hidden, dn_weight, (((0,), (0,)), ((), ())), preferred_element_type=jnp.float32
    )
    expert_out = lax.psum_scatter(
        partial_out.astype(jnp.bfloat16), "rep", scatter_dimension=1, tiled=True
    )
    returned = combine_rows(expert_out)
    picked = returned[target].reshape(tok_rows, top_count, part_width)
    gating = gate_codes.astype(jnp.float32) / 65536.0
    mixed = jnp.sum(gating[:, :, None] * picked.astype(jnp.float32), axis=1)
    student_out = mixed.astype(jnp.bfloat16)
    residual = mixed - teacher.astype(jnp.float32)
    pair_grad = (
        (gating[:, :, None] * residual[:, None, :]).astype(jnp.bfloat16).reshape(-1, part_width)
    )
    grad_outbox = (
        jnp.zeros((experts * capacity, part_width), jnp.bfloat16).at[target].set(pair_grad)
    )
    grad_part = upstream_rows(grad_outbox)
    out_grad = lax.all_gather(grad_part, "rep", axis=1, tiled=True)
    down_grad = jnp.dot(hidden, out_grad, preferred_element_type=jnp.float32)
    hidden_grad = lax.dot_general(
        dn_weight, out_grad, (((1,), (1,)), ((), ())), preferred_element_type=jnp.float32
    )
    gate_grad = (
        hidden_grad * pre_up * sigmoid_gate * (1.0 + pre_gate * (1.0 - sigmoid_gate))
    ).astype(jnp.bfloat16)
    up_grad = (hidden_grad * activated).astype(jnp.bfloat16)
    weight_grads = lax.dot_general(
        jnp.stack([gate_grad, up_grad]),
        expert_rows,
        (((2,), (0,)), ((), ())),
        preferred_element_type=jnp.float32,
    )
    new_gate_up = gate_up_latent - learn_rate * (gu_slope * weight_grads)[None]
    new_down = down_latent - learn_rate * (dn_slope * down_grad)[None]
    return (student_out, new_gate_up, new_down)


MESH = pl.DeviceIdType.MESH
LANES = 128
BF16 = jnp.bfloat16
F32 = jnp.float32


def dot_t(a, b):
    return lax.dot_general(a, b, (((1,), (1,)), ((), ())), preferred_element_type=F32)


def dense_kernel(
    n_inner, n_outer,
    tokens_ref, teacher_ref, ids_ref, codes_ref, gu_ref, dn_ref,
    student, grads, rows, resid, latent, slope,
    teacher, ids, codes, resid_own, gates_own, gates, weight, factor, sums, returned,
    load_sem, gate_send, gate_recv, tok_send, tok_recv, pair_send, pair_recv,
    sum_send, sum_recv, res_send, res_recv, res_rep,
):
    n = n_inner * n_outer
    tok_rows, width = tokens_ref.shape
    part = tok_rows // 2
    count = n * part
    hid = latent.shape[1]
    inner, outer, rep = lax.axis_index("inner"), lax.axis_index("outer"), lax.axis_index("rep")
    me = inner * n_outer + outer
    sides = (rep, 1 - rep)
    partner = {"rep": 1 - rep}

    def peer_at(step):
        peer = lax.rem(me + step + n, n)
        return peer, {"inner": peer // n_outer, "outer": lax.rem(peer, n_outer)}

    def remote(source, target, send, recv, device):
        return pltpu.make_async_remote_copy(
            src_ref=source, dst_ref=target, send_sem=send, recv_sem=recv,
            device_id=device, device_id_type=MESH,
        )

    others = [(step, side) for step in range(n) for side in range(2) if step or side]

    def part_rows(side):
        return pl.ds(pl.multiple_of(side * part, part), part)

    loads = [
        pltpu.make_async_copy(gu_ref.at[0, 0], latent.at[0], load_sem.at[0]),
        pltpu.make_async_copy(gu_ref.at[0, 1], latent.at[1], load_sem.at[1]),
        pltpu.make_async_copy(dn_ref.at[0], latent.at[2], load_sem.at[2]),
        pltpu.make_async_copy(
            tokens_ref.at[part_rows(rep)], rows.at[rep, rep, me], load_sem.at[3]
        ),
        pltpu.make_async_copy(teacher_ref, teacher, load_sem.at[4]),
        pltpu.make_async_copy(ids_ref, ids, load_sem.at[5]),
        pltpu.make_async_copy(codes_ref, codes, load_sem.at[6]),
    ]
    for load in loads:
        load.start()

    barrier = pltpu.get_barrier_semaphore()
    for step, side in others:
        device = dict(peer_at(step)[1], rep=sides[side])
        pl.semaphore_signal(barrier, inc=1, device_id=device, device_id_type=MESH)
    pl.semaphore_wait(barrier, len(others))

    sent = []

    def spread(source_of, target_of, send, recv, slot_of):
        for at, (step, side) in enumerate(others):
            peer, device = peer_at(step)
            copy = remote(
                source_of(peer, sides[side]), target_of(sides[side]),
                send.at[at], recv.at[slot_of], dict(device, rep=sides[side]),
            )
            copy.start()
            sent.append(copy)

    def arrived(source, target_of, send, recv, step, side):
        peer = peer_at(-step)[0]
        slot = sides[side] * n + peer
        remote(
            source, target_of(sides[side], peer), send.at[0], recv.at[slot], partner
        ).wait_recv()

    mine = rep * n + me
    spread(
        lambda peer, side: tokens_ref.at[part_rows(side)],
        lambda side: rows.at[side, rep, me],
        tok_send, tok_recv, mine,
    )

    loads[5].wait()
    loads[6].wait()
    gate_of = codes[...].astype(F32) * (1.0 / 65536.0)
    line = lax.broadcasted_iota(jnp.int32, (gates_own.shape[1], tok_rows), 0)
    table = jnp.zeros((gates_own.shape[1], tok_rows), F32)
    for expert in range(n):
        row = jnp.sum(jnp.where(ids[...] == expert, gate_of, 0.0), axis=0, keepdims=True)
        table = jnp.where(line == expert, row, table)
    gates_own[...] = jnp.zeros_like(gates_own)
    for half in range(2):
        gates_own[half, :, :part] = table[:, half * part : (half + 1) * part]
    for step in range(1, n):
        copy = remote(
            gates_own, gates.at[me], gate_send.at[step - 1], gate_recv.at[me], peer_at(step)[1]
        )
        copy.start()
        sent.append(copy)
    gates[me] = gates_own[...]

    fan_root = [1.0 / math.sqrt(latent.shape[2])] * 2 + [1.0 / math.sqrt(2 * hid)]
    piece = 32

    def soften_rows(matrix):
        root = fan_root[matrix]

        def body(at, carry):
            lines = pl.ds(pl.multiple_of(at * piece, piece), piece)
            value = latent[matrix, lines, :]
            row_scale = jnp.mean(jnp.abs(value), axis=-1, keepdims=True) + 1e-06
            steep = value * (4.0 / row_scale)
            lower = jnp.tanh(steep - 2.0)
            upper = jnp.tanh(steep + 2.0)
            weight[rep, matrix, lines, :] = (row_scale * (0.5 * root) * (lower + upper)).astype(BF16)
            slope[matrix, lines, :] = (2.0 * root) * (2.0 - lower * lower - upper * upper)
            return carry

        lax.fori_loop(0, hid // piece, body, 0)

    weight_copies = []
    for matrix in range(3):
        loads[matrix].wait()
        soften_rows(matrix)
        copy = remote(
            weight.at[rep, matrix], weight.at[rep, matrix],
            pair_send.at[matrix], pair_recv.at[matrix], partner,
        )
        copy.start()
        weight_copies.append(copy)
    sent.extend(weight_copies)

    for step in range(1, n):
        slot = peer_at(-step)[0]
        remote(gates_own, gates.at[slot], gate_send.at[0], gate_recv.at[slot], partner).wait_recv()
    per_row = LANES // part

    def gates_for(half):
        return jnp.concatenate(
            [
                sum(
                    pltpu.roll(gates[base + at, half, pl.ds(me, 1), :], at * part, 1) if at
                    else gates[base, half, pl.ds(me, 1), :]
                    for at in range(per_row)
                )
                for base in range(0, n, per_row)
            ],
            axis=1,
        )

    both_gates = [gates_for(half) for half in range(2)]
    own_gate = jnp.where(rep == 0, both_gates[0], both_gates[1])
    other_gate = jnp.where(rep == 0, both_gates[1], both_gates[0])

    def features(buf, half, column):
        return buf[half, column].reshape(count, width)

    def forward(units, half, gate_row):
        both = weight[units, 0:2].reshape(2 * hid, 2 * width)
        pre = dot_t(both[:, :width], features(rows, half, 0))
        pre = pre + dot_t(both[:, width:], features(rows, half, 1))
        pre_gate, pre_up = pre[:hid], pre[hid:]
        sigmoid_gate = jax.nn.sigmoid(pre_gate)
        activated = pre_gate * sigmoid_gate
        return pre_gate, pre_up, sigmoid_gate, activated, activated * pre_up * gate_row

    def keep(half, gate_row, values):
        pre_gate, pre_up, sigmoid_gate, activated, hidden = values
        cols = pl.ds(pl.multiple_of(half * count, count), count)
        grads[2, :, cols] = hidden.astype(BF16)
        factor[0, half] = gate_row * pre_up * sigmoid_gate * (1.0 + pre_gate * (1.0 - sigmoid_gate))
        factor[1, half] = gate_row * activated

    loads[3].wait()
    for step, side in others:
        arrived(
            tokens_ref.at[part_rows(0)], lambda side, peer: rows.at[rep, side, peer],
            tok_send, tok_recv, step, side,
        )
    rows_copy = remote(rows.at[rep], rows.at[rep], pair_send.at[3], pair_recv.at[3], partner)
    rows_copy.start()
    sent.append(rows_copy)
    own_values = forward(rep, rep, own_gate)
    out = jnp.dot(own_values[-1].T.astype(BF16), weight[rep, 2], preferred_element_type=F32)
    for copy in weight_copies:
        copy.wait_recv()
    hidden = forward(1 - rep, rep, own_gate)[-1]
    out = out + jnp.dot(hidden.T.astype(BF16), weight[1 - rep, 2], preferred_element_type=F32)
    for column in range(2):
        sums[column] = (
            out[:, column * width : (column + 1) * width].astype(BF16).reshape(n, part, width)
        )
    spread(
        lambda peer, side: sums.at[side, peer],
        lambda side: returned.at[rep, me],
        sum_send, sum_recv, mine,
    )
    returned[rep, me] = sums[rep, me]

    keep(rep, own_gate, own_values)
    rows_copy.wait_recv()
    keep(1 - rep, other_gate, forward(rep, 1 - rep, other_gate))

    loads[4].wait()
    for step, side in others:
        arrived(
            resid_own.at[0], lambda side, peer: returned.at[side, peer],
            sum_send, sum_recv, step, side,
        )
    for half in range(2):
        mixed = returned[half, 0].astype(F32)
        for peer in range(1, n):
            mixed = mixed + returned[half, peer].astype(F32)
        lines = slice(half * part, (half + 1) * part)
        student[lines] = mixed.astype(BF16)
        resid_own[half] = (mixed - teacher[lines].astype(F32)).astype(BF16)
    spread(
        lambda peer, side: resid_own.at[side],
        lambda side: resid.at[side, rep, me],
        res_send, res_recv, mine,
    )
    resid[rep, rep, me] = resid_own[rep]

    def pass_on(column, peer, at):
        copy = remote(
            resid.at[rep, column, peer], resid.at[rep, column, peer],
            res_send.at[2 * n + at], res_rep.at[column * n + peer], partner,
        )
        copy.start()
        sent.append(copy)

    pass_on(rep, me, 2 * n - 1)
    for at, (step, side) in enumerate(others):
        arrived(
            resid_own.at[0], lambda side, peer: resid.at[rep, side, peer],
            res_send, res_recv, step, side,
        )
        pass_on(sides[side], peer_at(-step)[0], at)

    def backward(half):
        down = weight[rep, 2]
        hidden_grad = dot_t(down[:, :width], features(resid, half, 0))
        hidden_grad = hidden_grad + dot_t(down[:, width:], features(resid, half, 1))
        cols = pl.ds(pl.multiple_of(half * count, count), count)
        grads[0, :, cols] = (hidden_grad * factor[0, half]).astype(BF16)
        grads[1, :, cols] = (hidden_grad * factor[1, half]).astype(BF16)

    backward(rep)
    for column in range(2):
        for peer in range(n):
            remote(
                resid_own.at[0], resid.at[1 - rep, column, peer],
                res_send.at[0], res_rep.at[column * n + peer], partner,
            ).wait_recv()
    backward(1 - rep)
    for copy in sent:
        copy.wait_send()


def update_kernel(
    student, grads, rows, resid, latent, slope,
    student_ref, new_gu_ref, new_dn_ref, fresh, store_sem,
):
    n, part, width = rows.shape[2:]
    stores = [pltpu.make_async_copy(student, student_ref, store_sem.at[3])]
    stores[0].start()
    targets = [new_gu_ref.at[0, 0], new_gu_ref.at[0, 1], new_dn_ref.at[0]]
    tile = min(width, 256)
    for matrix in range(3):
        source = resid if matrix == 2 else rows
        for side in range(2):
            for first in range(0, width, tile):
                block = source[:, side, :, :, first : first + tile].reshape(2 * n * part, tile)
                grad = jnp.dot(grads[matrix], block, preferred_element_type=F32)
                cols = slice(side * width + first, side * width + first + tile)
                fresh[matrix, :, cols] = latent[matrix, :, cols] - learn_rate * (
                    slope[matrix, :, cols] * grad
                )
        store = pltpu.make_async_copy(fresh.at[matrix], targets[matrix], store_sem.at[matrix])
        store.start()
        stores.append(store)
    for store in stores:
        store.wait()


def dense_step(tokens, teacher, expert_ids, gate_codes, gate_up_latent, down_latent):
    n_inner, n_outer = lax.axis_size("inner"), lax.axis_size("outer")
    n = n_inner * n_outer
    tok_rows, width = tokens.shape
    hid, full = down_latent.shape[1:]
    sublanes = -(-n // 8) * 8
    part = tok_rows // 2
    dma = pltpu.SemaphoreType.DMA
    halves = (2, n, part, width)
    vmem = pl.BlockSpec(memory_space=pltpu.VMEM)
    hbm = pl.BlockSpec(memory_space=pltpu.HBM)
    inputs = (tokens, teacher, expert_ids.T, gate_codes.T, gate_up_latent, down_latent)
    state = pl.pallas_call(
        functools.partial(dense_kernel, n_inner, n_outer),
        out_shape=(
            jax.ShapeDtypeStruct(tokens.shape, BF16),
            jax.ShapeDtypeStruct((3, hid, n * tok_rows), BF16),
            jax.ShapeDtypeStruct((2, *halves), BF16),
            jax.ShapeDtypeStruct((2, *halves), BF16),
            jax.ShapeDtypeStruct((3, hid, full), F32),
            jax.ShapeDtypeStruct((3, hid, full), F32),
        ),
        in_specs=[hbm] * 6,
        out_specs=(vmem,) * 6,
        scratch_shapes=[
            pltpu.VMEM((tok_rows, width), BF16),
            pltpu.VMEM(expert_ids.shape[::-1], jnp.int32),
            pltpu.VMEM(expert_ids.shape[::-1], jnp.int32),
            pltpu.VMEM((2, part, width), BF16),
            pltpu.VMEM((2, sublanes, LANES), F32),
            pltpu.VMEM((n, 2, sublanes, LANES), F32),
            pltpu.VMEM((2, 3, hid, full), BF16),
            pltpu.VMEM((2, 2, hid, n * part), F32),
            pltpu.VMEM(halves, BF16),
            pltpu.VMEM(halves, BF16),
            dma((7,)),
            dma((n,)),
            dma((n,)),
            dma((2 * n,)),
            dma((2 * n,)),
            dma((4,)),
            dma((4,)),
            dma((2 * n,)),
            dma((2 * n,)),
            dma((4 * n,)),
            dma((2 * n,)),
            dma((2 * n,)),
        ],
        compiler_params=pltpu.CompilerParams(
            collective_id=0, has_side_effects=True, vmem_limit_bytes=24 * 1024 * 1024
        ),
    )(*[pltpu.with_memory_space_constraint(value, pltpu.HBM) for value in inputs])
    return pl.pallas_call(
        update_kernel,
        out_shape=(
            jax.ShapeDtypeStruct(tokens.shape, BF16),
            jax.ShapeDtypeStruct(gate_up_latent.shape, F32),
            jax.ShapeDtypeStruct(down_latent.shape, F32),
        ),
        in_specs=[vmem] * 6,
        out_specs=(hbm,) * 3,
        scratch_shapes=[pltpu.VMEM((3, hid, full), F32), dma((4,))],
        compiler_params=pltpu.CompilerParams(vmem_limit_bytes=24 * 1024 * 1024),
    )(*state)


def on_device(tokens, teacher, expert_ids, gate_codes, gate_up_latent, down_latent):
    experts = lax.axis_size("inner") * lax.axis_size("outer")
    tok_rows, top_count = expert_ids.shape
    whole_block = 2 * top_count >= experts
    fits = (
        lax.axis_size("rep") == 2
        and LANES % tok_rows == 0
        and tok_rows % 32 == 0
        and experts <= LANES
        and experts * tok_rows % (2 * LANES) == 0
        and tokens.shape[1] % LANES == 0
        and down_latent.shape[1] % 64 == 0
    )
    step = dense_step if whole_block and fits else routed_step
    return step(tokens, teacher, expert_ids, gate_codes, gate_up_latent, down_latent)


def solution(mesh):
    return jax.shard_map(
        on_device,
        mesh=mesh,
        in_specs=(
            P(("parts", "inner", "outer"), "rep"),
            P(("parts", "inner", "outer"), "rep"),
            P(("parts", "inner", "outer"), None),
            P(("parts", "inner", "outer"), None),
            P(("inner", "outer"), None, "rep", None),
            P(("inner", "outer"), "rep", None),
        ),
        out_specs=(
            P(("parts", "inner", "outer"), "rep"),
            P(("parts", "inner", "outer"), None, "rep", None),
            P(("parts", "inner", "outer"), "rep", None),
        ),
        check_vma=False,
    )
```

```python
import functools
import math

import jax
import jax.numpy as jnp
from jax import lax
from jax.experimental import pallas as pl
from jax.experimental.pallas import tpu as pltpu
from jax.sharding import PartitionSpec as P

D = 1024
HID = 384


learn_rate = 1.0


def soften(latent, fan_in):
    row_scale = jnp.mean(jnp.abs(latent), axis=-1, keepdims=True) + 1e-06
    normed = latent / row_scale
    lower = jnp.tanh(4.0 * (normed - 0.5))
    upper = jnp.tanh(4.0 * (normed + 0.5))
    fan_root = 1.0 / math.sqrt(fan_in)
    weight = (row_scale * 0.5 * (lower + upper) * fan_root).astype(jnp.bfloat16)
    slope = 2.0 * (2.0 - lower * lower - upper * upper) * fan_root
    return (weight, slope)


def dispatch_rows(outbox):
    return lax.all_to_all(outbox, ("inner", "outer"), split_axis=0, concat_axis=0, tiled=True)


def combine_rows(outbox):
    return lax.all_to_all(outbox, ("inner", "outer"), split_axis=0, concat_axis=0, tiled=True)


def upstream_rows(outbox):
    return lax.all_to_all(outbox, ("inner", "outer"), split_axis=0, concat_axis=0, tiled=True)


def routed_step(tokens, teacher, expert_ids, gate_codes, gate_up_latent, down_latent):
    experts = lax.axis_size("inner") * lax.axis_size("outer")
    tok_rows, top_count = expert_ids.shape
    part_width = tokens.shape[1]
    capacity = min(tok_rows, 2 * tok_rows * top_count // experts)
    flat_ids = expert_ids.reshape(-1)
    one_hot = (flat_ids[:, None] == jnp.arange(experts, dtype=jnp.int32)[None, :]).astype(jnp.int32)
    before = jnp.cumsum(one_hot, axis=0) - one_hot
    route_slot = jnp.sum(before * one_hot, axis=1)
    target = flat_ids * capacity + route_slot
    payload = jnp.repeat(tokens, top_count, axis=0)
    outbox = jnp.zeros((experts * capacity, part_width), jnp.bfloat16).at[target].set(payload)
    received = dispatch_rows(outbox)
    expert_rows = lax.all_gather(received, "rep", axis=1, tiled=True)
    gu_weight, gu_slope = soften(gate_up_latent[0], D)
    dn_weight, dn_slope = soften(down_latent[0], HID)
    projected = lax.dot_general(
        gu_weight, expert_rows, (((2,), (1,)), ((), ())), preferred_element_type=jnp.float32
    )
    pre_gate = projected[0]
    pre_up = projected[1]
    sigmoid_gate = jax.nn.sigmoid(pre_gate)
    activated = pre_gate * sigmoid_gate
    hidden = (activated * pre_up).astype(jnp.bfloat16)
    partial_out = lax.dot_general(
        hidden, dn_weight, (((0,), (0,)), ((), ())), preferred_element_type=jnp.float32
    )
    expert_out = lax.psum_scatter(
        partial_out.astype(jnp.bfloat16), "rep", scatter_dimension=1, tiled=True
    )
    returned = combine_rows(expert_out)
    picked = returned[target].reshape(tok_rows, top_count, part_width)
    gating = gate_codes.astype(jnp.float32) / 65536.0
    mixed = jnp.sum(gating[:, :, None] * picked.astype(jnp.float32), axis=1)
    student_out = mixed.astype(jnp.bfloat16)
    residual = mixed - teacher.astype(jnp.float32)
    pair_grad = (
        (gating[:, :, None] * residual[:, None, :]).astype(jnp.bfloat16).reshape(-1, part_width)
    )
    grad_outbox = (
        jnp.zeros((experts * capacity, part_width), jnp.bfloat16).at[target].set(pair_grad)
    )
    grad_part = upstream_rows(grad_outbox)
    out_grad = lax.all_gather(grad_part, "rep", axis=1, tiled=True)
    down_grad = jnp.dot(hidden, out_grad, preferred_element_type=jnp.float32)
    hidden_grad = lax.dot_general(
        dn_weight, out_grad, (((1,), (1,)), ((), ())), preferred_element_type=jnp.float32
    )
    gate_grad = (
        hidden_grad * pre_up * sigmoid_gate * (1.0 + pre_gate * (1.0 - sigmoid_gate))
    ).astype(jnp.bfloat16)
    up_grad = (hidden_grad * activated).astype(jnp.bfloat16)
    weight_grads = lax.dot_general(
        jnp.stack([gate_grad, up_grad]),
        expert_rows,
        (((2,), (0,)), ((), ())),
        preferred_element_type=jnp.float32,
    )
    new_gate_up = gate_up_latent - learn_rate * (gu_slope * weight_grads)[None]
    new_down = down_latent - learn_rate * (dn_slope * down_grad)[None]
    return (student_out, new_gate_up, new_down)


MESH = pl.DeviceIdType.MESH
LANES = 128
BF16 = jnp.bfloat16
F32 = jnp.float32


def dot_t(a, b):
    return lax.dot_general(a, b, (((1,), (1,)), ((), ())), preferred_element_type=F32)


def dense_kernel(
    n_inner, n_outer,
    tokens_ref, teacher_ref, ids_ref, codes_ref, gu_ref, dn_ref,
    student, grads, rows, resid, latent, slope,
    teacher, ids, codes, resid_own, gates_own, gates, weight, factor, sums, returned,
    load_sem, gate_send, gate_recv, tok_send, tok_recv, pair_send, pair_recv,
    sum_send, sum_recv, res_send, res_recv, res_rep,
):
    n = n_inner * n_outer
    tok_rows, width = tokens_ref.shape
    part = tok_rows // 2
    count = n * part
    hid = latent.shape[1]
    inner, outer, rep = lax.axis_index("inner"), lax.axis_index("outer"), lax.axis_index("rep")
    me = inner * n_outer + outer
    sides = (rep, 1 - rep)
    partner = {"rep": 1 - rep}

    def peer_at(step):
        peer = lax.rem(me + step + n, n)
        return peer, {"inner": peer // n_outer, "outer": lax.rem(peer, n_outer)}

    def remote(source, target, send, recv, device):
        return pltpu.make_async_remote_copy(
            src_ref=source, dst_ref=target, send_sem=send, recv_sem=recv,
            device_id=device, device_id_type=MESH,
        )

    others = [(step, side) for step in range(n) for side in range(2) if step or side]

    def part_rows(side):
        return pl.ds(pl.multiple_of(side * part, part), part)

    loads = [
        pltpu.make_async_copy(gu_ref.at[0, 0], latent.at[0], load_sem.at[0]),
        pltpu.make_async_copy(gu_ref.at[0, 1], latent.at[1], load_sem.at[1]),
        pltpu.make_async_copy(dn_ref.at[0], latent.at[2], load_sem.at[2]),
        pltpu.make_async_copy(
            tokens_ref.at[part_rows(rep)], rows.at[rep, rep, me], load_sem.at[3]
        ),
        pltpu.make_async_copy(teacher_ref, teacher, load_sem.at[4]),
        pltpu.make_async_copy(ids_ref, ids, load_sem.at[5]),
        pltpu.make_async_copy(codes_ref, codes, load_sem.at[6]),
    ]
    barrier = pltpu.get_barrier_semaphore()
    for step, side in others:
        device = dict(peer_at(step)[1], rep=sides[side])
        pl.semaphore_signal(barrier, inc=1, device_id=device, device_id_type=MESH)
    for load in loads:
        load.start()
    pl.semaphore_wait(barrier, len(others))

    sent = []

    def spread(source_of, target_of, send, recv, slot_of):
        for at, (step, side) in enumerate(others):
            peer, device = peer_at(step)
            copy = remote(
                source_of(peer, sides[side]), target_of(sides[side]),
                send.at[at], recv.at[slot_of], dict(device, rep=sides[side]),
            )
            copy.start()
            sent.append(copy)

    def arrived(source, target_of, send, recv, step, side):
        peer = peer_at(-step)[0]
        slot = sides[side] * n + peer
        remote(
            source, target_of(sides[side], peer), send.at[0], recv.at[slot], partner
        ).wait_recv()

    mine = rep * n + me
    spread(
        lambda peer, side: tokens_ref.at[part_rows(side)],
        lambda side: rows.at[side, rep, me],
        tok_send, tok_recv, mine,
    )

    loads[5].wait()
    loads[6].wait()
    gate_of = codes[...].astype(F32) * (1.0 / 65536.0)
    line = lax.broadcasted_iota(jnp.int32, (gates_own.shape[1], tok_rows), 0)
    table = jnp.zeros((gates_own.shape[1], tok_rows), F32)
    for expert in range(n):
        row = jnp.sum(jnp.where(ids[...] == expert, gate_of, 0.0), axis=0, keepdims=True)
        table = jnp.where(line == expert, row, table)
    gates_own[...] = jnp.zeros_like(gates_own)
    for half in range(2):
        gates_own[half, :, :part] = table[:, half * part : (half + 1) * part]
    for step in range(1, n):
        copy = remote(
            gates_own, gates.at[me], gate_send.at[step - 1], gate_recv.at[me], peer_at(step)[1]
        )
        copy.start()
        sent.append(copy)
    gates[me] = gates_own[...]

    fan_root = [1.0 / math.sqrt(latent.shape[2])] * 2 + [1.0 / math.sqrt(2 * hid)]
    piece = 32

    def soften_rows(matrix):
        root = fan_root[matrix]

        def body(at, carry):
            lines = pl.ds(pl.multiple_of(at * piece, piece), piece)
            value = latent[matrix, lines, :]
            row_scale = jnp.mean(jnp.abs(value), axis=-1, keepdims=True) + 1e-06
            steep = value * (4.0 / row_scale)
            lower = jnp.tanh(steep - 2.0)
            upper = jnp.tanh(steep + 2.0)
            weight[rep, matrix, lines, :] = (row_scale * (0.5 * root) * (lower + upper)).astype(BF16)
            slope[matrix, lines, :] = (2.0 * root) * (2.0 - lower * lower - upper * upper)
            return carry

        lax.fori_loop(0, hid // piece, body, 0, unroll=3 if hid % (3 * piece) == 0 else 2)

    weight_copies = []
    for matrix in range(3):
        loads[matrix].wait()
        soften_rows(matrix)
        copy = remote(
            weight.at[rep, matrix], weight.at[rep, matrix],
            pair_send.at[matrix], pair_recv.at[matrix], partner,
        )
        copy.start()
        weight_copies.append(copy)
    sent.extend(weight_copies)

    for step in range(1, n):
        slot = peer_at(-step)[0]
        remote(gates_own, gates.at[slot], gate_send.at[0], gate_recv.at[slot], partner).wait_recv()
    per_row = LANES // part

    def gates_for(half):
        return jnp.concatenate(
            [
                sum(
                    pltpu.roll(gates[base + at, half, pl.ds(me, 1), :], at * part, 1) if at
                    else gates[base, half, pl.ds(me, 1), :]
                    for at in range(per_row)
                )
                for base in range(0, n, per_row)
            ],
            axis=1,
        )

    both_gates = [gates_for(half) for half in range(2)]
    own_gate = jnp.where(rep == 0, both_gates[0], both_gates[1])
    other_gate = jnp.where(rep == 0, both_gates[1], both_gates[0])

    def features(buf, half, column):
        return buf[half, column].reshape(count, width)

    def forward(units, half, gate_row):
        both = weight[units, 0:2].reshape(2 * hid, 2 * width)
        pre = dot_t(both[:, :width], features(rows, half, 0))
        pre = pre + dot_t(both[:, width:], features(rows, half, 1))
        pre_gate, pre_up = pre[:hid], pre[hid:]
        sigmoid_gate = jax.nn.sigmoid(pre_gate)
        activated = pre_gate * sigmoid_gate
        return pre_gate, pre_up, sigmoid_gate, activated, activated * pre_up * gate_row

    def keep(half, gate_row, values):
        pre_gate, pre_up, sigmoid_gate, activated, hidden = values
        cols = pl.ds(pl.multiple_of(half * count, count), count)
        grads[2, :, cols] = hidden.astype(BF16)
        factor[0, half] = gate_row * pre_up * sigmoid_gate * (1.0 + pre_gate * (1.0 - sigmoid_gate))
        factor[1, half] = gate_row * activated

    loads[3].wait()
    for step, side in others:
        arrived(
            tokens_ref.at[part_rows(0)], lambda side, peer: rows.at[rep, side, peer],
            tok_send, tok_recv, step, side,
        )
    own_values = forward(rep, rep, own_gate)
    out = jnp.dot(own_values[-1].T.astype(BF16), weight[rep, 2], preferred_element_type=F32)
    weight_copies[0].wait_recv()
    weight_copies[1].wait_recv()
    hidden = forward(1 - rep, rep, own_gate)[-1]
    weight_copies[2].wait_recv()
    out = out + jnp.dot(hidden.T.astype(BF16), weight[1 - rep, 2], preferred_element_type=F32)
    for column in range(2):
        sums[column] = (
            out[:, column * width : (column + 1) * width].astype(BF16).reshape(n, part, width)
        )
    spread(
        lambda peer, side: sums.at[side, peer],
        lambda side: returned.at[rep, me],
        sum_send, sum_recv, mine,
    )
    rows_copy = remote(rows.at[rep], rows.at[rep], pair_send.at[3], pair_recv.at[3], partner)
    rows_copy.start()
    sent.append(rows_copy)
    returned[rep, me] = sums[rep, me]

    keep(rep, own_gate, own_values)
    rows_copy.wait_recv()
    keep(1 - rep, other_gate, forward(rep, 1 - rep, other_gate))

    loads[4].wait()
    for step, side in others:
        arrived(
            resid_own.at[0], lambda side, peer: returned.at[side, peer],
            sum_send, sum_recv, step, side,
        )
    for half in range(2):
        mixed = returned[half, 0].astype(F32)
        for peer in range(1, n):
            mixed = mixed + returned[half, peer].astype(F32)
        lines = slice(half * part, (half + 1) * part)
        student[lines] = mixed.astype(BF16)
        resid_own[half] = (mixed - teacher[lines].astype(F32)).astype(BF16)
    spread(
        lambda peer, side: resid_own.at[side],
        lambda side: resid.at[side, rep, me],
        res_send, res_recv, mine,
    )
    resid[rep, rep, me] = resid_own[rep]

    def pass_on(column, peer, at):
        copy = remote(
            resid.at[rep, column, peer], resid.at[rep, column, peer],
            res_send.at[2 * n + at], res_rep.at[column * n + peer], partner,
        )
        copy.start()
        sent.append(copy)

    pass_on(rep, me, 2 * n - 1)
    for at, (step, side) in enumerate(others):
        arrived(
            resid_own.at[0], lambda side, peer: resid.at[rep, side, peer],
            res_send, res_recv, step, side,
        )
        pass_on(sides[side], peer_at(-step)[0], at)

    def backward(half):
        down = weight[rep, 2]
        hidden_grad = dot_t(down[:, :width], features(resid, half, 0))
        hidden_grad = hidden_grad + dot_t(down[:, width:], features(resid, half, 1))
        cols = pl.ds(pl.multiple_of(half * count, count), count)
        grads[0, :, cols] = (hidden_grad * factor[0, half]).astype(BF16)
        grads[1, :, cols] = (hidden_grad * factor[1, half]).astype(BF16)

    backward(rep)
    for column in range(2):
        for peer in range(n):
            remote(
                resid_own.at[0], resid.at[1 - rep, column, peer],
                res_send.at[0], res_rep.at[column * n + peer], partner,
            ).wait_recv()
    backward(1 - rep)
    for copy in sent:
        copy.wait_send()


def update_kernel(
    student, grads, rows, resid, latent, slope,
    student_ref, new_gu_ref, new_dn_ref, fresh, store_sem,
):
    n, part, width = rows.shape[2:]
    stores = [pltpu.make_async_copy(student, student_ref, store_sem.at[3])]
    stores[0].start()
    targets = [new_gu_ref.at[0, 0], new_gu_ref.at[0, 1], new_dn_ref.at[0]]
    tile = min(width, 256)
    for matrix in range(3):
        source = resid if matrix == 2 else rows
        for side in range(2):
            for first in range(0, width, tile):
                block = source[:, side, :, :, first : first + tile].reshape(2 * n * part, tile)
                grad = jnp.dot(grads[matrix], block, preferred_element_type=F32)
                cols = slice(side * width + first, side * width + first + tile)
                fresh[matrix, :, cols] = latent[matrix, :, cols] - learn_rate * (
                    slope[matrix, :, cols] * grad
                )
        store = pltpu.make_async_copy(fresh.at[matrix], targets[matrix], store_sem.at[matrix])
        store.start()
        stores.append(store)
    for store in stores:
        store.wait()


def dense_step(tokens, teacher, expert_ids, gate_codes, gate_up_latent, down_latent):
    n_inner, n_outer = lax.axis_size("inner"), lax.axis_size("outer")
    n = n_inner * n_outer
    tok_rows, width = tokens.shape
    hid, full = down_latent.shape[1:]
    sublanes = -(-n // 8) * 8
    part = tok_rows // 2
    dma = pltpu.SemaphoreType.DMA
    halves = (2, n, part, width)
    vmem = pl.BlockSpec(memory_space=pltpu.VMEM)
    hbm = pl.BlockSpec(memory_space=pltpu.HBM)
    inputs = (tokens, teacher, expert_ids.T, gate_codes.T, gate_up_latent, down_latent)
    state = pl.pallas_call(
        functools.partial(dense_kernel, n_inner, n_outer),
        out_shape=(
            jax.ShapeDtypeStruct(tokens.shape, BF16),
            jax.ShapeDtypeStruct((3, hid, n * tok_rows), BF16),
            jax.ShapeDtypeStruct((2, *halves), BF16),
            jax.ShapeDtypeStruct((2, *halves), BF16),
            jax.ShapeDtypeStruct((3, hid, full), F32),
            jax.ShapeDtypeStruct((3, hid, full), F32),
        ),
        in_specs=[hbm] * 6,
        out_specs=(vmem,) * 6,
        scratch_shapes=[
            pltpu.VMEM((tok_rows, width), BF16),
            pltpu.VMEM(expert_ids.shape[::-1], jnp.int32),
            pltpu.VMEM(expert_ids.shape[::-1], jnp.int32),
            pltpu.VMEM((2, part, width), BF16),
            pltpu.VMEM((2, sublanes, LANES), F32),
            pltpu.VMEM((n, 2, sublanes, LANES), F32),
            pltpu.VMEM((2, 3, hid, full), BF16),
            pltpu.VMEM((2, 2, hid, n * part), F32),
            pltpu.VMEM(halves, BF16),
            pltpu.VMEM(halves, BF16),
            dma((7,)),
            dma((n,)),
            dma((n,)),
            dma((2 * n,)),
            dma((2 * n,)),
            dma((4,)),
            dma((4,)),
            dma((2 * n,)),
            dma((2 * n,)),
            dma((4 * n,)),
            dma((2 * n,)),
            dma((2 * n,)),
        ],
        compiler_params=pltpu.CompilerParams(
            collective_id=0, has_side_effects=True, vmem_limit_bytes=24 * 1024 * 1024
        ),
    )(*[pltpu.with_memory_space_constraint(value, pltpu.HBM) for value in inputs])
    return pl.pallas_call(
        update_kernel,
        out_shape=(
            jax.ShapeDtypeStruct(tokens.shape, BF16),
            jax.ShapeDtypeStruct(gate_up_latent.shape, F32),
            jax.ShapeDtypeStruct(down_latent.shape, F32),
        ),
        in_specs=[vmem] * 6,
        out_specs=(hbm,) * 3,
        scratch_shapes=[pltpu.VMEM((3, hid, full), F32), dma((4,))],
        compiler_params=pltpu.CompilerParams(vmem_limit_bytes=24 * 1024 * 1024),
    )(*state)


def on_device(tokens, teacher, expert_ids, gate_codes, gate_up_latent, down_latent):
    experts = lax.axis_size("inner") * lax.axis_size("outer")
    tok_rows, top_count = expert_ids.shape
    whole_block = 2 * top_count >= experts
    fits = (
        lax.axis_size("rep") == 2
        and LANES % tok_rows == 0
        and tok_rows % 32 == 0
        and experts <= LANES
        and experts * tok_rows % (2 * LANES) == 0
        and tokens.shape[1] % LANES == 0
        and down_latent.shape[1] % 64 == 0
    )
    step = dense_step if whole_block and fits else routed_step
    return step(tokens, teacher, expert_ids, gate_codes, gate_up_latent, down_latent)


def solution(mesh):
    return jax.shard_map(
        on_device,
        mesh=mesh,
        in_specs=(
            P(("parts", "inner", "outer"), "rep"),
            P(("parts", "inner", "outer"), "rep"),
            P(("parts", "inner", "outer"), None),
            P(("parts", "inner", "outer"), None),
            P(("inner", "outer"), None, "rep", None),
            P(("inner", "outer"), "rep", None),
        ),
        out_specs=(
            P(("parts", "inner", "outer"), "rep"),
            P(("parts", "inner", "outer"), None, "rep", None),
            P(("parts", "inner", "outer"), "rep", None),
        ),
        check_vma=False,
    )
```

```python
import functools
import math

import jax
import jax.numpy as jnp
from jax import lax
from jax.experimental import pallas as pl
from jax.experimental.pallas import tpu as pltpu
from jax.sharding import PartitionSpec as P

D = 1024
HID = 384


learn_rate = 1.0


def soften(latent, fan_in):
    row_scale = jnp.mean(jnp.abs(latent), axis=-1, keepdims=True) + 1e-06
    normed = latent / row_scale
    lower = jnp.tanh(4.0 * (normed - 0.5))
    upper = jnp.tanh(4.0 * (normed + 0.5))
    fan_root = 1.0 / math.sqrt(fan_in)
    weight = (row_scale * 0.5 * (lower + upper) * fan_root).astype(jnp.bfloat16)
    slope = 2.0 * (2.0 - lower * lower - upper * upper) * fan_root
    return (weight, slope)


def dispatch_rows(outbox):
    return lax.all_to_all(outbox, ("inner", "outer"), split_axis=0, concat_axis=0, tiled=True)


def combine_rows(outbox):
    return lax.all_to_all(outbox, ("inner", "outer"), split_axis=0, concat_axis=0, tiled=True)


def upstream_rows(outbox):
    return lax.all_to_all(outbox, ("inner", "outer"), split_axis=0, concat_axis=0, tiled=True)


def routed_step(tokens, teacher, expert_ids, gate_codes, gate_up_latent, down_latent):
    experts = lax.axis_size("inner") * lax.axis_size("outer")
    tok_rows, top_count = expert_ids.shape
    part_width = tokens.shape[1]
    capacity = min(tok_rows, 2 * tok_rows * top_count // experts)
    flat_ids = expert_ids.reshape(-1)
    one_hot = (flat_ids[:, None] == jnp.arange(experts, dtype=jnp.int32)[None, :]).astype(jnp.int32)
    before = jnp.cumsum(one_hot, axis=0) - one_hot
    route_slot = jnp.sum(before * one_hot, axis=1)
    target = flat_ids * capacity + route_slot
    payload = jnp.repeat(tokens, top_count, axis=0)
    outbox = jnp.zeros((experts * capacity, part_width), jnp.bfloat16).at[target].set(payload)
    received = dispatch_rows(outbox)
    expert_rows = lax.all_gather(received, "rep", axis=1, tiled=True)
    gu_weight, gu_slope = soften(gate_up_latent[0], D)
    dn_weight, dn_slope = soften(down_latent[0], HID)
    projected = lax.dot_general(
        gu_weight, expert_rows, (((2,), (1,)), ((), ())), preferred_element_type=jnp.float32
    )
    pre_gate = projected[0]
    pre_up = projected[1]
    sigmoid_gate = jax.nn.sigmoid(pre_gate)
    activated = pre_gate * sigmoid_gate
    hidden = (activated * pre_up).astype(jnp.bfloat16)
    partial_out = lax.dot_general(
        hidden, dn_weight, (((0,), (0,)), ((), ())), preferred_element_type=jnp.float32
    )
    expert_out = lax.psum_scatter(
        partial_out.astype(jnp.bfloat16), "rep", scatter_dimension=1, tiled=True
    )
    returned = combine_rows(expert_out)
    picked = returned[target].reshape(tok_rows, top_count, part_width)
    gating = gate_codes.astype(jnp.float32) / 65536.0
    mixed = jnp.sum(gating[:, :, None] * picked.astype(jnp.float32), axis=1)
    student_out = mixed.astype(jnp.bfloat16)
    residual = mixed - teacher.astype(jnp.float32)
    pair_grad = (
        (gating[:, :, None] * residual[:, None, :]).astype(jnp.bfloat16).reshape(-1, part_width)
    )
    grad_outbox = (
        jnp.zeros((experts * capacity, part_width), jnp.bfloat16).at[target].set(pair_grad)
    )
    grad_part = upstream_rows(grad_outbox)
    out_grad = lax.all_gather(grad_part, "rep", axis=1, tiled=True)
    down_grad = jnp.dot(hidden, out_grad, preferred_element_type=jnp.float32)
    hidden_grad = lax.dot_general(
        dn_weight, out_grad, (((1,), (1,)), ((), ())), preferred_element_type=jnp.float32
    )
    gate_grad = (
        hidden_grad * pre_up * sigmoid_gate * (1.0 + pre_gate * (1.0 - sigmoid_gate))
    ).astype(jnp.bfloat16)
    up_grad = (hidden_grad * activated).astype(jnp.bfloat16)
    weight_grads = lax.dot_general(
        jnp.stack([gate_grad, up_grad]),
        expert_rows,
        (((2,), (0,)), ((), ())),
        preferred_element_type=jnp.float32,
    )
    new_gate_up = gate_up_latent - learn_rate * (gu_slope * weight_grads)[None]
    new_down = down_latent - learn_rate * (dn_slope * down_grad)[None]
    return (student_out, new_gate_up, new_down)


MESH = pl.DeviceIdType.MESH
LANES = 128
BF16 = jnp.bfloat16
F32 = jnp.float32


def dot_t(a, b):
    return lax.dot_general(a, b, (((1,), (1,)), ((), ())), preferred_element_type=F32)


def dense_kernel(
    n_inner, n_outer,
    tokens_ref, teacher_ref, ids_ref, codes_ref, gu_ref, dn_ref,
    student, grads, rows, resid, latent, slope,
    teacher, ids, codes, resid_own, gates_own, gates, weight, factor, sums, returned,
    load_sem, gate_send, gate_recv, tok_send, tok_recv, pair_send, pair_recv,
    sum_send, sum_recv, res_send, res_recv, res_rep,
):
    n = n_inner * n_outer
    tok_rows, width = tokens_ref.shape
    part = tok_rows // 2
    count = n * part
    hid = latent.shape[1]
    inner, outer, rep = lax.axis_index("inner"), lax.axis_index("outer"), lax.axis_index("rep")
    me = inner * n_outer + outer
    sides = (rep, 1 - rep)
    partner = {"rep": 1 - rep}

    def peer_at(step, sign=1):
        at_inner = lax.rem(inner + sign * step[0] + n_inner, n_inner)
        at_outer = lax.rem(outer + sign * step[1] + n_outer, n_outer)
        return at_inner * n_outer + at_outer, {"inner": at_inner, "outer": at_outer}

    def remote(source, target, send, recv, device):
        return pltpu.make_async_remote_copy(
            src_ref=source, dst_ref=target, send_sem=send, recv_sem=recv,
            device_id=device, device_id_type=MESH,
        )

    steps = [(up, across) for up in range(n_inner) for across in range(n_outer)]
    others = [(step, side) for step in steps for side in range(2) if any(step) or side]
    lined = [((up, 0), 0) for up in range(1, n_inner)]
    others = lined + [pair for pair in others if pair not in lined]
    relayed = [(step, side) for step, side in others if all(step) and not side]

    def part_rows(side):
        return pl.ds(pl.multiple_of(side * part, part), part)

    loads = [
        pltpu.make_async_copy(gu_ref.at[0, 0], latent.at[0], load_sem.at[0]),
        pltpu.make_async_copy(gu_ref.at[0, 1], latent.at[1], load_sem.at[1]),
        pltpu.make_async_copy(dn_ref.at[0], latent.at[2], load_sem.at[2]),
        pltpu.make_async_copy(
            tokens_ref.at[part_rows(rep)], rows.at[rep, rep, me], load_sem.at[3]
        ),
        pltpu.make_async_copy(teacher_ref, teacher, load_sem.at[4]),
        pltpu.make_async_copy(ids_ref, ids, load_sem.at[5]),
        pltpu.make_async_copy(codes_ref, codes, load_sem.at[6]),
    ]
    barrier = pltpu.get_barrier_semaphore()
    for step, side in others:
        device = dict(peer_at(step)[1], rep=sides[side])
        pl.semaphore_signal(barrier, inc=1, device_id=device, device_id_type=MESH)
    for load in loads:
        load.start()
    pl.semaphore_wait(barrier, len(others))

    sent = []

    def spread(source_of, target_of, send, recv, slot_of, skip=()):
        for at, (step, side) in enumerate(others):
            if (step, side) in skip:
                continue
            peer, device = peer_at(step)
            copy = remote(
                source_of(peer, sides[side]), target_of(sides[side]),
                send.at[at], recv.at[slot_of], dict(device, rep=sides[side]),
            )
            copy.start()
            sent.append(copy)

    def arrived(source, target_of, send, recv, step, side):
        peer = peer_at(step, -1)[0]
        slot = sides[side] * n + peer
        remote(
            source, target_of(sides[side], peer), send.at[0], recv.at[slot], partner
        ).wait_recv()

    def relay(source, buf, send, recv, step):
        arrived(source, lambda side, peer: buf.at[rep, side, peer], send, recv, step, 0)
        peer = peer_at(step, -1)[0]
        for across in range(1, n_outer):
            copy = remote(
                buf.at[rep, rep, peer], buf.at[rep, rep, peer],
                send.at[others.index(((step[0], across), 0))], recv.at[rep * n + peer],
                {"outer": lax.rem(outer + across, n_outer)},
            )
            copy.start()
            sent.append(copy)

    mine = rep * n + me
    spread(
        lambda peer, side: tokens_ref.at[part_rows(side)],
        lambda side: rows.at[side, rep, me],
        tok_send, tok_recv, mine, relayed,
    )

    loads[5].wait()
    loads[6].wait()
    gate_of = codes[...].astype(F32) * (1.0 / 65536.0)
    line = lax.broadcasted_iota(jnp.int32, (gates_own.shape[1], tok_rows), 0)
    table = jnp.zeros((gates_own.shape[1], tok_rows), F32)
    for expert in range(n):
        row = jnp.sum(jnp.where(ids[...] == expert, gate_of, 0.0), axis=0, keepdims=True)
        table = jnp.where(line == expert, row, table)
    gates_own[...] = jnp.zeros_like(gates_own)
    for half in range(2):
        gates_own[half, :, :part] = table[:, half * part : (half + 1) * part]
    for at, step in enumerate(steps[1:]):
        copy = remote(
            gates_own, gates.at[me], gate_send.at[at], gate_recv.at[me], peer_at(step)[1]
        )
        copy.start()
        sent.append(copy)
    gates[me] = gates_own[...]

    fan_root = [1.0 / math.sqrt(latent.shape[2])] * 2 + [1.0 / math.sqrt(2 * hid)]
    piece = 32

    def soften_rows(matrix):
        root = fan_root[matrix]

        def body(at, carry):
            lines = pl.ds(pl.multiple_of(at * piece, piece), piece)
            value = latent[matrix, lines, :]
            row_scale = jnp.mean(jnp.abs(value), axis=-1, keepdims=True) + 1e-06
            steep = value * (4.0 / row_scale)
            lower = jnp.tanh(steep - 2.0)
            upper = jnp.tanh(steep + 2.0)
            weight[rep, matrix, lines, :] = (row_scale * (0.5 * root) * (lower + upper)).astype(BF16)
            slope[matrix, lines, :] = (2.0 * root) * (2.0 - lower * lower - upper * upper)
            return carry

        lax.fori_loop(0, hid // piece, body, 0, unroll=3 if hid % (3 * piece) == 0 else 2)

    weight_copies = []
    for matrix in range(3):
        loads[matrix].wait()
        soften_rows(matrix)
        copy = remote(
            weight.at[rep, matrix], weight.at[rep, matrix],
            pair_send.at[matrix], pair_recv.at[matrix], partner,
        )
        copy.start()
        weight_copies.append(copy)
        if matrix == 0:
            for step, _ in lined:
                relay(tokens_ref.at[part_rows(0)], rows, tok_send, tok_recv, step)
    sent.extend(weight_copies)

    for step in steps[1:]:
        slot = peer_at(step, -1)[0]
        remote(gates_own, gates.at[slot], gate_send.at[0], gate_recv.at[slot], partner).wait_recv()
    per_row = LANES // part

    def gates_for(half):
        return jnp.concatenate(
            [
                sum(
                    pltpu.roll(gates[base + at, half, pl.ds(me, 1), :], at * part, 1) if at
                    else gates[base, half, pl.ds(me, 1), :]
                    for at in range(per_row)
                )
                for base in range(0, n, per_row)
            ],
            axis=1,
        )

    both_gates = [gates_for(half) for half in range(2)]
    own_gate = jnp.where(rep == 0, both_gates[0], both_gates[1])
    other_gate = jnp.where(rep == 0, both_gates[1], both_gates[0])

    def features(buf, half, column):
        return buf[half, column].reshape(count, width)

    def forward(units, half, gate_row):
        both = weight[units, 0:2].reshape(2 * hid, 2 * width)
        pre = dot_t(both[:, :width], features(rows, half, 0))
        pre = pre + dot_t(both[:, width:], features(rows, half, 1))
        pre_gate, pre_up = pre[:hid], pre[hid:]
        sigmoid_gate = jax.nn.sigmoid(pre_gate)
        activated = pre_gate * sigmoid_gate
        return pre_gate, pre_up, sigmoid_gate, activated, activated * pre_up * gate_row

    def keep(half, gate_row, values):
        pre_gate, pre_up, sigmoid_gate, activated, hidden = values
        cols = pl.ds(pl.multiple_of(half * count, count), count)
        grads[2, :, cols] = hidden.astype(BF16)
        factor[0, half] = gate_row * pre_up * sigmoid_gate * (1.0 + pre_gate * (1.0 - sigmoid_gate))
        factor[1, half] = gate_row * activated

    loads[3].wait()
    for step, side in others[len(lined):]:
        arrived(
            tokens_ref.at[part_rows(0)], lambda side, peer: rows.at[rep, side, peer],
            tok_send, tok_recv, step, side,
        )
    own_values = forward(rep, rep, own_gate)
    out = jnp.dot(own_values[-1].T.astype(BF16), weight[rep, 2], preferred_element_type=F32)
    weight_copies[0].wait_recv()
    weight_copies[1].wait_recv()
    hidden = forward(1 - rep, rep, own_gate)[-1]
    weight_copies[2].wait_recv()
    out = out + jnp.dot(hidden.T.astype(BF16), weight[1 - rep, 2], preferred_element_type=F32)
    for column in range(2):
        sums[column] = (
            out[:, column * width : (column + 1) * width].astype(BF16).reshape(n, part, width)
        )
    spread(
        lambda peer, side: sums.at[side, peer],
        lambda side: returned.at[rep, me],
        sum_send, sum_recv, mine,
    )
    rows_copy = remote(rows.at[rep], rows.at[rep], pair_send.at[3], pair_recv.at[3], partner)
    rows_copy.start()
    sent.append(rows_copy)
    returned[rep, me] = sums[rep, me]

    keep(rep, own_gate, own_values)
    rows_copy.wait_recv()
    keep(1 - rep, other_gate, forward(rep, 1 - rep, other_gate))

    loads[4].wait()
    for step, side in others:
        arrived(
            resid_own.at[0], lambda side, peer: returned.at[side, peer],
            sum_send, sum_recv, step, side,
        )
    for half in range(2):
        mixed = returned[half, 0].astype(F32)
        for peer in range(1, n):
            mixed = mixed + returned[half, peer].astype(F32)
        lines = slice(half * part, (half + 1) * part)
        student[lines] = mixed.astype(BF16)
        resid_own[half] = (mixed - teacher[lines].astype(F32)).astype(BF16)
    spread(
        lambda peer, side: resid_own.at[side],
        lambda side: resid.at[side, rep, me],
        res_send, res_recv, mine, relayed,
    )
    resid[rep, rep, me] = resid_own[rep]

    def pass_on(column, peer, at):
        copy = remote(
            resid.at[rep, column, peer], resid.at[rep, column, peer],
            res_send.at[2 * n + at], res_rep.at[column * n + peer], partner,
        )
        copy.start()
        sent.append(copy)

    pass_on(rep, me, 2 * n - 1)
    for at, (step, side) in enumerate(others):
        if at < len(lined):
            relay(resid_own.at[0], resid, res_send, res_recv, step)
        else:
            arrived(
                resid_own.at[0], lambda side, peer: resid.at[rep, side, peer],
                res_send, res_recv, step, side,
            )
        pass_on(sides[side], peer_at(step, -1)[0], at)

    def backward(half):
        down = weight[rep, 2]
        hidden_grad = dot_t(down[:, :width], features(resid, half, 0))
        hidden_grad = hidden_grad + dot_t(down[:, width:], features(resid, half, 1))
        cols = pl.ds(pl.multiple_of(half * count, count), count)
        grads[0, :, cols] = (hidden_grad * factor[0, half]).astype(BF16)
        grads[1, :, cols] = (hidden_grad * factor[1, half]).astype(BF16)

    backward(rep)
    for column in range(2):
        for peer in range(n):
            remote(
                resid_own.at[0], resid.at[1 - rep, column, peer],
                res_send.at[0], res_rep.at[column * n + peer], partner,
            ).wait_recv()
    backward(1 - rep)
    for copy in sent:
        copy.wait_send()


def update_kernel(
    student, grads, rows, resid, latent, slope,
    student_ref, new_gu_ref, new_dn_ref, fresh, store_sem,
):
    n, part, width = rows.shape[2:]
    stores = [pltpu.make_async_copy(student, student_ref, store_sem.at[3])]
    stores[0].start()
    targets = [new_gu_ref.at[0, 0], new_gu_ref.at[0, 1], new_dn_ref.at[0]]
    tile = min(width, 256)
    for matrix in range(3):
        source = resid if matrix == 2 else rows
        for side in range(2):
            for first in range(0, width, tile):
                block = source[:, side, :, :, first : first + tile].reshape(2 * n * part, tile)
                grad = jnp.dot(grads[matrix], block, preferred_element_type=F32)
                cols = slice(side * width + first, side * width + first + tile)
                fresh[matrix, :, cols] = latent[matrix, :, cols] - learn_rate * (
                    slope[matrix, :, cols] * grad
                )
        store = pltpu.make_async_copy(fresh.at[matrix], targets[matrix], store_sem.at[matrix])
        store.start()
        stores.append(store)
    for store in stores:
        store.wait()


def dense_step(tokens, teacher, expert_ids, gate_codes, gate_up_latent, down_latent):
    n_inner, n_outer = lax.axis_size("inner"), lax.axis_size("outer")
    n = n_inner * n_outer
    tok_rows, width = tokens.shape
    hid, full = down_latent.shape[1:]
    sublanes = -(-n // 8) * 8
    part = tok_rows // 2
    dma = pltpu.SemaphoreType.DMA
    halves = (2, n, part, width)
    vmem = pl.BlockSpec(memory_space=pltpu.VMEM)
    hbm = pl.BlockSpec(memory_space=pltpu.HBM)
    inputs = (tokens, teacher, expert_ids.T, gate_codes.T, gate_up_latent, down_latent)
    state = pl.pallas_call(
        functools.partial(dense_kernel, n_inner, n_outer),
        out_shape=(
            jax.ShapeDtypeStruct(tokens.shape, BF16),
            jax.ShapeDtypeStruct((3, hid, n * tok_rows), BF16),
            jax.ShapeDtypeStruct((2, *halves), BF16),
            jax.ShapeDtypeStruct((2, *halves), BF16),
            jax.ShapeDtypeStruct((3, hid, full), F32),
            jax.ShapeDtypeStruct((3, hid, full), F32),
        ),
        in_specs=[hbm] * 6,
        out_specs=(vmem,) * 6,
        scratch_shapes=[
            pltpu.VMEM((tok_rows, width), BF16),
            pltpu.VMEM(expert_ids.shape[::-1], jnp.int32),
            pltpu.VMEM(expert_ids.shape[::-1], jnp.int32),
            pltpu.VMEM((2, part, width), BF16),
            pltpu.VMEM((2, sublanes, LANES), F32),
            pltpu.VMEM((n, 2, sublanes, LANES), F32),
            pltpu.VMEM((2, 3, hid, full), BF16),
            pltpu.VMEM((2, 2, hid, n * part), F32),
            pltpu.VMEM(halves, BF16),
            pltpu.VMEM(halves, BF16),
            dma((7,)),
            dma((n,)),
            dma((n,)),
            dma((2 * n,)),
            dma((2 * n,)),
            dma((4,)),
            dma((4,)),
            dma((2 * n,)),
            dma((2 * n,)),
            dma((4 * n,)),
            dma((2 * n,)),
            dma((2 * n,)),
        ],
        compiler_params=pltpu.CompilerParams(
            collective_id=0, has_side_effects=True, vmem_limit_bytes=24 * 1024 * 1024
        ),
    )(*[pltpu.with_memory_space_constraint(value, pltpu.HBM) for value in inputs])
    return pl.pallas_call(
        update_kernel,
        out_shape=(
            jax.ShapeDtypeStruct(tokens.shape, BF16),
            jax.ShapeDtypeStruct(gate_up_latent.shape, F32),
            jax.ShapeDtypeStruct(down_latent.shape, F32),
        ),
        in_specs=[vmem] * 6,
        out_specs=(hbm,) * 3,
        scratch_shapes=[pltpu.VMEM((3, hid, full), F32), dma((4,))],
        compiler_params=pltpu.CompilerParams(vmem_limit_bytes=24 * 1024 * 1024),
    )(*state)


def on_device(tokens, teacher, expert_ids, gate_codes, gate_up_latent, down_latent):
    experts = lax.axis_size("inner") * lax.axis_size("outer")
    tok_rows, top_count = expert_ids.shape
    whole_block = 2 * top_count >= experts
    fits = (
        lax.axis_size("rep") == 2
        and LANES % tok_rows == 0
        and tok_rows % 32 == 0
        and experts <= LANES
        and experts * tok_rows % (2 * LANES) == 0
        and tokens.shape[1] % LANES == 0
        and down_latent.shape[1] % 64 == 0
    )
    step = dense_step if whole_block and fits else routed_step
    return step(tokens, teacher, expert_ids, gate_codes, gate_up_latent, down_latent)


def solution(mesh):
    return jax.shard_map(
        on_device,
        mesh=mesh,
        in_specs=(
            P(("parts", "inner", "outer"), "rep"),
            P(("parts", "inner", "outer"), "rep"),
            P(("parts", "inner", "outer"), None),
            P(("parts", "inner", "outer"), None),
            P(("inner", "outer"), None, "rep", None),
            P(("inner", "outer"), "rep", None),
        ),
        out_specs=(
            P(("parts", "inner", "outer"), "rep"),
            P(("parts", "inner", "outer"), None, "rep", None),
            P(("parts", "inner", "outer"), "rep", None),
        ),
        check_vma=False,
    )
```

```python
import functools
import math

import jax
import jax.numpy as jnp
from jax import lax
from jax.experimental import pallas as pl
from jax.experimental.pallas import tpu as pltpu
from jax.sharding import PartitionSpec as P

D = 1024
HID = 384


learn_rate = 1.0


def soften(latent, fan_in):
    row_scale = jnp.mean(jnp.abs(latent), axis=-1, keepdims=True) + 1e-06
    normed = latent / row_scale
    lower = jnp.tanh(4.0 * (normed - 0.5))
    upper = jnp.tanh(4.0 * (normed + 0.5))
    fan_root = 1.0 / math.sqrt(fan_in)
    weight = (row_scale * 0.5 * (lower + upper) * fan_root).astype(jnp.bfloat16)
    slope = 2.0 * (2.0 - lower * lower - upper * upper) * fan_root
    return (weight, slope)


def dispatch_rows(outbox):
    return lax.all_to_all(outbox, ("inner", "outer"), split_axis=0, concat_axis=0, tiled=True)


def combine_rows(outbox):
    return lax.all_to_all(outbox, ("inner", "outer"), split_axis=0, concat_axis=0, tiled=True)


def upstream_rows(outbox):
    return lax.all_to_all(outbox, ("inner", "outer"), split_axis=0, concat_axis=0, tiled=True)


def routed_step(tokens, teacher, expert_ids, gate_codes, gate_up_latent, down_latent):
    experts = lax.axis_size("inner") * lax.axis_size("outer")
    tok_rows, top_count = expert_ids.shape
    part_width = tokens.shape[1]
    capacity = min(tok_rows, 2 * tok_rows * top_count // experts)
    flat_ids = expert_ids.reshape(-1)
    one_hot = (flat_ids[:, None] == jnp.arange(experts, dtype=jnp.int32)[None, :]).astype(jnp.int32)
    before = jnp.cumsum(one_hot, axis=0) - one_hot
    route_slot = jnp.sum(before * one_hot, axis=1)
    target = flat_ids * capacity + route_slot
    payload = jnp.repeat(tokens, top_count, axis=0)
    outbox = jnp.zeros((experts * capacity, part_width), jnp.bfloat16).at[target].set(payload)
    received = dispatch_rows(outbox)
    expert_rows = lax.all_gather(received, "rep", axis=1, tiled=True)
    gu_weight, gu_slope = soften(gate_up_latent[0], D)
    dn_weight, dn_slope = soften(down_latent[0], HID)
    projected = lax.dot_general(
        gu_weight, expert_rows, (((2,), (1,)), ((), ())), preferred_element_type=jnp.float32
    )
    pre_gate = projected[0]
    pre_up = projected[1]
    sigmoid_gate = jax.nn.sigmoid(pre_gate)
    activated = pre_gate * sigmoid_gate
    hidden = (activated * pre_up).astype(jnp.bfloat16)
    partial_out = lax.dot_general(
        hidden, dn_weight, (((0,), (0,)), ((), ())), preferred_element_type=jnp.float32
    )
    expert_out = lax.psum_scatter(
        partial_out.astype(jnp.bfloat16), "rep", scatter_dimension=1, tiled=True
    )
    returned = combine_rows(expert_out)
    picked = returned[target].reshape(tok_rows, top_count, part_width)
    gating = gate_codes.astype(jnp.float32) / 65536.0
    mixed = jnp.sum(gating[:, :, None] * picked.astype(jnp.float32), axis=1)
    student_out = mixed.astype(jnp.bfloat16)
    residual = mixed - teacher.astype(jnp.float32)
    pair_grad = (
        (gating[:, :, None] * residual[:, None, :]).astype(jnp.bfloat16).reshape(-1, part_width)
    )
    grad_outbox = (
        jnp.zeros((experts * capacity, part_width), jnp.bfloat16).at[target].set(pair_grad)
    )
    grad_part = upstream_rows(grad_outbox)
    out_grad = lax.all_gather(grad_part, "rep", axis=1, tiled=True)
    down_grad = jnp.dot(hidden, out_grad, preferred_element_type=jnp.float32)
    hidden_grad = lax.dot_general(
        dn_weight, out_grad, (((1,), (1,)), ((), ())), preferred_element_type=jnp.float32
    )
    gate_grad = (
        hidden_grad * pre_up * sigmoid_gate * (1.0 + pre_gate * (1.0 - sigmoid_gate))
    ).astype(jnp.bfloat16)
    up_grad = (hidden_grad * activated).astype(jnp.bfloat16)
    weight_grads = lax.dot_general(
        jnp.stack([gate_grad, up_grad]),
        expert_rows,
        (((2,), (0,)), ((), ())),
        preferred_element_type=jnp.float32,
    )
    new_gate_up = gate_up_latent - learn_rate * (gu_slope * weight_grads)[None]
    new_down = down_latent - learn_rate * (dn_slope * down_grad)[None]
    return (student_out, new_gate_up, new_down)


MESH = pl.DeviceIdType.MESH
LANES = 128
BF16 = jnp.bfloat16
F32 = jnp.float32


def dot_t(a, b):
    return lax.dot_general(a, b, (((1,), (1,)), ((), ())), preferred_element_type=F32)


def dense_kernel(
    n_inner, n_outer,
    tokens_ref, teacher_ref, ids_ref, codes_ref, gu_ref, dn_ref,
    student, grads, rows, resid, latent, slope,
    tokens, teacher, ids, codes, resid_own, gates_own, gates, weight, factor, sums, returned,
    load_sem, gate_send, gate_recv, tok_send, tok_recv, pair_send, pair_recv,
    sum_send, sum_recv, res_send, res_recv, res_rep,
):
    n = n_inner * n_outer
    tok_rows, width = tokens_ref.shape
    part = tok_rows // 2
    count = n * part
    hid = latent.shape[1]
    inner, outer, rep = lax.axis_index("inner"), lax.axis_index("outer"), lax.axis_index("rep")
    me = inner * n_outer + outer
    sides = (rep, 1 - rep)
    partner = {"rep": 1 - rep}

    def peer_at(step):
        peer = lax.rem(me + step + n, n)
        return peer, {"inner": peer // n_outer, "outer": lax.rem(peer, n_outer)}

    def remote(source, target, send, recv, device):
        return pltpu.make_async_remote_copy(
            src_ref=source, dst_ref=target, send_sem=send, recv_sem=recv,
            device_id=device, device_id_type=MESH,
        )

    others = [(step, side) for step in range(n) for side in range(2) if step or side]

    def part_rows(side):
        return pl.ds(pl.multiple_of(side * part, part), part)

    loads = [
        pltpu.make_async_copy(gu_ref.at[0, 0], latent.at[0], load_sem.at[0]),
        pltpu.make_async_copy(gu_ref.at[0, 1], latent.at[1], load_sem.at[1]),
        pltpu.make_async_copy(dn_ref.at[0], latent.at[2], load_sem.at[2]),
        pltpu.make_async_copy(tokens_ref, tokens, load_sem.at[3]),
        pltpu.make_async_copy(teacher_ref, teacher, load_sem.at[4]),
        pltpu.make_async_copy(ids_ref, ids, load_sem.at[5]),
        pltpu.make_async_copy(codes_ref, codes, load_sem.at[6]),
    ]
    barrier = pltpu.get_barrier_semaphore()
    for step, side in others:
        device = dict(peer_at(step)[1], rep=sides[side])
        pl.semaphore_signal(barrier, inc=1, device_id=device, device_id_type=MESH)
    for load in loads[3:] + loads[:3]:
        load.start()
    pl.semaphore_wait(barrier, len(others))

    sent = []

    def spread(source_of, target_of, send, recv, slot_of):
        for at, (step, side) in enumerate(others):
            peer, device = peer_at(step)
            copy = remote(
                source_of(peer, sides[side]), target_of(sides[side]),
                send.at[at], recv.at[slot_of], dict(device, rep=sides[side]),
            )
            copy.start()
            sent.append(copy)

    def arrived(source, target_of, send, recv, step, side):
        peer = peer_at(-step)[0]
        slot = sides[side] * n + peer
        remote(
            source, target_of(sides[side], peer), send.at[0], recv.at[slot], partner
        ).wait_recv()

    mine = rep * n + me
    loads[3].wait()
    spread(
        lambda peer, side: tokens.at[part_rows(side)],
        lambda side: rows.at[side, rep, me],
        tok_send, tok_recv, mine,
    )

    loads[5].wait()
    loads[6].wait()
    gate_of = codes[...].astype(F32) * (1.0 / 65536.0)
    line = lax.broadcasted_iota(jnp.int32, (gates_own.shape[1], tok_rows), 0)
    table = jnp.zeros((gates_own.shape[1], tok_rows), F32)
    for expert in range(n):
        row = jnp.sum(jnp.where(ids[...] == expert, gate_of, 0.0), axis=0, keepdims=True)
        table = jnp.where(line == expert, row, table)
    gates_own[...] = jnp.zeros_like(gates_own)
    for half in range(2):
        gates_own[half, :, :part] = table[:, half * part : (half + 1) * part]
    for step in range(1, n):
        copy = remote(
            gates_own, gates.at[me], gate_send.at[step - 1], gate_recv.at[me], peer_at(step)[1]
        )
        copy.start()
        sent.append(copy)
    gates[me] = gates_own[...]

    fan_root = [1.0 / math.sqrt(latent.shape[2])] * 2 + [1.0 / math.sqrt(2 * hid)]
    piece = 32

    def soften_rows(matrix):
        root = fan_root[matrix]

        def body(at, carry):
            lines = pl.ds(pl.multiple_of(at * piece, piece), piece)
            value = latent[matrix, lines, :]
            row_scale = jnp.mean(jnp.abs(value), axis=-1, keepdims=True) + 1e-06
            steep = value * (4.0 / row_scale)
            lower = jnp.tanh(steep - 2.0)
            upper = jnp.tanh(steep + 2.0)
            weight[rep, matrix, lines, :] = (row_scale * (0.5 * root) * (lower + upper)).astype(BF16)
            slope[matrix, lines, :] = (2.0 * root) * (2.0 - lower * lower - upper * upper)
            return carry

        lax.fori_loop(0, hid // piece, body, 0, unroll=3 if hid % (3 * piece) == 0 else 2)

    weight_copies = []
    for matrix in range(3):
        loads[matrix].wait()
        soften_rows(matrix)
        copy = remote(
            weight.at[rep, matrix], weight.at[rep, matrix],
            pair_send.at[matrix], pair_recv.at[matrix], partner,
        )
        copy.start()
        weight_copies.append(copy)
    sent.extend(weight_copies)

    for step in range(1, n):
        slot = peer_at(-step)[0]
        remote(gates_own, gates.at[slot], gate_send.at[0], gate_recv.at[slot], partner).wait_recv()
    per_row = LANES // part

    def gates_for(half):
        return jnp.concatenate(
            [
                sum(
                    pltpu.roll(gates[base + at, half, pl.ds(me, 1), :], at * part, 1) if at
                    else gates[base, half, pl.ds(me, 1), :]
                    for at in range(per_row)
                )
                for base in range(0, n, per_row)
            ],
            axis=1,
        )

    both_gates = [gates_for(half) for half in range(2)]
    own_gate = jnp.where(rep == 0, both_gates[0], both_gates[1])
    other_gate = jnp.where(rep == 0, both_gates[1], both_gates[0])

    def features(buf, half, column):
        return buf[half, column].reshape(count, width)

    def forward(units, half, gate_row):
        both = weight[units, 0:2].reshape(2 * hid, 2 * width)
        pre = dot_t(both[:, :width], features(rows, half, 0))
        pre = pre + dot_t(both[:, width:], features(rows, half, 1))
        pre_gate, pre_up = pre[:hid], pre[hid:]
        sigmoid_gate = jax.nn.sigmoid(pre_gate)
        activated = pre_gate * sigmoid_gate
        return pre_gate, pre_up, sigmoid_gate, activated, activated * pre_up * gate_row

    def keep(half, gate_row, values):
        pre_gate, pre_up, sigmoid_gate, activated, hidden = values
        cols = pl.ds(pl.multiple_of(half * count, count), count)
        grads[2, :, cols] = hidden.astype(BF16)
        factor[0, half] = gate_row * pre_up * sigmoid_gate * (1.0 + pre_gate * (1.0 - sigmoid_gate))
        factor[1, half] = gate_row * activated

    rows[rep, rep, me] = tokens[part_rows(rep), :]
    for step, side in others:
        arrived(
            tokens.at[part_rows(0)], lambda side, peer: rows.at[rep, side, peer],
            tok_send, tok_recv, step, side,
        )
    own_values = forward(rep, rep, own_gate)
    out = jnp.dot(own_values[-1].T.astype(BF16), weight[rep, 2], preferred_element_type=F32)
    weight_copies[0].wait_recv()
    weight_copies[1].wait_recv()
    hidden = forward(1 - rep, rep, own_gate)[-1]
    weight_copies[2].wait_recv()
    out = out + jnp.dot(hidden.T.astype(BF16), weight[1 - rep, 2], preferred_element_type=F32)
    for column in range(2):
        sums[column] = (
            out[:, column * width : (column + 1) * width].astype(BF16).reshape(n, part, width)
        )
    spread(
        lambda peer, side: sums.at[side, peer],
        lambda side: returned.at[rep, me],
        sum_send, sum_recv, mine,
    )
    rows_copy = remote(rows.at[rep], rows.at[rep], pair_send.at[3], pair_recv.at[3], partner)
    rows_copy.start()
    sent.append(rows_copy)
    returned[rep, me] = sums[rep, me]

    keep(rep, own_gate, own_values)
    rows_copy.wait_recv()
    keep(1 - rep, other_gate, forward(rep, 1 - rep, other_gate))

    loads[4].wait()
    for step, side in others:
        arrived(
            resid_own.at[0], lambda side, peer: returned.at[side, peer],
            sum_send, sum_recv, step, side,
        )
    for half in range(2):
        mixed = returned[half, 0].astype(F32)
        for peer in range(1, n):
            mixed = mixed + returned[half, peer].astype(F32)
        lines = slice(half * part, (half + 1) * part)
        student[lines] = mixed.astype(BF16)
        resid_own[half] = (mixed - teacher[lines].astype(F32)).astype(BF16)
    spread(
        lambda peer, side: resid_own.at[side],
        lambda side: resid.at[side, rep, me],
        res_send, res_recv, mine,
    )
    resid[rep, rep, me] = resid_own[rep]

    passed = []
    for side in (1, 0):
        for step, of in others:
            if of == side:
                arrived(
                    resid_own.at[0], lambda side, peer: resid.at[rep, side, peer],
                    res_send, res_recv, step, side,
                )
        column = sides[side]
        copy = remote(
            resid.at[rep, column], resid.at[rep, column],
            res_send.at[2 * n + side], res_rep.at[side], partner,
        )
        copy.start()
        passed.append(copy)
    sent.extend(passed)

    def backward(half):
        down = weight[rep, 2]
        hidden_grad = dot_t(down[:, :width], features(resid, half, 0))
        hidden_grad = hidden_grad + dot_t(down[:, width:], features(resid, half, 1))
        cols = pl.ds(pl.multiple_of(half * count, count), count)
        grads[0, :, cols] = (hidden_grad * factor[0, half]).astype(BF16)
        grads[1, :, cols] = (hidden_grad * factor[1, half]).astype(BF16)

    backward(rep)
    for copy in passed:
        copy.wait_recv()
    backward(1 - rep)
    for copy in sent:
        copy.wait_send()


def update_kernel(
    student, grads, rows, resid, latent, slope,
    student_ref, new_gu_ref, new_dn_ref, fresh, store_sem,
):
    n, part, width = rows.shape[2:]
    stores = [pltpu.make_async_copy(student, student_ref, store_sem.at[3])]
    stores[0].start()
    targets = [new_gu_ref.at[0, 0], new_gu_ref.at[0, 1], new_dn_ref.at[0]]
    tile = min(width, 256)
    for matrix in range(3):
        source = resid if matrix == 2 else rows
        for side in range(2):
            for first in range(0, width, tile):
                block = source[:, side, :, :, first : first + tile].reshape(2 * n * part, tile)
                grad = jnp.dot(grads[matrix], block, preferred_element_type=F32)
                cols = slice(side * width + first, side * width + first + tile)
                fresh[matrix, :, cols] = latent[matrix, :, cols] - learn_rate * (
                    slope[matrix, :, cols] * grad
                )
        store = pltpu.make_async_copy(fresh.at[matrix], targets[matrix], store_sem.at[matrix])
        store.start()
        stores.append(store)
    for store in stores:
        store.wait()


def dense_step(tokens, teacher, expert_ids, gate_codes, gate_up_latent, down_latent):
    n_inner, n_outer = lax.axis_size("inner"), lax.axis_size("outer")
    n = n_inner * n_outer
    tok_rows, width = tokens.shape
    hid, full = down_latent.shape[1:]
    sublanes = -(-n // 8) * 8
    part = tok_rows // 2
    dma = pltpu.SemaphoreType.DMA
    halves = (2, n, part, width)
    vmem = pl.BlockSpec(memory_space=pltpu.VMEM)
    hbm = pl.BlockSpec(memory_space=pltpu.HBM)
    inputs = (tokens, teacher, expert_ids.T, gate_codes.T, gate_up_latent, down_latent)
    state = pl.pallas_call(
        functools.partial(dense_kernel, n_inner, n_outer),
        out_shape=(
            jax.ShapeDtypeStruct(tokens.shape, BF16),
            jax.ShapeDtypeStruct((3, hid, n * tok_rows), BF16),
            jax.ShapeDtypeStruct((2, *halves), BF16),
            jax.ShapeDtypeStruct((2, *halves), BF16),
            jax.ShapeDtypeStruct((3, hid, full), F32),
            jax.ShapeDtypeStruct((3, hid, full), F32),
        ),
        in_specs=[hbm] * 6,
        out_specs=(vmem,) * 6,
        scratch_shapes=[
            pltpu.VMEM((tok_rows, width), BF16),
            pltpu.VMEM((tok_rows, width), BF16),
            pltpu.VMEM(expert_ids.shape[::-1], jnp.int32),
            pltpu.VMEM(expert_ids.shape[::-1], jnp.int32),
            pltpu.VMEM((2, part, width), BF16),
            pltpu.VMEM((2, sublanes, LANES), F32),
            pltpu.VMEM((n, 2, sublanes, LANES), F32),
            pltpu.VMEM((2, 3, hid, full), BF16),
            pltpu.VMEM((2, 2, hid, n * part), F32),
            pltpu.VMEM(halves, BF16),
            pltpu.VMEM(halves, BF16),
            dma((7,)),
            dma((n,)),
            dma((n,)),
            dma((2 * n,)),
            dma((2 * n,)),
            dma((4,)),
            dma((4,)),
            dma((2 * n,)),
            dma((2 * n,)),
            dma((2 * n + 2,)),
            dma((2 * n,)),
            dma((2,)),
        ],
        compiler_params=pltpu.CompilerParams(
            collective_id=0, has_side_effects=True, vmem_limit_bytes=24 * 1024 * 1024
        ),
    )(*[pltpu.with_memory_space_constraint(value, pltpu.HBM) for value in inputs])
    return pl.pallas_call(
        update_kernel,
        out_shape=(
            jax.ShapeDtypeStruct(tokens.shape, BF16),
            jax.ShapeDtypeStruct(gate_up_latent.shape, F32),
            jax.ShapeDtypeStruct(down_latent.shape, F32),
        ),
        in_specs=[vmem] * 6,
        out_specs=(hbm,) * 3,
        scratch_shapes=[pltpu.VMEM((3, hid, full), F32), dma((4,))],
        compiler_params=pltpu.CompilerParams(vmem_limit_bytes=24 * 1024 * 1024),
    )(*state)


def on_device(tokens, teacher, expert_ids, gate_codes, gate_up_latent, down_latent):
    experts = lax.axis_size("inner") * lax.axis_size("outer")
    tok_rows, top_count = expert_ids.shape
    whole_block = 2 * top_count >= experts
    fits = (
        lax.axis_size("rep") == 2
        and LANES % tok_rows == 0
        and tok_rows % 32 == 0
        and experts <= LANES
        and experts * tok_rows % (2 * LANES) == 0
        and tokens.shape[1] % LANES == 0
        and down_latent.shape[1] % 64 == 0
    )
    step = dense_step if whole_block and fits else routed_step
    return step(tokens, teacher, expert_ids, gate_codes, gate_up_latent, down_latent)


def solution(mesh):
    return jax.shard_map(
        on_device,
        mesh=mesh,
        in_specs=(
            P(("parts", "inner", "outer"), "rep"),
            P(("parts", "inner", "outer"), "rep"),
            P(("parts", "inner", "outer"), None),
            P(("parts", "inner", "outer"), None),
            P(("inner", "outer"), None, "rep", None),
            P(("inner", "outer"), "rep", None),
        ),
        out_specs=(
            P(("parts", "inner", "outer"), "rep"),
            P(("parts", "inner", "outer"), None, "rep", None),
            P(("parts", "inner", "outer"), "rep", None),
        ),
        check_vma=False,
    )
```

```python
import functools
import math

import jax
import jax.numpy as jnp
from jax import lax
from jax.experimental import pallas as pl
from jax.experimental.pallas import tpu as pltpu
from jax.sharding import PartitionSpec as P

D = 1024
HID = 384


learn_rate = 1.0


def soften(latent, fan_in):
    row_scale = jnp.mean(jnp.abs(latent), axis=-1, keepdims=True) + 1e-06
    normed = latent / row_scale
    lower = jnp.tanh(4.0 * (normed - 0.5))
    upper = jnp.tanh(4.0 * (normed + 0.5))
    fan_root = 1.0 / math.sqrt(fan_in)
    weight = (row_scale * 0.5 * (lower + upper) * fan_root).astype(jnp.bfloat16)
    slope = 2.0 * (2.0 - lower * lower - upper * upper) * fan_root
    return (weight, slope)


def dispatch_rows(outbox):
    return lax.all_to_all(outbox, ("inner", "outer"), split_axis=0, concat_axis=0, tiled=True)


def combine_rows(outbox):
    return lax.all_to_all(outbox, ("inner", "outer"), split_axis=0, concat_axis=0, tiled=True)


def upstream_rows(outbox):
    return lax.all_to_all(outbox, ("inner", "outer"), split_axis=0, concat_axis=0, tiled=True)


def routed_step(tokens, teacher, expert_ids, gate_codes, gate_up_latent, down_latent):
    experts = lax.axis_size("inner") * lax.axis_size("outer")
    tok_rows, top_count = expert_ids.shape
    part_width = tokens.shape[1]
    capacity = min(tok_rows, 2 * tok_rows * top_count // experts)
    flat_ids = expert_ids.reshape(-1)
    one_hot = (flat_ids[:, None] == jnp.arange(experts, dtype=jnp.int32)[None, :]).astype(jnp.int32)
    before = jnp.cumsum(one_hot, axis=0) - one_hot
    route_slot = jnp.sum(before * one_hot, axis=1)
    target = flat_ids * capacity + route_slot
    payload = jnp.repeat(tokens, top_count, axis=0)
    outbox = jnp.zeros((experts * capacity, part_width), jnp.bfloat16).at[target].set(payload)
    received = dispatch_rows(outbox)
    expert_rows = lax.all_gather(received, "rep", axis=1, tiled=True)
    gu_weight, gu_slope = soften(gate_up_latent[0], D)
    dn_weight, dn_slope = soften(down_latent[0], HID)
    projected = lax.dot_general(
        gu_weight, expert_rows, (((2,), (1,)), ((), ())), preferred_element_type=jnp.float32
    )
    pre_gate = projected[0]
    pre_up = projected[1]
    sigmoid_gate = jax.nn.sigmoid(pre_gate)
    activated = pre_gate * sigmoid_gate
    hidden = (activated * pre_up).astype(jnp.bfloat16)
    partial_out = lax.dot_general(
        hidden, dn_weight, (((0,), (0,)), ((), ())), preferred_element_type=jnp.float32
    )
    expert_out = lax.psum_scatter(
        partial_out.astype(jnp.bfloat16), "rep", scatter_dimension=1, tiled=True
    )
    returned = combine_rows(expert_out)
    picked = returned[target].reshape(tok_rows, top_count, part_width)
    gating = gate_codes.astype(jnp.float32) / 65536.0
    mixed = jnp.sum(gating[:, :, None] * picked.astype(jnp.float32), axis=1)
    student_out = mixed.astype(jnp.bfloat16)
    residual = mixed - teacher.astype(jnp.float32)
    pair_grad = (
        (gating[:, :, None] * residual[:, None, :]).astype(jnp.bfloat16).reshape(-1, part_width)
    )
    grad_outbox = (
        jnp.zeros((experts * capacity, part_width), jnp.bfloat16).at[target].set(pair_grad)
    )
    grad_part = upstream_rows(grad_outbox)
    out_grad = lax.all_gather(grad_part, "rep", axis=1, tiled=True)
    down_grad = jnp.dot(hidden, out_grad, preferred_element_type=jnp.float32)
    hidden_grad = lax.dot_general(
        dn_weight, out_grad, (((1,), (1,)), ((), ())), preferred_element_type=jnp.float32
    )
    gate_grad = (
        hidden_grad * pre_up * sigmoid_gate * (1.0 + pre_gate * (1.0 - sigmoid_gate))
    ).astype(jnp.bfloat16)
    up_grad = (hidden_grad * activated).astype(jnp.bfloat16)
    weight_grads = lax.dot_general(
        jnp.stack([gate_grad, up_grad]),
        expert_rows,
        (((2,), (0,)), ((), ())),
        preferred_element_type=jnp.float32,
    )
    new_gate_up = gate_up_latent - learn_rate * (gu_slope * weight_grads)[None]
    new_down = down_latent - learn_rate * (dn_slope * down_grad)[None]
    return (student_out, new_gate_up, new_down)


MESH = pl.DeviceIdType.MESH
LANES = 128
BF16 = jnp.bfloat16
F32 = jnp.float32


def dot_t(a, b):
    return lax.dot_general(a, b, (((1,), (1,)), ((), ())), preferred_element_type=F32)


def dense_kernel(
    n_inner, n_outer,
    tokens_ref, teacher_ref, ids_ref, codes_ref, gu_ref, dn_ref,
    student, grads, rows, resid, latent, slope,
    tokens, teacher, ids, codes, resid_own, gates_own, gates, weight, factor, sums, returned,
    load_sem, gate_send, gate_recv, tok_send, tok_recv, pair_send, pair_recv,
    sum_send, sum_recv, res_send, res_recv, res_rep,
):
    n = n_inner * n_outer
    tok_rows, width = tokens_ref.shape
    part = tok_rows // 2
    count = n * part
    hid = latent.shape[1]
    inner, outer, rep = lax.axis_index("inner"), lax.axis_index("outer"), lax.axis_index("rep")
    me = inner * n_outer + outer
    sides = (rep, 1 - rep)
    partner = {"rep": 1 - rep}

    def peer_at(step):
        peer = lax.rem(me + step + n, n)
        return peer, {"inner": peer // n_outer, "outer": lax.rem(peer, n_outer)}

    def remote(source, target, send, recv, device):
        return pltpu.make_async_remote_copy(
            src_ref=source, dst_ref=target, send_sem=send, recv_sem=recv,
            device_id=device, device_id_type=MESH,
        )

    others = [(step, side) for step in range(n) for side in range(2) if step or side]
    others.sort(key=lambda pair: abs(pair[0] - n // 2))

    def part_rows(side):
        return pl.ds(pl.multiple_of(side * part, part), part)

    loads = [
        pltpu.make_async_copy(gu_ref.at[0, 0], latent.at[0], load_sem.at[0]),
        pltpu.make_async_copy(gu_ref.at[0, 1], latent.at[1], load_sem.at[1]),
        pltpu.make_async_copy(dn_ref.at[0], latent.at[2], load_sem.at[2]),
        pltpu.make_async_copy(tokens_ref, tokens, load_sem.at[3]),
        pltpu.make_async_copy(teacher_ref, teacher, load_sem.at[4]),
        pltpu.make_async_copy(ids_ref, ids, load_sem.at[5]),
        pltpu.make_async_copy(codes_ref, codes, load_sem.at[6]),
    ]
    barrier = pltpu.get_barrier_semaphore()
    for step, side in others:
        device = dict(peer_at(step)[1], rep=sides[side])
        pl.semaphore_signal(barrier, inc=1, device_id=device, device_id_type=MESH)
    for load in loads[3:] + loads[:3]:
        load.start()
    pl.semaphore_wait(barrier, len(others))

    sent = []

    def spread(source_of, target_of, send, recv, slot_of):
        for at, (step, side) in enumerate(others):
            peer, device = peer_at(step)
            copy = remote(
                source_of(peer, sides[side]), target_of(sides[side]),
                send.at[at], recv.at[slot_of], dict(device, rep=sides[side]),
            )
            copy.start()
            sent.append(copy)

    def arrived(source, target_of, send, recv, step, side):
        peer = peer_at(-step)[0]
        slot = sides[side] * n + peer
        remote(
            source, target_of(sides[side], peer), send.at[0], recv.at[slot], partner
        ).wait_recv()

    mine = rep * n + me
    loads[3].wait()
    spread(
        lambda peer, side: tokens.at[part_rows(side)],
        lambda side: rows.at[side, rep, me],
        tok_send, tok_recv, mine,
    )

    loads[5].wait()
    loads[6].wait()
    gate_of = codes[...].astype(F32) * (1.0 / 65536.0)
    line = lax.broadcasted_iota(jnp.int32, (gates_own.shape[1], tok_rows), 0)
    table = jnp.zeros((gates_own.shape[1], tok_rows), F32)
    for expert in range(n):
        row = jnp.sum(jnp.where(ids[...] == expert, gate_of, 0.0), axis=0, keepdims=True)
        table = jnp.where(line == expert, row, table)
    gates_own[...] = jnp.zeros_like(gates_own)
    for half in range(2):
        gates_own[half, :, :part] = table[:, half * part : (half + 1) * part]
    for step in range(1, n):
        copy = remote(
            gates_own, gates.at[me], gate_send.at[step - 1], gate_recv.at[me], peer_at(step)[1]
        )
        copy.start()
        sent.append(copy)
    gates[me] = gates_own[...]

    fan_root = [1.0 / math.sqrt(latent.shape[2])] * 2 + [1.0 / math.sqrt(2 * hid)]
    piece = 32

    def soften_rows(matrix):
        root = fan_root[matrix]

        def body(at, carry):
            lines = pl.ds(pl.multiple_of(at * piece, piece), piece)
            value = latent[matrix, lines, :]
            row_scale = jnp.mean(jnp.abs(value), axis=-1, keepdims=True) + 1e-06
            steep = value * (4.0 / row_scale)
            lower = jnp.tanh(steep - 2.0)
            upper = jnp.tanh(steep + 2.0)
            weight[rep, matrix, lines, :] = (row_scale * (0.5 * root) * (lower + upper)).astype(BF16)
            slope[matrix, lines, :] = (2.0 * root) * (2.0 - lower * lower - upper * upper)
            return carry

        lax.fori_loop(0, hid // piece, body, 0, unroll=3 if hid % (3 * piece) == 0 else 2)

    weight_copies = []
    for matrix in range(3):
        loads[matrix].wait()
        soften_rows(matrix)
        copy = remote(
            weight.at[rep, matrix], weight.at[rep, matrix],
            pair_send.at[matrix], pair_recv.at[matrix], partner,
        )
        copy.start()
        weight_copies.append(copy)
    sent.extend(weight_copies)

    for step in range(1, n):
        slot = peer_at(-step)[0]
        remote(gates_own, gates.at[slot], gate_send.at[0], gate_recv.at[slot], partner).wait_recv()
    per_row = LANES // part

    def gates_for(half):
        return jnp.concatenate(
            [
                sum(
                    pltpu.roll(gates[base + at, half, pl.ds(me, 1), :], at * part, 1) if at
                    else gates[base, half, pl.ds(me, 1), :]
                    for at in range(per_row)
                )
                for base in range(0, n, per_row)
            ],
            axis=1,
        )

    both_gates = [gates_for(half) for half in range(2)]
    own_gate = jnp.where(rep == 0, both_gates[0], both_gates[1])
    other_gate = jnp.where(rep == 0, both_gates[1], both_gates[0])

    def features(buf, half, column):
        return buf[half, column].reshape(count, width)

    def forward(units, half, gate_row):
        both = weight[units, 0:2].reshape(2 * hid, 2 * width)
        pre = dot_t(both[:, :width], features(rows, half, 0))
        pre = pre + dot_t(both[:, width:], features(rows, half, 1))
        pre_gate, pre_up = pre[:hid], pre[hid:]
        sigmoid_gate = jax.nn.sigmoid(pre_gate)
        activated = pre_gate * sigmoid_gate
        return pre_gate, pre_up, sigmoid_gate, activated, activated * pre_up * gate_row

    def keep(half, gate_row, values):
        pre_gate, pre_up, sigmoid_gate, activated, hidden = values
        cols = pl.ds(pl.multiple_of(half * count, count), count)
        grads[2, :, cols] = hidden.astype(BF16)
        factor[0, half] = gate_row * pre_up * sigmoid_gate * (1.0 + pre_gate * (1.0 - sigmoid_gate))
        factor[1, half] = gate_row * activated

    rows[rep, rep, me] = tokens[part_rows(rep), :]
    for step, side in others:
        arrived(
            tokens.at[part_rows(0)], lambda side, peer: rows.at[rep, side, peer],
            tok_send, tok_recv, step, side,
        )
    own_values = forward(rep, rep, own_gate)
    out = jnp.dot(own_values[-1].T.astype(BF16), weight[rep, 2], preferred_element_type=F32)
    weight_copies[0].wait_recv()
    weight_copies[1].wait_recv()
    hidden = forward(1 - rep, rep, own_gate)[-1]
    weight_copies[2].wait_recv()
    out = out + jnp.dot(hidden.T.astype(BF16), weight[1 - rep, 2], preferred_element_type=F32)
    for column in range(2):
        sums[column] = (
            out[:, column * width : (column + 1) * width].astype(BF16).reshape(n, part, width)
        )
    spread(
        lambda peer, side: sums.at[side, peer],
        lambda side: returned.at[rep, me],
        sum_send, sum_recv, mine,
    )
    rows_copy = remote(rows.at[rep], rows.at[rep], pair_send.at[3], pair_recv.at[3], partner)
    rows_copy.start()
    sent.append(rows_copy)
    returned[rep, me] = sums[rep, me]

    keep(rep, own_gate, own_values)
    rows_copy.wait_recv()
    keep(1 - rep, other_gate, forward(rep, 1 - rep, other_gate))

    loads[4].wait()
    for step, side in others:
        arrived(
            resid_own.at[0], lambda side, peer: returned.at[side, peer],
            sum_send, sum_recv, step, side,
        )
    for half in range(2):
        mixed = returned[half, 0].astype(F32)
        for peer in range(1, n):
            mixed = mixed + returned[half, peer].astype(F32)
        lines = slice(half * part, (half + 1) * part)
        student[lines] = mixed.astype(BF16)
        resid_own[half] = (mixed - teacher[lines].astype(F32)).astype(BF16)
    spread(
        lambda peer, side: resid_own.at[side],
        lambda side: resid.at[side, rep, me],
        res_send, res_recv, mine,
    )
    resid[rep, rep, me] = resid_own[rep]

    passed = []
    for side in (1, 0):
        for step, of in others:
            if of == side:
                arrived(
                    resid_own.at[0], lambda side, peer: resid.at[rep, side, peer],
                    res_send, res_recv, step, side,
                )
        column = sides[side]
        copy = remote(
            resid.at[rep, column], resid.at[rep, column],
            res_send.at[2 * n + side], res_rep.at[side], partner,
        )
        copy.start()
        passed.append(copy)
    sent.extend(passed)

    def backward(half):
        down = weight[rep, 2]
        hidden_grad = dot_t(down[:, :width], features(resid, half, 0))
        hidden_grad = hidden_grad + dot_t(down[:, width:], features(resid, half, 1))
        cols = pl.ds(pl.multiple_of(half * count, count), count)
        grads[0, :, cols] = (hidden_grad * factor[0, half]).astype(BF16)
        grads[1, :, cols] = (hidden_grad * factor[1, half]).astype(BF16)

    backward(rep)
    for copy in passed:
        copy.wait_recv()
    backward(1 - rep)
    for copy in sent:
        copy.wait_send()


def update_kernel(
    student, grads, rows, resid, latent, slope,
    student_ref, new_gu_ref, new_dn_ref, fresh, store_sem,
):
    n, part, width = rows.shape[2:]
    stores = [pltpu.make_async_copy(student, student_ref, store_sem.at[3])]
    stores[0].start()
    targets = [new_gu_ref.at[0, 0], new_gu_ref.at[0, 1], new_dn_ref.at[0]]
    tile = min(width, 256)
    for matrix in range(3):
        source = resid if matrix == 2 else rows
        for side in range(2):
            for first in range(0, width, tile):
                block = source[:, side, :, :, first : first + tile].reshape(2 * n * part, tile)
                grad = jnp.dot(grads[matrix], block, preferred_element_type=F32)
                cols = slice(side * width + first, side * width + first + tile)
                fresh[matrix, :, cols] = latent[matrix, :, cols] - learn_rate * (
                    slope[matrix, :, cols] * grad
                )
        store = pltpu.make_async_copy(fresh.at[matrix], targets[matrix], store_sem.at[matrix])
        store.start()
        stores.append(store)
    for store in stores:
        store.wait()


def dense_step(tokens, teacher, expert_ids, gate_codes, gate_up_latent, down_latent):
    n_inner, n_outer = lax.axis_size("inner"), lax.axis_size("outer")
    n = n_inner * n_outer
    tok_rows, width = tokens.shape
    hid, full = down_latent.shape[1:]
    sublanes = -(-n // 8) * 8
    part = tok_rows // 2
    dma = pltpu.SemaphoreType.DMA
    halves = (2, n, part, width)
    vmem = pl.BlockSpec(memory_space=pltpu.VMEM)
    hbm = pl.BlockSpec(memory_space=pltpu.HBM)
    inputs = (tokens, teacher, expert_ids.T, gate_codes.T, gate_up_latent, down_latent)
    state = pl.pallas_call(
        functools.partial(dense_kernel, n_inner, n_outer),
        out_shape=(
            jax.ShapeDtypeStruct(tokens.shape, BF16),
            jax.ShapeDtypeStruct((3, hid, n * tok_rows), BF16),
            jax.ShapeDtypeStruct((2, *halves), BF16),
            jax.ShapeDtypeStruct((2, *halves), BF16),
            jax.ShapeDtypeStruct((3, hid, full), F32),
            jax.ShapeDtypeStruct((3, hid, full), F32),
        ),
        in_specs=[hbm] * 6,
        out_specs=(vmem,) * 6,
        scratch_shapes=[
            pltpu.VMEM((tok_rows, width), BF16),
            pltpu.VMEM((tok_rows, width), BF16),
            pltpu.VMEM(expert_ids.shape[::-1], jnp.int32),
            pltpu.VMEM(expert_ids.shape[::-1], jnp.int32),
            pltpu.VMEM((2, part, width), BF16),
            pltpu.VMEM((2, sublanes, LANES), F32),
            pltpu.VMEM((n, 2, sublanes, LANES), F32),
            pltpu.VMEM((2, 3, hid, full), BF16),
            pltpu.VMEM((2, 2, hid, n * part), F32),
            pltpu.VMEM(halves, BF16),
            pltpu.VMEM(halves, BF16),
            dma((7,)),
            dma((n,)),
            dma((n,)),
            dma((2 * n,)),
            dma((2 * n,)),
            dma((4,)),
            dma((4,)),
            dma((2 * n,)),
            dma((2 * n,)),
            dma((2 * n + 2,)),
            dma((2 * n,)),
            dma((2,)),
        ],
        compiler_params=pltpu.CompilerParams(
            collective_id=0, has_side_effects=True, vmem_limit_bytes=24 * 1024 * 1024
        ),
    )(*[pltpu.with_memory_space_constraint(value, pltpu.HBM) for value in inputs])
    return pl.pallas_call(
        update_kernel,
        out_shape=(
            jax.ShapeDtypeStruct(tokens.shape, BF16),
            jax.ShapeDtypeStruct(gate_up_latent.shape, F32),
            jax.ShapeDtypeStruct(down_latent.shape, F32),
        ),
        in_specs=[vmem] * 6,
        out_specs=(hbm,) * 3,
        scratch_shapes=[pltpu.VMEM((3, hid, full), F32), dma((4,))],
        compiler_params=pltpu.CompilerParams(vmem_limit_bytes=24 * 1024 * 1024),
    )(*state)


def on_device(tokens, teacher, expert_ids, gate_codes, gate_up_latent, down_latent):
    experts = lax.axis_size("inner") * lax.axis_size("outer")
    tok_rows, top_count = expert_ids.shape
    whole_block = 2 * top_count >= experts
    fits = (
        lax.axis_size("rep") == 2
        and LANES % tok_rows == 0
        and tok_rows % 32 == 0
        and experts <= LANES
        and experts * tok_rows % (2 * LANES) == 0
        and tokens.shape[1] % LANES == 0
        and down_latent.shape[1] % 64 == 0
    )
    step = dense_step if whole_block and fits else routed_step
    return step(tokens, teacher, expert_ids, gate_codes, gate_up_latent, down_latent)


def solution(mesh):
    return jax.shard_map(
        on_device,
        mesh=mesh,
        in_specs=(
            P(("parts", "inner", "outer"), "rep"),
            P(("parts", "inner", "outer"), "rep"),
            P(("parts", "inner", "outer"), None),
            P(("parts", "inner", "outer"), None),
            P(("inner", "outer"), None, "rep", None),
            P(("inner", "outer"), "rep", None),
        ),
        out_specs=(
            P(("parts", "inner", "outer"), "rep"),
            P(("parts", "inner", "outer"), None, "rep", None),
            P(("parts", "inner", "outer"), "rep", None),
        ),
        check_vma=False,
    )
```
